256 devices in a mesh: dp: 16 (over z, core), expert: 16 (over y, x).
Axes of the slice: x: 4, y: 4, z: 8, core: 2. Of those that a mesh axis runs over, the one named last changes fastest.
Arguments:
- tokens: bfloat16 [32768, 2048], P(('dp', 'expert')), may hold values from -24 to 24
- out_grad: bfloat16 [32768, 2048], P(('dp', 'expert')), may hold values from -6 to 6
- gates: bfloat16 [32768, 4], P(('dp', 'expert')), may hold values from 0.099609375 to 1
- expert_ids: int32 [32768, 4], P(('dp', 'expert')), may hold values from 0 to 15, all different within a row; in each aligned block of 128 rows (0 to 127, 128 to 255, ...) at most 40 rows name the same one
- w_gate: bfloat16 [16, 2048, 768], P('expert'), may hold values from -0.125 to 0.125
- w_up: bfloat16 [16, 2048, 768], P('expert'), may hold values from -0.125 to 0.125
- w_down: bfloat16 [16, 768, 2048], P('expert'), may hold values from -0.21875 to 0.21875
Outputs:
- token_grad: bfloat16 [32768, 2048], P(('dp', 'expert'))
- gate_grad: bfloat16 [32768, 4], P(('dp', 'expert'))
- grad_gate: bfloat16 [16, 2048, 768], P('expert', 'dp')
- grad_up: bfloat16 [16, 2048, 768], P('expert', 'dp')
- grad_down: bfloat16 [16, 768, 2048], P('expert', 'dp')
The draws below stay inside these ranges and needn't reach their ends.
Inputs may be any that keep to these rules, and one draw needn't show every extreme that they name: `expert_ids`: in each aligned block of 128 rows (one device's tokens) no expert is named by more than 40 rows, a bound that some block reaches; a row names 4 different experts.
All inputs are finite; a program needn't handle non-finite values.
Results may differ from the reference program's by a relative error of at most 0.023.
Values may be sent and summed in bfloat16 or wider, within the bound.
No kernel may reach another device: no remote copies, remote signals or barrier semaphores. Data moves between devices by JAX's collectives and lax.ppermute only.
A program may use at most 128 MiB of HBM per device.

```python
import math
import jax
import jax.numpy as jnp
import numpy as np
from jax import lax

D = 2048
FF = 768
TOP = 4
TOK_DEV = 128
EXPERTS = 16
CAP = 40
TOKENS = 32768
N_DP = 16
N_EXPERT = 16


def with_spikes(drawn, rng, source, target, blocks, factor):
    owner, partner = [(jnp.arange(drawn.shape[position]) // (drawn.shape[position] // blocks)).reshape([-1 if axis == position else 1 for axis in range(drawn.ndim)]) for position in (source, target)]
    chosen = jax.random.permutation(rng, blocks)[partner]
    strong = (owner == chosen) | (owner == (partner + blocks // 2) % blocks)
    return jnp.where(strong, factor * drawn, drawn)


def block_levels(stream_key, extent, pieces, least, largest):
    factor_of, own = 1.0, jax.random.fold_in(stream_key, 6)
    for axis_at, shards_of in pieces:
        steps = jnp.exp(jax.random.uniform(jax.random.fold_in(own, axis_at), (shards_of,), jnp.float32, least / len(pieces), largest / len(pieces)))
        factor_of = factor_of * jnp.repeat(steps, extent[axis_at] // shards_of).reshape([-1 if axis == axis_at else 1 for axis in range(len(extent))])
    return factor_of


def deal_out(key, own, number, rows, amount, top, limit, slope):
    order = jax.random.permutation(key, amount)
    packed, usual = shares(amount, rows * top, limit, slope, True), shares(amount, rows * top, limit, slope, False)
    places = jnp.arange(amount)

    def named(tallies, turn):
        used = int((tallies > 0).sum())
        fixed = max(1, used // 4)
        moved = fixed + (places - fixed + turn * (used - fixed)) % max(1, amount - fixed)
        return jnp.zeros((amount,), jnp.int32).at[order[jnp.where(places < fixed, places, moved)]].set(jnp.asarray(tallies, jnp.int32))

    tallies = jnp.where(number % 4 == 0, named(packed, number // 4), named(usual, number - number // 4 - 1))
    mixed = jax.random.permutation(jax.random.fold_in(own, 3), amount)
    giver, taker = mixed[0:amount // 2 * 2:2], mixed[1:amount // 2 * 2:2]
    room = jnp.minimum(tallies[giver] - 1, limit - tallies[taker]) // 2
    room = jnp.where((giver == order[0]) | (taker == order[0]) | (tallies[taker] == 0), 0, jnp.maximum(room, 0))
    moved = jax.random.randint(jax.random.fold_in(own, 4), (amount // 2,), 0, 1 << 20) % (room + 1)
    tallies = tallies.at[giver].add(-moved).at[taker].add(moved)
    labels = jnp.searchsorted(jnp.cumsum(tallies), jnp.arange(rows * top), side="right").astype(jnp.int32)
    grid = labels.reshape(top, rows).T
    grid = grid[jax.random.permutation(jax.random.fold_in(own, 1), rows)]
    turn = jax.random.randint(jax.random.fold_in(own, 2), (rows, 1), 0, top)
    return jnp.take_along_axis(grid, (jnp.arange(top)[None, :] + turn) % top, axis=1)


def shares(amount, total, limit, slope, full):
    loads = [(1 << 20) // math.isqrt(standing ** slope) + 1 for standing in range(1, amount + 1)]
    largest = limit if full else min(limit, max(-(-total // amount), total * loads[0] // sum(loads)))
    least = 1 if total - largest >= amount - 1 else 0
    holding, spare = [largest] + [least] * (amount - 1), total - largest - least * (amount - 1)
    while spare > 0:
        free = [i for i in range(1, amount) if holding[i] < largest] or [i for i in range(1, amount) if holding[i] < limit]
        whole, remaining = sum([loads[i] for i in free]), spare
        for i in free:
            extra = min(limit - holding[i], max(1, remaining * loads[i] // whole), spare)
            holding[i] = holding[i] + extra
            spare = spare - extra
    return np.array(holding)


def noise(stream_key, shape, deviation, most, split=(), kind=jnp.bfloat16):
    gain = block_levels(stream_key, shape, split, -0.22, 0.18) if split else 1.0
    values = jax.random.normal(stream_key, shape, jnp.float32) * deviation * gain
    return jnp.minimum(jnp.maximum(values, -most), most).astype(kind)


def heavy_noise(key, dims, scale, most, split, heavy, kind=jnp.bfloat16):
    values = scale * jax.random.normal(key, dims, jnp.float32)
    if split:
        values = values * block_levels(key, dims, split, -0.22, 0.18)
    return jnp.clip(with_spikes(values, jax.random.fold_in(key, 3), *heavy), -most, most).astype(kind)


def setup_inputs(seed: int = 0) -> dict:
    keys = jax.random.split(jax.random.key(seed), 8)
    tokens = heavy_noise(keys[0], (TOKENS, D), 1.0, 24.0, ((0, 256),), (0, 1, 256, 6.0))
    out_grad = noise(keys[1], (TOKENS, D), 1.0, 6.0, ((0, 256),))
    gates = jnp.clip(0.099609375 + 0.9003906 * jax.random.uniform(keys[2], (TOKENS, TOP), jnp.float32) ** block_levels(keys[2], (TOKENS, TOP), ((0, 256),), -0.2, 0.2), 0.099609375, 1.0).astype(jnp.bfloat16)
    expert_ids_keys = jax.random.split(jax.random.fold_in(keys[3], 1), TOKENS // TOK_DEV)
    expert_ids_turns = jax.random.permutation(jax.random.fold_in(keys[3], 3), TOKENS // TOK_DEV)
    expert_ids = jax.vmap(lambda own, number: deal_out(jax.random.fold_in(keys[3], 2), own, number, TOK_DEV, EXPERTS, TOP, CAP, 2))(expert_ids_keys, expert_ids_turns).reshape((TOKENS, TOP))
    w_gate = noise(keys[4], (EXPERTS, D, FF), D ** -0.5, 0.125, ((0, 16),))
    w_up = noise(keys[5], (EXPERTS, D, FF), D ** -0.5, 0.125, ((0, 16),))
    w_down = noise(keys[6], (EXPERTS, FF, D), FF ** -0.5, 0.21875, ((0, 16),))
    return {"tokens": tokens, "out_grad": out_grad, "gates": gates, "expert_ids": expert_ids, "w_gate": w_gate, "w_up": w_up, "w_down": w_down}


def expert_block(expert, slot_index, valid_rows, x_pad, dy_pad, gate_pad, w_gate, w_up, w_down):
    token_index = (slot_index // TOP).astype(jnp.int32)
    x_rows = x_pad[token_index]
    dy_rows = dy_pad[token_index]
    probs = jnp.where(valid_rows, gate_pad[slot_index].astype(jnp.float32), 0.0)
    wg = w_gate[expert]
    wu = w_up[expert]
    wd = w_down[expert]
    pre_gate = jnp.dot(x_rows, wg, preferred_element_type=jnp.float32)
    pre_up = jnp.dot(x_rows, wu, preferred_element_type=jnp.float32)
    sigmoid_g = jax.nn.sigmoid(pre_gate)
    activated = pre_gate * sigmoid_g
    hidden = activated * pre_up
    back_hidden = jnp.dot(dy_rows, wd.T, preferred_element_type=jnp.float32)
    prob_grad = jnp.sum(back_hidden * hidden, axis=-1).astype(jnp.bfloat16)
    scaled_hidden = (probs[:, None] * hidden).astype(jnp.bfloat16)
    d_hidden = probs[:, None] * back_hidden
    d_gate = (d_hidden * pre_up * sigmoid_g * (1.0 + pre_gate * (1.0 - sigmoid_g))).astype(jnp.bfloat16)
    d_up = (d_hidden * activated).astype(jnp.bfloat16)
    pair_grad = (jnp.dot(d_gate, wg.T, preferred_element_type=jnp.float32)
                 + jnp.dot(d_up, wu.T, preferred_element_type=jnp.float32)).astype(jnp.bfloat16)
    part_gate = jnp.dot(x_rows.T, d_gate, preferred_element_type=jnp.float32).astype(jnp.bfloat16)
    part_up = jnp.dot(x_rows.T, d_up, preferred_element_type=jnp.float32).astype(jnp.bfloat16)
    part_down = jnp.dot(scaled_hidden.T, dy_rows, preferred_element_type=jnp.float32).astype(jnp.bfloat16)
    return pair_grad, prob_grad, part_gate, part_up, part_down


def reference(tokens, out_grad, gates, expert_ids, w_gate, w_up, w_down):
    row_count = N_EXPERT * TOK_DEV
    slot_count = row_count * TOP
    block_rows = N_EXPERT * CAP
    x_all = tokens.reshape(N_DP, row_count, D)
    dy_all = out_grad.reshape(N_DP, row_count, D)
    gate_all = gates.reshape(N_DP, slot_count)
    ids_all = expert_ids.reshape(N_DP, slot_count)
    expert_range = jnp.arange(EXPERTS, dtype=jnp.int32)

    def replica(carry, row_data):
        x_rows, dy_rows, gate_rows, flat_ids = row_data
        x_pad = jnp.concatenate([x_rows, jnp.zeros((1, D), jnp.bfloat16)], axis=0)
        dy_pad = jnp.concatenate([dy_rows, jnp.zeros((1, D), jnp.bfloat16)], axis=0)
        gate_pad = jnp.concatenate([gate_rows, jnp.zeros((1,), jnp.bfloat16)], axis=0)
        slot_order = jnp.argsort(flat_ids, stable=True).astype(jnp.int32)
        counts = jnp.sum((flat_ids[:, None] == expert_range[None, :]).astype(jnp.int32), axis=0)
        starts = (jnp.cumsum(counts) - counts).astype(jnp.int32)
        order_pad = jnp.concatenate([slot_order, jnp.full((block_rows,), slot_count, jnp.int32)])

        def one_expert(expert):
            picked = lax.dynamic_slice(order_pad, (starts[expert].astype(jnp.int32),), (block_rows,))
            valid_rows = jnp.arange(block_rows, dtype=jnp.int32) < counts[expert]
            slot_index = jnp.where(valid_rows, picked, slot_count).astype(jnp.int32)
            result = expert_block(expert, slot_index, valid_rows, x_pad, dy_pad, gate_pad, w_gate, w_up, w_down)
            return result + (slot_index,)

        pair_grad, prob_grad, part_gate, part_up, part_down, slot_index = lax.map(one_expert, expert_range)
        slot_flat = slot_index.reshape(-1)
        token_flat = (slot_flat // TOP).astype(jnp.int32)
        summed = jnp.zeros((row_count + 1, D), jnp.float32).at[token_flat].add(pair_grad.reshape(-1, D).astype(jnp.float32))
        prob_out = jnp.zeros((slot_count + 1,), jnp.bfloat16).at[slot_flat].set(prob_grad.reshape(-1))
        carry = (carry[0] + part_gate.astype(jnp.float32), carry[1] + part_up.astype(jnp.float32),
                 carry[2] + part_down.astype(jnp.float32))
        return carry, (summed[:row_count].astype(jnp.bfloat16), prob_out[:slot_count])

    start = (jnp.zeros((EXPERTS, D, FF), jnp.float32), jnp.zeros((EXPERTS, D, FF), jnp.float32),
             jnp.zeros((EXPERTS, FF, D), jnp.float32))
    totals, (token_grad, gate_grad) = lax.scan(replica, start, (x_all, dy_all, gate_all, ids_all))
    return (token_grad.reshape(TOKENS, D), gate_grad.reshape(TOKENS, TOP),
            totals[0].astype(jnp.bfloat16), totals[1].astype(jnp.bfloat16), totals[2].astype(jnp.bfloat16))
```

```python
import jax
import jax.numpy as jnp
from jax import lax
from jax.experimental import pallas as pl
from jax.experimental.pallas import tpu as pltpu
from jax.sharding import PartitionSpec as P

F32 = jnp.float32
BF16 = jnp.bfloat16
N_TOK = 128
D = 2048
FF = 768
CAP = 40
N_EXP = 16
ROWS = N_EXP * CAP
N_Z = 8
EXTRA = 128
VMEM_LIMIT = 48 * 1024 * 1024


def params():
    return pltpu.CompilerParams(vmem_limit_bytes=VMEM_LIMIT)


def cost(flops, nbytes):
    return pl.CostEstimate(flops=int(flops), bytes_accessed=int(nbytes), transcendentals=0)


def dot(a, b, ca=1, cb=0):
    return lax.dot_general(a, b, (((ca,), (cb,)), ((), ())), preferred_element_type=F32)


def slot_matrix(ids_t, gates_t=None):
    expert = lax.broadcasted_iota(jnp.int32, (N_EXP, N_TOK), 0)
    member = jnp.zeros((N_EXP, N_TOK), F32)
    weight = jnp.zeros((N_EXP, N_TOK), F32)
    for k in range(4):
        hit = ids_t[k : k + 1, :] == expert
        member = jnp.where(hit, 1.0, member)
        if gates_t is not None:
            weight = jnp.where(hit, gates_t[k : k + 1, :].astype(F32), weight)
    row = lax.broadcasted_iota(jnp.int32, (N_TOK, N_TOK), 0)
    col = lax.broadcasted_iota(jnp.int32, (N_TOK, N_TOK), 1)
    before = jnp.where(row < col, 1.0, 0.0).astype(BF16)
    position = dot(member.astype(BF16), before)
    code = jnp.where(member > 0.0, position, -1.0)
    slot = lax.broadcasted_iota(jnp.int32, (CAP, N_TOK), 0).astype(F32)
    pieces = []
    for e in range(N_EXP):
        value = 1.0 if gates_t is None else weight[e : e + 1, :]
        pieces.append(jnp.where(code[e : e + 1, :] == slot, value, 0.0))
    return jnp.concatenate(pieces, axis=0).astype(BF16)


def dispatch_kernel(ids_ref, x_ref, out_ref, slots):
    @pl.when(pl.program_id(0) == 0)
    def _():
        slots[...] = slot_matrix(ids_ref[...])

    out_ref[...] = dot(slots[...], x_ref[...]).astype(BF16)


def dispatch_gated_kernel(ids_ref, gates_ref, x_ref, out_ref, slots):
    @pl.when(pl.program_id(0) == 0)
    def _():
        slots[...] = slot_matrix(ids_ref[...], gates_ref[...])

    out_ref[...] = dot(slots[...], x_ref[...]).astype(BF16)


def dispatch(x, ids_t, gates_t=None):
    width = 512
    small = [pl.BlockSpec((4, N_TOK), lambda n: (0, 0))]
    args = [ids_t]
    if gates_t is not None:
        small = small * 2
        args.append(gates_t)
    return pl.pallas_call(
        dispatch_kernel if gates_t is None else dispatch_gated_kernel,
        grid=(D // width,),
        in_specs=small + [pl.BlockSpec((N_TOK, width), lambda n: (0, n))],
        out_specs=pl.BlockSpec((ROWS, width), lambda n: (0, n)),
        out_shape=jax.ShapeDtypeStruct((ROWS, D), BF16),
        scratch_shapes=[pltpu.VMEM((ROWS, N_TOK), BF16)],
        compiler_params=params(),
        cost_estimate=cost(2 * ROWS * N_TOK * D, 2 * ROWS * D),
    )(*args, x)


def forward_kernel(x_ref, wg_ref, wu_ref, ht_ref, h_ref, f_ref, a_ref):
    x = x_ref[...]
    g = dot(x, wg_ref[0])
    u = dot(x, wu_ref[0])
    s = jax.nn.sigmoid(g)
    a = g * s
    h = a * u
    h_ref[...] = h
    ht_ref[...] = h.T.astype(BF16)
    a_ref[...] = a
    f_ref[...] = u * s * (1.0 + g * (1.0 - s))


def forward(x, wg, wu):
    width = 256
    full = jax.ShapeDtypeStruct((ROWS, FF), F32)
    out = pl.BlockSpec((ROWS, width), lambda n: (0, n))
    return pl.pallas_call(
        forward_kernel,
        grid=(FF // width,),
        in_specs=[
            pl.BlockSpec((ROWS, D), lambda n: (0, 0)),
            pl.BlockSpec((1, D, width), lambda n: (0, 0, n)),
            pl.BlockSpec((1, D, width), lambda n: (0, 0, n)),
        ],
        out_specs=[pl.BlockSpec((width, ROWS), lambda n: (n, 0)), out, out, out],
        out_shape=[jax.ShapeDtypeStruct((FF, ROWS), BF16), full, full, full],
        compiler_params=params(),
        cost_estimate=cost(4 * ROWS * D * FF, 16_000_000),
    )(x, wg, wu)


def split_kernel(x_ref, out_ref):
    for c in range(2):
        out_ref[c, 0] = x_ref[:, c * 128 : (c + 1) * 128].T


def split_transposed(x):
    return pl.pallas_call(
        split_kernel,
        grid=(N_Z,),
        in_specs=[pl.BlockSpec((ROWS, 256), lambda n: (0, n))],
        out_specs=pl.BlockSpec((2, 1, 128, ROWS), lambda n: (0, n, 0, 0)),
        out_shape=jax.ShapeDtypeStruct((2, N_Z, 128, ROWS), BF16),
        compiler_params=params(),
        cost_estimate=cost(0, 4 * ROWS * D),
    )(x)


def backward_kernel(me_ref, dy_ref, wd_ref, h_ref, f_ref, a_ref, dg_ref, du_ref, gg_ref, total):
    n = pl.program_id(0)
    b = dot(dy_ref[...], wd_ref[0], 1, 1)
    dg_ref[...] = (b * f_ref[...]).astype(BF16)
    du_ref[...] = (b * a_ref[...]).astype(BF16)
    part = jnp.sum(b * h_ref[...], axis=1, keepdims=True)
    part = jnp.broadcast_to(part, (ROWS, EXTRA))

    @pl.when(n == 0)
    def _():
        total[...] = part

    @pl.when(n > 0)
    def _():
        total[...] += part

    @pl.when(n == pl.num_programs(0) - 1)
    def _():
        value = total[...]
        high = value.astype(BF16).astype(F32)
        col = lax.broadcasted_iota(jnp.int32, (ROWS, EXTRA), 1)
        me = me_ref[0]
        low = jnp.where(col == me + N_EXP, value - high, 0.0)
        gg_ref[...] = jnp.where(col == me, high, low).astype(BF16)


def backward(me, dy, wd, h, f, a):
    width = 256
    part = pl.BlockSpec((ROWS, width), lambda n: (0, n))
    return pl.pallas_call(
        backward_kernel,
        grid=(FF // width,),
        in_specs=[
            pl.BlockSpec(memory_space=pltpu.SMEM),
            pl.BlockSpec((ROWS, D), lambda n: (0, 0)),
            pl.BlockSpec((1, width, D), lambda n: (0, n, 0)),
            part,
            part,
            part,
        ],
        out_specs=[part, part, pl.BlockSpec((ROWS, EXTRA), lambda n: (0, 0))],
        out_shape=[
            jax.ShapeDtypeStruct((ROWS, FF), BF16),
            jax.ShapeDtypeStruct((ROWS, FF), BF16),
            jax.ShapeDtypeStruct((ROWS, EXTRA), BF16),
        ],
        scratch_shapes=[pltpu.VMEM((ROWS, EXTRA), F32)],
        compiler_params=params(),
        cost_estimate=cost(2 * ROWS * D * FF, 14_000_000),
    )(me, dy, wd, h, f, a)


def pair_kernel(dg_ref, du_ref, wg_ref, wu_ref, gg_ref, out_ref):
    n = pl.program_id(0)
    width = wg_ref.shape[1]
    value = dot(dg_ref[...], wg_ref[0], 1, 1) + dot(du_ref[...], wu_ref[0], 1, 1)
    out_ref[:, pl.ds(pl.multiple_of(n * width, width), width)] = value.astype(BF16)

    @pl.when(n == 0)
    def _():
        out_ref[:, D:] = gg_ref[...]


def pair_grads(dg, du, wg, wu, gg):
    width = 512
    whole = pl.BlockSpec((ROWS, FF), lambda n: (0, 0))
    weight = pl.BlockSpec((1, width, FF), lambda n: (0, n, 0))
    return pl.pallas_call(
        pair_kernel,
        grid=(D // width,),
        in_specs=[whole, whole, weight, weight, pl.BlockSpec((ROWS, EXTRA), lambda n: (0, 0))],
        out_specs=pl.BlockSpec((ROWS, D + EXTRA), lambda n: (0, 0)),
        out_shape=jax.ShapeDtypeStruct((ROWS, D + EXTRA), BF16),
        compiler_params=params(),
        cost_estimate=cost(4 * ROWS * D * FF, 12_000_000),
    )(dg, du, wg, wu, gg)


def outer_kernel(at_ref, bt_ref, a_ref, b_ref, out_ref):
    value = dot(at_ref[...], a_ref[...]) + dot(bt_ref[...], b_ref[...])
    out_ref[...] = value.astype(BF16)


def outer_sum(own_t, other_t, own, other):
    m, n, width = own_t.shape[0], own.shape[1], 256
    left = pl.BlockSpec((m, ROWS), lambda j: (0, 0))
    right = pl.BlockSpec((ROWS, width), lambda j: (0, j))
    return pl.pallas_call(
        outer_kernel,
        grid=(n // width,),
        in_specs=[left, left, right, right],
        out_specs=pl.BlockSpec((m, width), lambda j: (0, j)),
        out_shape=jax.ShapeDtypeStruct((m, n), BF16),
        compiler_params=params(),
        cost_estimate=cost(4 * ROWS * m * n, 2 * (m * n + 2 * ROWS * (m + n))),
    )(own_t, other_t, own, other)


def combine_kernel(ids_ref, gates_ref, rows_ref, extra_ref, tok_ref, gate_ref, slots):
    @pl.when(pl.program_id(0) == 0)
    def _():
        matrix = slot_matrix(ids_ref[...])
        slots[...] = matrix
        by_expert = dot(extra_ref[...], matrix, 0, 0)
        value = by_expert[:N_EXP] + by_expert[N_EXP : 2 * N_EXP]
        expert = lax.broadcasted_iota(jnp.int32, (N_EXP, N_TOK), 0)
        for k in range(4):
            mine = jnp.where(ids_ref[k : k + 1, :] == expert, value, 0.0)
            total = jnp.sum(mine, axis=0, keepdims=True)
            gate = gates_ref[k : k + 1, :].astype(F32)
            gate_ref[k : k + 1, :] = total / gate

    tok_ref[...] = dot(slots[...], rows_ref[...], 0, 0).astype(BF16)


def combine(ids_t, gates_t, rows):
    width = 512
    small = pl.BlockSpec((4, N_TOK), lambda n: (0, 0))
    return pl.pallas_call(
        combine_kernel,
        grid=(D // width,),
        in_specs=[
            small,
            small,
            pl.BlockSpec((ROWS, width), lambda n: (0, n)),
            pl.BlockSpec((ROWS, EXTRA), lambda n: (0, D // EXTRA)),
        ],
        out_specs=[pl.BlockSpec((N_TOK, width), lambda n: (0, n)), small],
        out_shape=[
            jax.ShapeDtypeStruct((N_TOK, D), BF16),
            jax.ShapeDtypeStruct((4, N_TOK), F32),
        ],
        scratch_shapes=[pltpu.VMEM((ROWS, N_TOK), BF16)],
        compiler_params=params(),
        cost_estimate=cost(2 * ROWS * N_TOK * D, 2 * ROWS * D),
    )(ids_t, gates_t, rows, rows)


def exchange_experts(rows):
    width = rows.shape[1]
    moved = lax.all_to_all(
        rows.reshape(N_EXP, CAP, width), "expert", split_axis=0, concat_axis=0, tiled=True
    )
    return moved.reshape(ROWS, width)


def swap_cores(a):
    return lax.ppermute(a, "dp", [(i, i ^ 1) for i in range(2 * N_Z)])


def pick(a, index):
    return lax.dynamic_index_in_dim(a, index, 0, keepdims=False)


def ring_sum(chains, z, core):
    sign = 1 - 2 * core
    route = []
    for i in range(N_Z):
        route.append((2 * i, 2 * ((i + 1) % N_Z)))
        route.append((2 * i + 1, 2 * ((i - 1) % N_Z) + 1))
    held = [pick(g, lax.rem(z - sign + 2 * N_Z, N_Z)) for g in chains]
    for step in range(2, N_Z + 1):
        block = lax.rem(z - step * sign + 2 * N_Z, N_Z)
        came = [lax.ppermute(a, "dp", route) for a in held]
        held = [
            (c.astype(F32) + pick(g, block).astype(F32)).astype(BF16)
            for c, g in zip(came, chains, strict=True)
        ]
    return held


def body(tokens, out_grad, gates, expert_ids, w_gate, w_up, w_down):
    dp = lax.axis_index("dp")
    z, core = dp // 2, lax.rem(dp, 2)
    me = lax.axis_index("expert").astype(jnp.int32).reshape(1)
    ids_t, gates_t = expert_ids.T, gates.T

    x = exchange_experts(dispatch(tokens, ids_t))
    dy = exchange_experts(dispatch(out_grad, ids_t, gates_t))

    hidden_t, hidden, factor, active = forward(x, w_gate, w_up)
    x_split = split_transposed(x)
    x_own = pick(x_split, core).reshape(D // 2, ROWS)
    x_other = swap_cores(pick(x_split, 1 - core)).reshape(D // 2, ROWS)
    hidden_other_t = swap_cores(hidden_t)

    dy_own = lax.dynamic_slice_in_dim(dy, core * (D // 2), D // 2, axis=1)
    dy_other = swap_cores(lax.dynamic_slice_in_dim(dy, (1 - core) * (D // 2), D // 2, axis=1))
    d_gate, d_up, prob = backward(me, dy, w_down, hidden, factor, active)
    d_gate_other, d_up_other = swap_cores(d_gate), swap_cores(d_up)

    rows = exchange_experts(pair_grads(d_gate, d_up, w_gate, w_up, prob))

    part_down = outer_sum(hidden_t, hidden_other_t, dy_own, dy_other)
    part_gate = outer_sum(x_own, x_other, d_gate, d_gate_other)
    part_up = outer_sum(x_own, x_other, d_up, d_up_other)
    sum_down, sum_gate, sum_up = ring_sum(
        [
            part_down.reshape(N_Z, FF // N_Z, D // 2),
            part_gate.reshape(N_Z, D // (2 * N_Z), FF),
            part_up.reshape(N_Z, D // (2 * N_Z), FF),
        ],
        z,
        core,
    )
    halves = sum_down.reshape(2, FF // (2 * N_Z), D // 2)
    mine = pick(halves, core)
    theirs = swap_cores(pick(halves, 1 - core))
    low = jnp.where(core == 0, mine, theirs)
    high = jnp.where(core == 0, theirs, mine)
    grad_down = jnp.concatenate([low, high], axis=1)

    token_grad, gate_grad_t = combine(ids_t, gates_t, rows)
    gate_grad = gate_grad_t.astype(BF16).T
    return token_grad, gate_grad, sum_gate[None], sum_up[None], grad_down[None]


def solution(mesh):
    both = P(("dp", "expert"), None)
    weight = P("expert", None, None)
    grad = P("expert", "dp", None)
    return jax.shard_map(
        body,
        mesh=mesh,
        in_specs=(both, both, both, both, weight, weight, weight),
        out_specs=(both, both, grad, grad, grad),
        check_vma=False,
    )
```

```python
import jax
import jax.numpy as jnp
from jax import lax
from jax.experimental import pallas as pl
from jax.experimental.pallas import tpu as pltpu
from jax.sharding import PartitionSpec as P

F32 = jnp.float32
BF16 = jnp.bfloat16
N_TOK = 128
D = 2048
FF = 768
CAP = 40
N_EXP = 16
ROWS = N_EXP * CAP
N_Z = 8
EXTRA = 128
H = D // 2
Q = D // 4


def params(mib=60):
    return pltpu.CompilerParams(vmem_limit_bytes=mib * 1024 * 1024)


def cost(flops, nbytes):
    return pl.CostEstimate(flops=int(flops), bytes_accessed=int(nbytes), transcendentals=0)


def dot(a, b, ca=1, cb=0):
    return lax.dot_general(a, b, (((ca,), (cb,)), ((), ())), preferred_element_type=F32)


def slot_matrix(ids_t, gates_t=None):
    expert = lax.broadcasted_iota(jnp.int32, (N_EXP, N_TOK), 0)
    member = jnp.zeros((N_EXP, N_TOK), F32)
    weight = jnp.zeros((N_EXP, N_TOK), F32)
    for k in range(4):
        hit = ids_t[k : k + 1, :] == expert
        member = jnp.where(hit, 1.0, member)
        if gates_t is not None:
            weight = jnp.where(hit, gates_t[k : k + 1, :].astype(F32), weight)
    row = lax.broadcasted_iota(jnp.int32, (N_TOK, N_TOK), 0)
    col = lax.broadcasted_iota(jnp.int32, (N_TOK, N_TOK), 1)
    before = jnp.where(row < col, 1.0, 0.0).astype(BF16)
    position = dot(member.astype(BF16), before)
    code = jnp.where(member > 0.0, position, -1.0)
    slot = lax.broadcasted_iota(jnp.int32, (CAP, N_TOK), 0).astype(F32)
    pieces = []
    for e in range(N_EXP):
        value = 1.0 if gates_t is None else weight[e : e + 1, :]
        pieces.append(jnp.where(code[e : e + 1, :] == slot, value, 0.0))
    return jnp.concatenate(pieces, axis=0).astype(BF16)


def first_dispatch_kernel(core_ref, ids_ref, gates_ref, x_ref, dy_ref, out_ref, slots, gated):
    n = pl.program_id(0)

    @pl.when(n == 0)
    def _():
        slots[...] = slot_matrix(ids_ref[...])
        gated[...] = slot_matrix(ids_ref[...], gates_ref[...])

    @pl.when(n < 4)
    def _():
        out_ref[...] = dot(slots[...], x_ref[...]).astype(BF16)

    @pl.when(n >= 4)
    def _():
        out_ref[...] = dot(gated[...], dy_ref[...]).astype(BF16)


def first_dispatch(core, ids_t, gates_t, x, dy):
    small = pl.BlockSpec((4, N_TOK), lambda n, c: (0, 0))
    mask = pltpu.VMEM((ROWS, N_TOK), BF16)

    def quarter(n, c):
        return 0, jnp.where(n == 5, 2 * (1 - c[0]), 2 * c[0])

    return pl.pallas_call(
        first_dispatch_kernel,
        grid_spec=pltpu.PrefetchScalarGridSpec(
            num_scalar_prefetch=1,
            grid=(6,),
            in_specs=[
                small,
                small,
                pl.BlockSpec((N_TOK, Q), lambda n, c: (0, jnp.minimum(n, 3))),
                pl.BlockSpec((N_TOK, Q), quarter),
            ],
            out_specs=pl.BlockSpec((ROWS, Q), lambda n, c: (0, n)),
            scratch_shapes=[mask, mask],
        ),
        out_shape=jax.ShapeDtypeStruct((ROWS, D + H), BF16),
        compiler_params=params(),
        cost_estimate=cost(2 * ROWS * N_TOK * 3072, 2 * ROWS * 3072),
    )(core, ids_t, gates_t, x, dy)


def second_dispatch_kernel(core_ref, ids_ref, gates_ref, dy_ref, out_ref, gated):
    @pl.when(pl.program_id(0) == 0)
    def _():
        gated[...] = slot_matrix(ids_ref[...], gates_ref[...])

    out_ref[...] = dot(gated[...], dy_ref[...]).astype(BF16)


def second_dispatch(core, ids_t, gates_t, dy):
    small = pl.BlockSpec((4, N_TOK), lambda n, c: (0, 0))

    def quarter(n, c):
        return 0, jnp.where(n == 1, 2 * (1 - c[0]), 2 * c[0]) + 1

    return pl.pallas_call(
        second_dispatch_kernel,
        grid_spec=pltpu.PrefetchScalarGridSpec(
            num_scalar_prefetch=1,
            grid=(2,),
            in_specs=[small, small, pl.BlockSpec((N_TOK, Q), quarter)],
            out_specs=pl.BlockSpec((ROWS, Q), lambda n, c: (0, n)),
            scratch_shapes=[pltpu.VMEM((ROWS, N_TOK), BF16)],
        ),
        out_shape=jax.ShapeDtypeStruct((ROWS, H), BF16),
        compiler_params=params(),
        cost_estimate=cost(2 * ROWS * N_TOK * H, 2 * ROWS * H),
    )(core, ids_t, gates_t, dy)


def down_turn_kernel(core_ref, w_ref, out_ref):
    out_ref[...] = w_ref[0].T


def turn_down(core, w):
    def quarter(n, c):
        own = 2 * c[0]
        other = 2 * (1 - c[0])
        return 0, 0, jnp.where(n % 2 == 0, own, other) + n // 2

    return pl.pallas_call(
        down_turn_kernel,
        grid_spec=pltpu.PrefetchScalarGridSpec(
            num_scalar_prefetch=1,
            grid=(4,),
            in_specs=[pl.BlockSpec((1, FF, Q), quarter)],
            out_specs=pl.BlockSpec((Q, FF), lambda n, c: (n, 0)),
        ),
        out_shape=jax.ShapeDtypeStruct((D, FF), BF16),
        compiler_params=params(),
        cost_estimate=cost(0, 4 * D * FF),
    )(core, w)


def up_turn_kernel(g_ref, u_ref, gt_ref, ut_ref):
    gt_ref[...] = g_ref[0].T
    ut_ref[...] = u_ref[0].T


def turn_up(wg, wu):
    weight = pl.BlockSpec((1, Q, FF), lambda n: (0, n, 0))
    out = pl.BlockSpec((FF, Q), lambda n: (0, n))
    shape = jax.ShapeDtypeStruct((FF, D), BF16)
    return pl.pallas_call(
        up_turn_kernel,
        grid=(4,),
        in_specs=[weight, weight],
        out_specs=[out, out],
        out_shape=[shape, shape],
        compiler_params=params(),
        cost_estimate=cost(0, 8 * D * FF),
    )(wg, wu)


def forward_kernel(x_ref, dy_ref, wg_ref, wu_ref, wd_ref, ht_ref, h_ref, f_ref, a_ref, b_ref):
    x = x_ref[...]
    g = dot(x, wg_ref[0])
    u = dot(x, wu_ref[0])
    s = jax.nn.sigmoid(g)
    a = g * s
    h = a * u
    h_ref[...] = h
    ht_ref[...] = h.T.astype(BF16)
    a_ref[...] = a
    f_ref[...] = u * s * (1.0 + g * (1.0 - s))
    b_ref[...] = dot(dy_ref[...], wd_ref[...])


def forward(first, wg, wu, wd_t):
    width = 256
    full = jax.ShapeDtypeStruct((ROWS, FF), F32)
    out = pl.BlockSpec((ROWS, width), lambda n: (0, n))
    return pl.pallas_call(
        forward_kernel,
        grid=(FF // width,),
        in_specs=[
            pl.BlockSpec((ROWS, D), lambda n: (0, 0)),
            pl.BlockSpec((ROWS, H), lambda n: (0, 2)),
            pl.BlockSpec((1, D, width), lambda n: (0, 0, n)),
            pl.BlockSpec((1, D, width), lambda n: (0, 0, n)),
            pl.BlockSpec((H, width), lambda n: (0, n)),
        ],
        out_specs=[pl.BlockSpec((width, ROWS), lambda n: (n, 0)), out, out, out, out],
        out_shape=[jax.ShapeDtypeStruct((FF, ROWS), BF16), full, full, full, full],
        compiler_params=params(),
        cost_estimate=cost(5 * ROWS * D * FF, 20_000_000),
    )(first, first, wg, wu, wd_t)


def split_kernel(core_ref, mine_ref, theirs_ref, own_ref, other_ref):
    own_ref[...] = mine_ref[...].T
    other_ref[...] = theirs_ref[...].T


def split_transposed(core, first):
    shape = jax.ShapeDtypeStruct((H, ROWS), BF16)
    out = pl.BlockSpec((128, ROWS), lambda n, c: (n, 0))
    return pl.pallas_call(
        split_kernel,
        grid_spec=pltpu.PrefetchScalarGridSpec(
            num_scalar_prefetch=1,
            grid=(N_Z,),
            in_specs=[
                pl.BlockSpec((ROWS, 128), lambda n, c: (0, 2 * n + c[0])),
                pl.BlockSpec((ROWS, 128), lambda n, c: (0, 2 * n + 1 - c[0])),
            ],
            out_specs=[out, out],
        ),
        out_shape=[shape, shape],
        compiler_params=params(),
        cost_estimate=cost(0, 4 * ROWS * D),
    )(core, first, first)


def backward_kernel(me_ref, dy_ref, wd_ref, h_ref, f_ref, a_ref, b_ref, dg_ref, du_ref, gg_ref, total):
    n = pl.program_id(0)
    b = b_ref[...] + dot(dy_ref[...], wd_ref[...])
    dg_ref[...] = (b * f_ref[...]).astype(BF16)
    du_ref[...] = (b * a_ref[...]).astype(BF16)
    part = jnp.sum(b * h_ref[...], axis=1, keepdims=True)
    part = jnp.broadcast_to(part, (ROWS, EXTRA))

    @pl.when(n == 0)
    def _():
        total[...] = part

    @pl.when(n > 0)
    def _():
        total[...] += part

    @pl.when(n == pl.num_programs(0) - 1)
    def _():
        value = total[...]
        high = value.astype(BF16).astype(F32)
        col = lax.broadcasted_iota(jnp.int32, (ROWS, EXTRA), 1)
        me = me_ref[0]
        low = jnp.where(col == me + N_EXP, value - high, 0.0)
        gg_ref[...] = jnp.where(col == me, high, low).astype(BF16)


def backward(me, second, wd_t, h, f, a, b):
    width = 256
    part = pl.BlockSpec((ROWS, width), lambda n: (0, n))
    return pl.pallas_call(
        backward_kernel,
        grid=(FF // width,),
        in_specs=[
            pl.BlockSpec(memory_space=pltpu.SMEM),
            pl.BlockSpec((ROWS, H), lambda n: (0, 0)),
            pl.BlockSpec((H, width), lambda n: (1, n)),
            part,
            part,
            part,
            part,
        ],
        out_specs=[part, part, pl.BlockSpec((ROWS, EXTRA), lambda n: (0, 0))],
        out_shape=[
            jax.ShapeDtypeStruct((ROWS, FF), BF16),
            jax.ShapeDtypeStruct((ROWS, FF), BF16),
            jax.ShapeDtypeStruct((ROWS, EXTRA), BF16),
        ],
        scratch_shapes=[pltpu.VMEM((ROWS, EXTRA), F32)],
        compiler_params=params(),
        cost_estimate=cost(ROWS * D * FF, 12_000_000),
    )(me, second, wd_t, h, f, a, b)


def pair_kernel(dg_ref, du_ref, wg_ref, wu_ref, gg_ref, after_ref, out_ref):
    n = pl.program_id(0)
    width = wg_ref.shape[1]
    value = dot(dg_ref[...], wg_ref[...]) + dot(du_ref[...], wu_ref[...])
    out_ref[:, pl.ds(pl.multiple_of(n * width, width), width)] = value.astype(BF16)

    @pl.when(n == 0)
    def _():
        out_ref[:, D:] = gg_ref[...]


def pair_grads(dg, du, wg_t, wu_t, gg, after):
    width = 512
    whole = pl.BlockSpec((ROWS, FF), lambda n: (0, 0))
    weight = pl.BlockSpec((FF, width), lambda n: (0, n))
    return pl.pallas_call(
        pair_kernel,
        grid=(D // width,),
        in_specs=[
            whole,
            whole,
            weight,
            weight,
            pl.BlockSpec((ROWS, EXTRA), lambda n: (0, 0)),
            pl.BlockSpec(memory_space=pl.ANY),
        ],
        out_specs=pl.BlockSpec((ROWS, D + EXTRA), lambda n: (0, 0)),
        out_shape=jax.ShapeDtypeStruct((ROWS, D + EXTRA), BF16),
        compiler_params=params(28),
        cost_estimate=cost(4 * ROWS * D * FF, 12_000_000),
    )(dg, du, wg_t, wu_t, gg, after)


def outer_kernel(at_ref, bt_ref, a_ref, b_ref, after_ref, out_ref):
    value = dot(at_ref[...], a_ref[...]) + dot(bt_ref[...], b_ref[...])
    out_ref[...] = value.astype(BF16)


def outer_sum(own_t, other_t, own, other, n, at, after, total=None):
    m, width = own_t.shape[0], 256
    own_at, other_at, out_at = (place // width for place in at)
    left = pl.BlockSpec((m, ROWS), lambda j: (0, 0))
    return pl.pallas_call(
        outer_kernel,
        grid=(n // width,),
        in_specs=[
            left,
            left,
            pl.BlockSpec((ROWS, width), lambda j: (0, j + own_at)),
            pl.BlockSpec((ROWS, width), lambda j: (0, j + other_at)),
            pl.BlockSpec(memory_space=pl.ANY),
        ],
        out_specs=pl.BlockSpec((m, width), lambda j: (0, j + out_at)),
        out_shape=jax.ShapeDtypeStruct((m, total or n), BF16),
        input_output_aliases={4: 0} if out_at else {},
        compiler_params=params(28),
        cost_estimate=cost(4 * ROWS * m * n, 2 * (m * n + 2 * ROWS * (m + n))),
    )(own_t, other_t, own, other, after)


def combine_kernel(ids_ref, gates_ref, rows_ref, extra_ref, tok_ref, gate_ref, slots):
    @pl.when(pl.program_id(0) == 0)
    def _():
        matrix = slot_matrix(ids_ref[...])
        slots[...] = matrix
        by_expert = dot(extra_ref[...], matrix, 0, 0)
        value = by_expert[:N_EXP] + by_expert[N_EXP : 2 * N_EXP]
        expert = lax.broadcasted_iota(jnp.int32, (N_EXP, N_TOK), 0)
        choice = lax.broadcasted_iota(jnp.int32, (4, N_TOK), 0)
        grads = jnp.zeros((4, N_TOK), F32)
        for k in range(4):
            mine = jnp.where(ids_ref[k : k + 1, :] == expert, value, 0.0)
            grads = jnp.where(choice == k, jnp.sum(mine, axis=0, keepdims=True), grads)
        gate_ref[...] = (grads / gates_ref[...].astype(F32)).astype(BF16)

    tok_ref[...] = dot(slots[...], rows_ref[...], 0, 0).astype(BF16)


def combine(ids_t, gates_t, rows):
    width = 512
    small = pl.BlockSpec((4, N_TOK), lambda n: (0, 0))
    return pl.pallas_call(
        combine_kernel,
        grid=(D // width,),
        in_specs=[
            small,
            small,
            pl.BlockSpec((ROWS, width), lambda n: (0, n)),
            pl.BlockSpec((ROWS, EXTRA), lambda n: (0, D // EXTRA)),
        ],
        out_specs=[pl.BlockSpec((N_TOK, width), lambda n: (0, n)), small],
        out_shape=[
            jax.ShapeDtypeStruct((N_TOK, D), BF16),
            jax.ShapeDtypeStruct((4, N_TOK), BF16),
        ],
        scratch_shapes=[pltpu.VMEM((ROWS, N_TOK), BF16)],
        compiler_params=params(28),
        cost_estimate=cost(2 * ROWS * N_TOK * D, 2 * ROWS * D),
    )(ids_t, gates_t, rows, rows)


def exchange_experts(rows):
    width = rows.shape[1]
    moved = lax.all_to_all(
        rows.reshape(N_EXP, CAP, width), "expert", split_axis=0, concat_axis=0, tiled=True
    )
    return moved.reshape(ROWS, width)


def hold_kernel(*refs):
    pass


def hold(a, *after, mib=60):
    place = pl.BlockSpec(memory_space=pl.ANY)
    return pl.pallas_call(
        hold_kernel,
        in_specs=[place] * (1 + len(after)),
        out_specs=place,
        out_shape=jax.ShapeDtypeStruct(a.shape, a.dtype),
        input_output_aliases={0: 0},
        compiler_params=params(mib),
    )(a, *after)


def swap_cores(a):
    return lax.ppermute(a, "dp", [(i, i ^ 1) for i in range(2 * N_Z)])


def pick(a, index):
    return lax.dynamic_index_in_dim(a, index, 0, keepdims=False)


ROUTE = tuple((2 * i, 2 * ((i + 1) % N_Z)) for i in range(N_Z)) + tuple(
    (2 * i + 1, 2 * ((i - 1) % N_Z) + 1) for i in range(N_Z)
)


def ring_step(g, held, z, sign, step):
    if step == 1:
        held = pick(g, (z - sign) & (N_Z - 1))
    came = lax.ppermute(held, "dp", ROUTE)
    block = pick(g, (z - (step + 1) * sign) & (N_Z - 1))
    return (came.astype(F32) + block.astype(F32)).astype(BF16)


def body(tokens, out_grad, gates, expert_ids, w_gate, w_up, w_down):
    dp = lax.axis_index("dp").astype(jnp.int32)
    z, core = dp >> 1, dp & 1
    sign = 1 - 2 * core
    core_arg = core.reshape(1)
    me = lax.axis_index("expert").astype(jnp.int32).reshape(1)
    ids_t, gates_t = expert_ids.T, gates.T

    second_rows = second_dispatch(core_arg, ids_t, gates_t, out_grad)
    first = exchange_experts(first_dispatch(core_arg, ids_t, gates_t, tokens, out_grad))
    down_t = turn_down(core_arg, w_down)
    gate_t, up_t = turn_up(w_gate, w_up)
    second = exchange_experts(hold(second_rows, first, down_t, gate_t))

    hidden_t, hidden, factor, active, back = forward(first, w_gate, w_up, down_t)
    hidden_other_t = swap_cores(hidden_t)
    first_other = swap_cores(first[:, D + Q :])
    x_own, x_theirs = split_transposed(core_arg, first)
    x_other = swap_cores(x_theirs)
    part_low = outer_sum(hidden_t, hidden_other_t, first, first_other, Q, (D, 0, 0), first, H)

    second = hold(second, part_low, x_other)
    second_other = swap_cores(second)
    d_gate, d_up, prob = backward(me, second, down_t, hidden, factor, active, back)
    d_gate_other, d_up_other = swap_cores(d_gate), swap_cores(d_up)
    part_down = outer_sum(
        hidden_t, hidden_other_t, second, second_other, Q, (0, Q, Q), part_low, H
    )
    pairs = pair_grads(d_gate, d_up, gate_t, up_t, prob, part_down)
    part_gate = outer_sum(x_own, x_other, d_gate, d_gate_other, FF, (0, 0, 0), pairs)
    part_up = outer_sum(x_own, x_other, d_up, d_up_other, FF, (0, 0, 0), pairs)
    pairs = hold(pairs, part_gate, part_up, mib=1)
    rows = exchange_experts(pairs)
    token_grad, gate_grad_t = combine(ids_t, gates_t, rows)

    part_down = part_down.reshape(N_Z, FF // N_Z, H)
    part_gate = part_gate.reshape(N_Z, D // (2 * N_Z), FF)
    part_up = part_up.reshape(N_Z, D // (2 * N_Z), FF)
    sum_down = sum_gate = sum_up = None
    for step in range(1, N_Z):
        sum_down = ring_step(part_down, sum_down, z, sign, step)
        sum_gate = ring_step(part_gate, sum_gate, z, sign, step)
        sum_up = ring_step(part_up, sum_up, z, sign, step)
        if step == 1:
            sum_down = hold(sum_down, pairs, mib=1)
        if step == 6:
            sum_down = hold(sum_down, token_grad, mib=1)

    halves = sum_down.reshape(2, FF // (2 * N_Z), H)
    mine = pick(halves, core)
    theirs = swap_cores(pick(halves, 1 - core))
    left = jnp.where(core == 0, mine, theirs)
    right = jnp.where(core == 0, theirs, mine)
    grad_down = jnp.concatenate([left, right], axis=1)
    return token_grad, gate_grad_t.T, sum_gate[None], sum_up[None], grad_down[None]


def solution(mesh):
    both = P(("dp", "expert"), None)
    weight = P("expert", None, None)
    grad = P("expert", "dp", None)
    return jax.shard_map(
        body,
        mesh=mesh,
        in_specs=(both, both, both, both, weight, weight, weight),
        out_specs=(both, both, grad, grad, grad),
        check_vma=False,
    )
```

```python
import functools

import jax
import jax.numpy as jnp
from jax import lax
from jax.experimental import pallas as pl
from jax.experimental.pallas import tpu as pltpu
from jax.sharding import PartitionSpec as P

F32 = jnp.float32
BF16 = jnp.bfloat16
N_TOK = 128
D = 2048
FF = 768
CAP = 40
N_EXP = 16
ROWS = N_EXP * CAP
N_Z = 8
EXTRA = 128
CHUNK = 160
FULL = 64
H = D // 2
Q = D // 4


def params(mib=FULL):
    return pltpu.CompilerParams(vmem_limit_bytes=mib * 1024 * 1024)


def cost(flops, nbytes):
    return pl.CostEstimate(flops=int(flops), bytes_accessed=int(nbytes), transcendentals=0)


def dot(a, b, ca=1, cb=0):
    return lax.dot_general(a, b, (((ca,), (cb,)), ((), ())), preferred_element_type=F32)


def slot_matrix(ids_t, gates_t=None):
    expert = lax.broadcasted_iota(jnp.int32, (N_EXP, N_TOK), 0)
    member = jnp.zeros((N_EXP, N_TOK), F32)
    weight = jnp.zeros((N_EXP, N_TOK), F32)
    for k in range(4):
        hit = ids_t[k : k + 1, :] == expert
        member = jnp.where(hit, 1.0, member)
        if gates_t is not None:
            weight = jnp.where(hit, gates_t[k : k + 1, :].astype(F32), weight)
    row = lax.broadcasted_iota(jnp.int32, (N_TOK, N_TOK), 0)
    col = lax.broadcasted_iota(jnp.int32, (N_TOK, N_TOK), 1)
    before = jnp.where(row < col, 1.0, 0.0).astype(BF16)
    position = dot(member.astype(BF16), before)
    code = jnp.where(member > 0.0, position, -1.0)
    slot = lax.broadcasted_iota(jnp.int32, (CAP, N_TOK), 0).astype(F32)
    pieces = []
    for e in range(N_EXP):
        value = 1.0 if gates_t is None else weight[e : e + 1, :]
        pieces.append(jnp.where(code[e : e + 1, :] == slot, value, 0.0))
    return jnp.concatenate(pieces, axis=0).astype(BF16)


ANY = pl.BlockSpec(memory_space=pl.ANY)
SMEM = pl.BlockSpec(memory_space=pltpu.SMEM)


def shape(*dims):
    return jax.ShapeDtypeStruct(dims, BF16)


def vmem(*dims, dtype=BF16):
    return pltpu.VMEM(dims, dtype)


def start(sems, at, source, target):
    copy = pltpu.make_async_copy(source, target, sems.at[at])
    copy.start()
    return copy


def start_sorted(sems, at, core, source, target, rows):
    copies = []
    for kind in range(2):
        for b in range(N_Z):
            place = b * 256 + kind * 128 + core * (128 - 256 * kind)
            place = pl.ds(pl.multiple_of(place, 128), 128)
            to = pl.ds(kind * H + b * 128, 128)
            if rows:
                pair = source.at[place, :], target.at[to, :]
            else:
                pair = source.at[:, place], target.at[:, to]
            copies.append(start(sems, at + kind * N_Z + b, *pair))
    return copies


def wait(copies):
    for copy in copies:
        copy.wait()


def dispatch_kernel(core_ref, ids_hbm, gates_hbm, x_hbm, dy_hbm, out_hbm, ids, gates, x, dy, slots, gated, out, sems, out_sems):
    core = core_ref[0]
    own = pl.multiple_of(core * H, H)
    other = pl.multiple_of((1 - core) * H, H)
    few = [start(sems, 0, ids_hbm, ids), start(sems, 1, gates_hbm, gates)]
    loads = start_sorted(sems, 4, core, x_hbm, x, False)
    loads.append(start(sems, 2, dy_hbm.at[:, pl.ds(own, H)], dy.at[:, :H]))
    loads.append(start(sems, 3, dy_hbm.at[:, pl.ds(other, H)], dy.at[:, H:]))
    wait(few)
    slots[...] = slot_matrix(ids[...])
    gated[...] = slot_matrix(ids[...], gates[...])
    wait(loads)
    stores = []
    for i in range(ROWS // CHUNK):
        part = slice(i * CHUNK, (i + 1) * CHUNK)
        for half in range(2):
            at = slice(half * H, (half + 1) * H)
            out[part, 2 * half * H : (2 * half + 1) * H] = dot(slots[part, :], x[:, at]).astype(BF16)
            out[part, (2 * half + 1) * H : (2 * half + 2) * H] = dot(gated[part, :], dy[:, at]).astype(BF16)
        stores.append(start(out_sems, i, out.at[part, :], out_hbm.at[part, :]))
    wait(stores)


def dispatch(core, ids_t, gates_t, x, dy):
    return pl.pallas_call(
        dispatch_kernel,
        in_specs=[SMEM, ANY, ANY, ANY, ANY],
        out_specs=ANY,
        out_shape=shape(ROWS, 2 * D),
        scratch_shapes=[
            vmem(4, N_TOK, dtype=jnp.int32),
            vmem(4, N_TOK),
            vmem(N_TOK, D),
            vmem(N_TOK, D),
            vmem(ROWS, N_TOK),
            vmem(ROWS, N_TOK),
            vmem(ROWS, 2 * D),
            pltpu.SemaphoreType.DMA((20,)),
            pltpu.SemaphoreType.DMA((ROWS // CHUNK,)),
        ],
        compiler_params=params(),
        cost_estimate=cost(4 * ROWS * N_TOK * D, 4 * ROWS * D),
    )(core, ids_t, gates_t, x, dy)


def down_turn_kernel(core_ref, w_ref, out_ref):
    out_ref[...] = w_ref[0].T


def turn_down(core, w):
    def quarter(n, c):
        return 0, 0, jnp.where(n < 2, 2 * c[0], 2 - 2 * c[0]) + n % 2

    return pl.pallas_call(
        down_turn_kernel,
        grid_spec=pltpu.PrefetchScalarGridSpec(
            num_scalar_prefetch=1,
            grid=(4,),
            in_specs=[pl.BlockSpec((1, FF, Q), quarter)],
            out_specs=pl.BlockSpec((Q, FF), lambda n, c: (n, 0)),
        ),
        out_shape=jax.ShapeDtypeStruct((D, FF), BF16),
        compiler_params=params(),
        cost_estimate=cost(0, 4 * D * FF),
    )(core, w)


def up_turn_kernel(g_ref, u_ref, gt_ref, ut_ref):
    gt_ref[0] = g_ref[0].T
    ut_ref[0] = u_ref[0].T


def turn_up(wg, wu):
    weight = pl.BlockSpec((1, Q, FF), lambda n: (0, n, 0))
    out = pl.BlockSpec((1, FF, Q), lambda n: (n, 0, 0))
    turned = jax.ShapeDtypeStruct((4, FF, Q), BF16)
    return pl.pallas_call(
        up_turn_kernel,
        grid=(4,),
        in_specs=[weight, weight],
        out_specs=[out, out],
        out_shape=[turned, turned],
        compiler_params=params(),
        cost_estimate=cost(0, 8 * D * FF),
    )(wg, wu)


def expert_kernel(
    me_ref, core_ref, rows_hbm, wg_hbm, wu_hbm, wd_hbm, xt_hbm, ht_hbm, dg_hbm, du_hbm, gg_hbm,
    x, dy, wg, wu, wd, g_all, a_all, h_all, f_all, xt, ht, dg, du, gg, sems, out_sems,
):
    core = core_ref[0]
    x_loads = [start(sems, i, rows_hbm.at[:, pl.ds(i * D, H)], x.at[:, pl.ds(i * H, H)]) for i in range(2)]
    wg_loads = start_sorted(sems, 5, core, wg_hbm.at[0], wg, True)
    wu_loads = start_sorted(sems, 21, core, wu_hbm.at[0], wu, True)
    b_loads = [start(sems, 2 + i, rows_hbm.at[:, pl.ds(i * D + H, H)], dy.at[:, pl.ds(i * H, H)]) for i in range(2)]
    b_loads.append(start(sems, 4, wd_hbm, wd))
    stores = []
    wait(x_loads)
    wait(wg_loads)
    for n in range(3):
        at = slice(n * 256, (n + 1) * 256)
        g_all[:, at] = dot(x[...], wg[:, at])
    for b in range(N_Z):
        xt[b * 128 : (b + 1) * 128, :] = x[:, b * 128 : (b + 1) * 128].T
    stores.append(start(out_sems, 0, xt, xt_hbm))
    wait(wu_loads)
    for n in range(3):
        at = slice(n * 256, (n + 1) * 256)
        u = dot(x[...], wu[:, at])
        g = g_all[:, at]
        s = jax.nn.sigmoid(g)
        a = g * s
        h = a * u
        a_all[:, at] = a
        h_all[:, at] = h
        f_all[:, at] = u * s * (1.0 + g * (1.0 - s))
        ht[at, :] = h.astype(BF16).T
        stores.append(start(out_sems, 1 + n, ht.at[at, :], ht_hbm.at[at, :]))
    wait(b_loads)
    total = jnp.zeros((ROWS, 1), F32)
    for n in range(3):
        at = slice(n * 256, (n + 1) * 256)
        b = dot(dy[...], wd[:, at])
        dg[n] = (b * f_all[:, at]).astype(BF16)
        du[n] = (b * a_all[:, at]).astype(BF16)
        stores.append(start(out_sems, 4 + n, dg.at[n], dg_hbm.at[n]))
        stores.append(start(out_sems, 7 + n, du.at[n], du_hbm.at[n]))
        total = total + jnp.sum(b * h_all[:, at], axis=1, keepdims=True)
    value = jnp.broadcast_to(total, (ROWS, EXTRA))
    high = value.astype(BF16).astype(F32)
    col = lax.broadcasted_iota(jnp.int32, (ROWS, EXTRA), 1)
    me = me_ref[0]
    low = jnp.where(col == me + N_EXP, value - high, 0.0)
    gg[...] = jnp.where(col == me, high, low).astype(BF16)
    stores.append(start(out_sems, 10, gg, gg_hbm))
    wait(stores)


def expert(me, core, rows, wg, wu, wd_t):
    return pl.pallas_call(
        expert_kernel,
        in_specs=[SMEM, SMEM, ANY, ANY, ANY, ANY],
        out_specs=[ANY] * 5,
        out_shape=[
            shape(H, ROWS),
            shape(FF, ROWS),
            shape(3, ROWS, 256),
            shape(3, ROWS, 256),
            shape(ROWS, EXTRA),
        ],
        scratch_shapes=[
            vmem(ROWS, D),
            vmem(ROWS, D),
            vmem(D, FF),
            vmem(D, FF),
            vmem(D, FF),
            vmem(ROWS, FF, dtype=F32),
            vmem(ROWS, FF, dtype=F32),
            vmem(ROWS, FF, dtype=F32),
            vmem(ROWS, FF, dtype=F32),
            vmem(H, ROWS),
            vmem(FF, ROWS),
            vmem(3, ROWS, 256),
            vmem(3, ROWS, 256),
            vmem(ROWS, EXTRA),
            pltpu.SemaphoreType.DMA((37,)),
            pltpu.SemaphoreType.DMA((11,)),
        ],
        compiler_params=params(),
        cost_estimate=cost(6 * ROWS * D * FF, 18_000_000),
    )(me, core, rows, wg, wu, wd_t)


def pair_kernel(
    dg_hbm, du_hbm, wg_hbm, wu_hbm, gg_hbm, other_hbm, out_hbm, xt_hbm, dg, du, wg, wu, x, xt, out, sems, out_sems
):
    stores = [start(out_sems, 5, gg_hbm, out_hbm.at[:, pl.ds(D, EXTRA)])]
    d_loads = [start(sems, n, dg_hbm.at[n], dg.at[:, pl.ds(n * 256, 256)]) for n in range(3)]
    d_loads += [start(sems, 3 + n, du_hbm.at[n], du.at[:, pl.ds(n * 256, 256)]) for n in range(3)]
    w_loads = [
        (start(sems, 6 + n, wg_hbm.at[n], wg.at[n]), start(sems, 10 + n, wu_hbm.at[n], wu.at[n])) for n in range(4)
    ]
    x_load = start(sems, 14, other_hbm.at[:, pl.ds(0, H)], x)
    wait(d_loads)
    for n in range(4):
        if n == 2:
            x_load.wait()
        wait(w_loads[n])
        value = dot(dg[...], wg[n]) + dot(du[...], wu[n])
        out[n] = value.astype(BF16)
        stores.append(start(out_sems, n, out.at[n], out_hbm.at[:, pl.ds(n * Q, Q)]))
        if n >= 2:
            for b in range(4 * n - 8, 4 * n - 4):
                xt[b * 128 : (b + 1) * 128, :] = x[:, b * 128 : (b + 1) * 128].T
    stores.append(start(out_sems, 4, xt, xt_hbm))
    wait(stores)


def pair_grads(dg, du, wg_t, wu_t, gg, other):
    return pl.pallas_call(
        pair_kernel,
        in_specs=[ANY] * 6,
        out_specs=[ANY] * 2,
        out_shape=[shape(ROWS, D + EXTRA), shape(H, ROWS)],
        scratch_shapes=[
            vmem(ROWS, FF),
            vmem(ROWS, FF),
            vmem(4, FF, Q),
            vmem(4, FF, Q),
            vmem(ROWS, H),
            vmem(H, ROWS),
            vmem(4, ROWS, Q),
            pltpu.SemaphoreType.DMA((15,)),
            pltpu.SemaphoreType.DMA((6,)),
        ],
        compiler_params=params(),
        cost_estimate=cost(4 * ROWS * D * FF, 14_000_000),
    )(dg, du, wg_t, wu_t, gg, other)


def outer_kernel(blocked, own_t_hbm, other_t_hbm, own_hbm, other_hbm, after_hbm, out_hbm, flag_ref, left, right, out, sems, out_sems):
    flag_ref[...] = jnp.zeros_like(flag_ref)
    loads = [
        start(sems, 0, own_t_hbm, left.at[:, pl.ds(0, ROWS)]),
        start(sems, 1, other_t_hbm, left.at[:, pl.ds(ROWS, ROWS)]),
    ]
    pieces = []
    for n in range(out.shape[0]):
        pair = []
        for i, source in enumerate((own_hbm, other_hbm)):
            part = source.at[n] if blocked else source.at[:, pl.ds(H + n * 256, 256)]
            pair.append(start(sems, 2 + 2 * n + i, part, right.at[n, pl.ds(i * ROWS, ROWS), :]))
        pieces.append(pair)
    wait(loads)
    stores = []
    for n in range(out.shape[0]):
        wait(pieces[n])
        out[n] = dot(left[...], right[n]).astype(BF16)
        stores.append(start(out_sems, n, out.at[n], out_hbm.at[:, pl.ds(n * 256, 256)]))
    wait(stores)


def outer_sum(own_t, other_t, own, other, blocked, after):
    m, blocks = own_t.shape[0], 3 if blocked else 4
    return pl.pallas_call(
        functools.partial(outer_kernel, blocked),
        in_specs=[ANY] * 5,
        out_specs=[ANY, pl.BlockSpec(memory_space=pltpu.VMEM)],
        out_shape=[shape(m, blocks * 256), shape(16, 128)],
        scratch_shapes=[
            vmem(m, 2 * ROWS),
            vmem(blocks, 2 * ROWS, 256),
            vmem(blocks, m, 256),
            pltpu.SemaphoreType.DMA((2 + 2 * blocks,)),
            pltpu.SemaphoreType.DMA((blocks,)),
        ],
        compiler_params=params(),
        cost_estimate=cost(4 * ROWS * m * blocks * 256, 2 * ROWS * (2 * m + blocks * 512)),
    )(own_t, other_t, own, other, after)


def combine_kernel(ids_hbm, gates_hbm, rows_hbm, tok_hbm, gate_hbm, ids, gates, rows, extra, tok, gate, sems, out_sems):
    few = [start(sems, 0, ids_hbm, ids), start(sems, 1, gates_hbm, gates)]
    extra_load = start(sems, 2, rows_hbm.at[:, pl.ds(D, EXTRA)], extra)
    loads = [start(sems, 3 + n, rows_hbm.at[:, pl.ds(n * Q, Q)], rows.at[n]) for n in range(4)]
    wait(few)
    slots = slot_matrix(ids[...])
    stores = []
    for n in range(4):
        loads[n].wait()
        tok[:, n * Q : (n + 1) * Q] = dot(slots, rows[n], 0, 0).astype(BF16)
    stores.append(start(out_sems, 0, tok, tok_hbm))
    extra_load.wait()
    by_expert = dot(extra[...], slots, 0, 0)
    value = by_expert[:N_EXP] + by_expert[N_EXP : 2 * N_EXP]
    expert_at = lax.broadcasted_iota(jnp.int32, (N_EXP, N_TOK), 0)
    choice = lax.broadcasted_iota(jnp.int32, (4, N_TOK), 0)
    grads = jnp.zeros((4, N_TOK), F32)
    for k in range(4):
        mine = jnp.where(ids[k : k + 1, :] == expert_at, value, 0.0)
        grads = jnp.where(choice == k, jnp.sum(mine, axis=0, keepdims=True), grads)
    gate[...] = (grads / gates[...].astype(F32)).astype(BF16)
    stores.append(start(out_sems, 1, gate, gate_hbm))
    wait(stores)


def combine(ids_t, gates_t, rows):
    return pl.pallas_call(
        combine_kernel,
        in_specs=[ANY] * 3,
        out_specs=[ANY] * 2,
        out_shape=[shape(N_TOK, D), shape(4, N_TOK)],
        scratch_shapes=[
            vmem(4, N_TOK, dtype=jnp.int32),
            vmem(4, N_TOK),
            vmem(4, ROWS, Q),
            vmem(ROWS, EXTRA),
            vmem(N_TOK, D),
            vmem(4, N_TOK),
            pltpu.SemaphoreType.DMA((7,)),
            pltpu.SemaphoreType.DMA((2,)),
        ],
        compiler_params=params(16),
        cost_estimate=cost(2 * ROWS * N_TOK * D, 2 * ROWS * D),
    )(ids_t, gates_t, rows)


def exchange_experts(rows):
    width = rows.shape[1]
    moved = lax.all_to_all(
        rows.reshape(N_EXP, CAP, width), "expert", split_axis=0, concat_axis=0, tiled=True
    )
    return moved.reshape(ROWS, width)


def hold_kernel(*refs):
    pass


def hold(a, *after, mib=1):
    place = pl.BlockSpec(memory_space=pl.ANY)
    return pl.pallas_call(
        hold_kernel,
        in_specs=[place] * (1 + len(after)),
        out_specs=place,
        out_shape=jax.ShapeDtypeStruct(a.shape, a.dtype),
        input_output_aliases={0: 0},
        compiler_params=params(mib),
    )(a, *after)


def swap_cores(a):
    return lax.ppermute(a, "dp", [(i, i ^ 1) for i in range(2 * N_Z)])


def pick(a, index):
    return lax.dynamic_index_in_dim(a, index, 0, keepdims=False)


ROUTE = tuple((2 * i, 2 * ((i + 1) % N_Z)) for i in range(N_Z)) + tuple(
    (2 * i + 1, 2 * ((i - 1) % N_Z) + 1) for i in range(N_Z)
)


def ring_step(g, held, z, sign, step, after=None):
    if step == 1:
        held = pick(g, (z - sign) & (N_Z - 1))
    came = lax.ppermute(held, "dp", ROUTE)
    if after is not None:
        came = hold(came, after)
    block = pick(g, (z - (step + 1) * sign) & (N_Z - 1))
    return (came.astype(F32) + block.astype(F32)).astype(BF16)


def body(tokens, out_grad, gates, expert_ids, w_gate, w_up, w_down):
    dp = lax.axis_index("dp").astype(jnp.int32)
    z, core = dp >> 1, dp & 1
    sign = 1 - 2 * core
    core_arg = core.reshape(1)
    me = lax.axis_index("expert").astype(jnp.int32).reshape(1)
    ids_t, gates_t = expert_ids.T, gates.T

    down_t = turn_down(core_arg, w_down)
    gate_t, up_t = turn_up(w_gate, w_up)
    rows = exchange_experts(dispatch(core_arg, ids_t, gates_t, tokens, out_grad))

    rows = hold(rows, down_t, up_t, mib=FULL)
    theirs = swap_cores(rows[:, D:])
    x_own, hidden_t, d_gate, d_up, prob = expert(me, core_arg, rows, w_gate, w_up, down_t)
    hidden_other_t = swap_cores(hidden_t)
    d_gate_other, d_up_other = swap_cores(d_gate), swap_cores(d_up)
    pairs, x_other = pair_grads(d_gate, d_up, gate_t, up_t, prob, theirs)
    part_down, flag = outer_sum(hidden_t, hidden_other_t, rows, theirs, False, pairs)
    part_gate, flag = outer_sum(x_own, x_other, d_gate, d_gate_other, True, flag)
    part_up, flag = outer_sum(x_own, x_other, d_up, d_up_other, True, flag)
    pairs = hold(pairs, flag, mib=FULL)
    back_rows = exchange_experts(pairs)
    token_grad, gate_grad_t = combine(ids_t, gates_t, back_rows)

    part_down = part_down.reshape(N_Z, FF // N_Z, H)
    part_gate = part_gate.reshape(N_Z, D // (2 * N_Z), FF)
    part_up = part_up.reshape(N_Z, D // (2 * N_Z), FF)
    sum_down = sum_gate = sum_up = None
    for step in range(1, N_Z):
        sum_down = ring_step(part_down, sum_down, z, sign, step)
        sum_gate = ring_step(part_gate, sum_gate, z, sign, step)
        sum_up = ring_step(part_up, sum_up, z, sign, step, gate_grad_t if step == 7 else None)
        if step == 1:
            sum_down = hold(sum_down, flag)

    halves = sum_down.reshape(2, FF // (2 * N_Z), H)
    mine = pick(halves, core)
    theirs = swap_cores(pick(halves, 1 - core))
    left = jnp.where(core == 0, mine, theirs)
    right = jnp.where(core == 0, theirs, mine)
    grad_down = jnp.concatenate([left, right], axis=1)
    return token_grad, gate_grad_t.T, sum_gate[None], sum_up[None], grad_down[None]


def solution(mesh):
    both = P(("dp", "expert"), None)
    weight = P("expert", None, None)
    grad = P("expert", "dp", None)
    return jax.shard_map(
        body,
        mesh=mesh,
        in_specs=(both, both, both, both, weight, weight, weight),
        out_specs=(both, both, grad, grad, grad),
        check_vma=False,
    )
```

```python
import jax
import jax.numpy as jnp
from jax import lax
from jax.experimental import pallas as pl
from jax.experimental.pallas import tpu as pltpu
from jax.sharding import PartitionSpec as P

F32 = jnp.float32
BF16 = jnp.bfloat16
N_TOK = 128
D = 2048
FF = 768
CAP = 40
N_EXP = 16
ROWS = N_EXP * CAP
N_Z = 8
EXTRA = 128
CHUNK = 160
FULL = 64
MID = 26
H = D // 2
Q = D // 4


def params(mib=FULL):
    return pltpu.CompilerParams(vmem_limit_bytes=mib * 1024 * 1024)


def cost(flops, nbytes):
    return pl.CostEstimate(flops=int(flops), bytes_accessed=int(nbytes), transcendentals=0)


def dot(a, b, ca=1, cb=0):
    return lax.dot_general(a, b, (((ca,), (cb,)), ((), ())), preferred_element_type=F32)


def slot_matrix(ids_t, gates_t=None):
    expert = lax.broadcasted_iota(jnp.int32, (N_EXP, N_TOK), 0)
    member = jnp.zeros((N_EXP, N_TOK), F32)
    weight = jnp.zeros((N_EXP, N_TOK), F32)
    for k in range(4):
        hit = ids_t[k : k + 1, :] == expert
        member = jnp.where(hit, 1.0, member)
        if gates_t is not None:
            weight = jnp.where(hit, gates_t[k : k + 1, :].astype(F32), weight)
    row = lax.broadcasted_iota(jnp.int32, (N_TOK, N_TOK), 0)
    col = lax.broadcasted_iota(jnp.int32, (N_TOK, N_TOK), 1)
    before = jnp.where(row < col, 1.0, 0.0).astype(BF16)
    position = dot(member.astype(BF16), before)
    code = jnp.where(member > 0.0, position, -1.0)
    slot = lax.broadcasted_iota(jnp.int32, (CAP, N_TOK), 0).astype(F32)
    pieces = []
    for e in range(N_EXP):
        value = 1.0 if gates_t is None else weight[e : e + 1, :]
        pieces.append(jnp.where(code[e : e + 1, :] == slot, value, 0.0))
    return jnp.concatenate(pieces, axis=0).astype(BF16)


ANY = pl.BlockSpec(memory_space=pl.ANY)
SMEM = pl.BlockSpec(memory_space=pltpu.SMEM)


def shape(*dims):
    return jax.ShapeDtypeStruct(dims, BF16)


def vmem(*dims, dtype=BF16):
    return pltpu.VMEM(dims, dtype)


def start(sems, at, source, target):
    copy = pltpu.make_async_copy(source, target, sems.at[at])
    copy.start()
    return copy


def wait(copies):
    for copy in copies:
        copy.wait()


def dispatch_kernel(core_ref, ids_hbm, gates_hbm, x_hbm, out_hbm, ids, gates, x, slots, out, sems, out_sems):
    few = [start(sems, 0, ids_hbm, ids)]
    if gates_hbm is None:
        loads = [start(sems, 2, x_hbm, x)]
    else:
        few.append(start(sems, 1, gates_hbm, gates))
        core = core_ref[0]
        own = pl.ds(pl.multiple_of(core * H, H), H)
        other = pl.ds(pl.multiple_of((1 - core) * H, H), H)
        loads = [
            start(sems, 2, x_hbm.at[:, own], x.at[:, pl.ds(0, H)]),
            start(sems, 3, x_hbm.at[:, other], x.at[:, pl.ds(H, H)]),
        ]
    wait(few)
    slots[...] = slot_matrix(ids[...], None if gates_hbm is None else gates[...])
    wait(loads)
    stores = []
    for i in range(ROWS // CHUNK):
        part = slice(i * CHUNK, (i + 1) * CHUNK)
        out[part, :] = dot(slots[part, :], x[...]).astype(BF16)
        stores.append(start(out_sems, i, out.at[part, :], out_hbm.at[part, :]))
    wait(stores)


def plain_kernel(core_ref, ids_hbm, x_hbm, *refs):
    dispatch_kernel(core_ref, ids_hbm, None, x_hbm, *refs)


def dispatch(core, ids_t, gates_t, x):
    plain = gates_t is None
    args = [core, ids_t] + ([] if plain else [gates_t]) + [x]
    return pl.pallas_call(
        plain_kernel if plain else dispatch_kernel,
        in_specs=[SMEM] + [ANY] * (len(args) - 1),
        out_specs=ANY,
        out_shape=shape(ROWS, D),
        scratch_shapes=[
            vmem(4, N_TOK, dtype=jnp.int32),
            vmem(4, N_TOK),
            vmem(N_TOK, D),
            vmem(ROWS, N_TOK),
            vmem(ROWS, D),
            pltpu.SemaphoreType.DMA((4,)),
            pltpu.SemaphoreType.DMA((ROWS // CHUNK,)),
        ],
        compiler_params=params(),
        cost_estimate=cost(2 * ROWS * N_TOK * D, 2 * ROWS * D),
    )(*args)


def down_turn_kernel(core_ref, w_ref, out_ref):
    out_ref[0] = w_ref[0].T


def turn_down(core, w):
    return pl.pallas_call(
        down_turn_kernel,
        grid_spec=pltpu.PrefetchScalarGridSpec(
            num_scalar_prefetch=1,
            grid=(3, 2),
            in_specs=[pl.BlockSpec((1, 256, H), lambda n, i, c: (0, n, i + c[0] - 2 * i * c[0]))],
            out_specs=pl.BlockSpec((1, H, 256), lambda n, i, c: (n, i, 0)),
        ),
        out_shape=shape(3, D, 256),
        compiler_params=params(),
        cost_estimate=cost(0, 4 * D * FF),
    )(core, w)


def up_turn_kernel(g_ref, u_ref, gt_ref, ut_ref):
    gt_ref[0] = g_ref[0].T
    ut_ref[0] = u_ref[0].T


def turn_up(wg, wu):
    weight = pl.BlockSpec((1, Q, FF), lambda n: (0, n, 0))
    out = pl.BlockSpec((1, FF, Q), lambda n: (n, 0, 0))
    turned = jax.ShapeDtypeStruct((4, FF, Q), BF16)
    return pl.pallas_call(
        up_turn_kernel,
        grid=(4,),
        in_specs=[weight, weight],
        out_specs=[out, out],
        out_shape=[turned, turned],
        compiler_params=params(),
        cost_estimate=cost(0, 8 * D * FF),
    )(wg, wu)


def forward_kernel(x_ref, wg_ref, wu_ref, ht_ref, h_ref, f_ref, a_ref):
    x = x_ref[...]
    g = dot(x, wg_ref[0])
    u = dot(x, wu_ref[0])
    s = jax.nn.sigmoid(g)
    a = g * s
    h = (a * u).astype(BF16)
    h_ref[0] = h
    ht_ref[...] = h.T
    a_ref[0] = a.astype(BF16)
    f_ref[0] = (u * s * (1.0 + g * (1.0 - s))).astype(BF16)


def forward(x, wg, wu):
    weight = pl.BlockSpec((1, D, 256), lambda n: (0, 0, n))
    out = pl.BlockSpec((1, ROWS, 256), lambda n: (n, 0, 0))
    return pl.pallas_call(
        forward_kernel,
        grid=(3,),
        in_specs=[pl.BlockSpec((ROWS, D), lambda n: (0, 0)), weight, weight],
        out_specs=[pl.BlockSpec((256, ROWS), lambda n: (n, 0)), out, out, out],
        out_shape=[shape(FF, ROWS)] + [shape(3, ROWS, 256)] * 3,
        compiler_params=params(MID),
        cost_estimate=cost(4 * ROWS * D * FF, 13_000_000),
    )(x, wg, wu)


def split_kernel(core_ref, mine_ref, theirs_ref, own_ref, other_ref):
    own_ref[...] = mine_ref[...].T
    other_ref[...] = theirs_ref[...].T


def split_transposed(core, first):
    out = pl.BlockSpec((128, ROWS), lambda n, c: (n, 0))
    return pl.pallas_call(
        split_kernel,
        grid_spec=pltpu.PrefetchScalarGridSpec(
            num_scalar_prefetch=1,
            grid=(N_Z,),
            in_specs=[
                pl.BlockSpec((ROWS, 128), lambda n, c: (0, 2 * n + c[0])),
                pl.BlockSpec((ROWS, 128), lambda n, c: (0, 2 * n + 1 - c[0])),
            ],
            out_specs=[out, out],
        ),
        out_shape=[shape(H, ROWS), shape(H, ROWS)],
        compiler_params=params(MID),
        cost_estimate=cost(0, 4 * ROWS * D),
    )(core, first, first)


def backward_kernel(me_ref, dy_ref, wd_ref, h_ref, f_ref, a_ref, dg_ref, du_ref, gg_ref, total):
    n = pl.program_id(0)
    b = dot(dy_ref[...], wd_ref[0])
    dg_ref[...] = (b * f_ref[0].astype(F32)).astype(BF16)
    du_ref[...] = (b * a_ref[0].astype(F32)).astype(BF16)
    part = jnp.sum(b * h_ref[0].astype(F32), axis=1, keepdims=True)
    part = jnp.broadcast_to(part, (ROWS, EXTRA))

    @pl.when(n == 0)
    def _():
        total[...] = part

    @pl.when(n > 0)
    def _():
        total[...] += part

    @pl.when(n == pl.num_programs(0) - 1)
    def _():
        value = total[...]
        high = value.astype(BF16).astype(F32)
        col = lax.broadcasted_iota(jnp.int32, (ROWS, EXTRA), 1)
        me = me_ref[0]
        low = jnp.where(col == me + N_EXP, value - high, 0.0)
        gg_ref[...] = jnp.where(col == me, high, low).astype(BF16)


def backward(me, dy, wd_t, h, f, a):
    block = pl.BlockSpec((1, ROWS, 256), lambda n: (n, 0, 0))
    part = pl.BlockSpec((ROWS, 256), lambda n: (0, n))
    return pl.pallas_call(
        backward_kernel,
        grid=(3,),
        in_specs=[
            SMEM,
            pl.BlockSpec((ROWS, D), lambda n: (0, 0)),
            pl.BlockSpec((1, D, 256), lambda n: (n, 0, 0)),
            block,
            block,
            block,
        ],
        out_specs=[part, part, pl.BlockSpec((ROWS, EXTRA), lambda n: (0, 0))],
        out_shape=[shape(ROWS, FF), shape(ROWS, FF), shape(ROWS, EXTRA)],
        scratch_shapes=[vmem(ROWS, EXTRA, dtype=F32)],
        compiler_params=params(),
        cost_estimate=cost(2 * ROWS * D * FF, 11_000_000),
    )(me, dy, wd_t, h, f, a)


def pair_kernel(*refs):
    dg_ref, du_ref, wg_ref, wu_ref, gg_ref, _, _, _, _, out_ref, flag_ref = refs
    n = pl.program_id(0)
    value = dot(dg_ref[...], wg_ref[0]) + dot(du_ref[...], wu_ref[0])
    out_ref[:, pl.ds(pl.multiple_of(n * Q, Q), Q)] = value.astype(BF16)
    flag_ref[...] = jnp.zeros_like(flag_ref)

    @pl.when(n == 0)
    def _():
        out_ref[:, D:] = gg_ref[...]


def pair_grads(half, dg, du, wg_t, wu_t, gg, pairs, after):
    size = ROWS // 2
    part = pl.BlockSpec((size, FF), lambda n: (half, 0))
    weight = pl.BlockSpec((1, FF, Q), lambda n: (n, 0, 0))
    return pl.pallas_call(
        pair_kernel,
        grid=(4,),
        in_specs=[part, part, weight, weight, pl.BlockSpec((size, EXTRA), lambda n: (half, 0))] + [ANY] * 4,
        out_specs=[
            pl.BlockSpec((size, D + EXTRA), lambda n: (half, 0)),
            pl.BlockSpec((16, 128), lambda n: (0, 0)),
        ],
        out_shape=[shape(ROWS, D + EXTRA), shape(16, 128)],
        input_output_aliases={5: 0} if half else {},
        compiler_params=params(MID),
        cost_estimate=cost(2 * ROWS * D * FF, 9_000_000),
    )(dg, du, wg_t, wu_t, gg, pairs, *after)


def outer_kernel(at_ref, bt_ref, a_ref, b_ref, after_ref, out_ref, flag_ref):
    value = dot(at_ref[...], a_ref[...]) + dot(bt_ref[...], b_ref[...])
    out_ref[...] = value.astype(BF16)
    flag_ref[...] = jnp.zeros_like(flag_ref)


def outer_sum(own_t, other_t, own, other, other_at, n, after):
    m, width = own_t.shape[0], 256
    left = pl.BlockSpec((m, ROWS), lambda j: (0, 0))
    return pl.pallas_call(
        outer_kernel,
        grid=(n // width,),
        in_specs=[
            left,
            left,
            pl.BlockSpec((ROWS, width), lambda j: (0, j)),
            pl.BlockSpec((ROWS, width), lambda j: (0, j + other_at // width)),
            ANY,
        ],
        out_specs=[
            pl.BlockSpec((m, width), lambda j: (0, j)),
            pl.BlockSpec((16, 128), lambda j: (0, 0)),
        ],
        out_shape=[shape(m, n), shape(16, 128)],
        compiler_params=params(MID),
        cost_estimate=cost(4 * ROWS * m * n, 2 * (m * n + 2 * ROWS * (m + n))),
    )(own_t, other_t, own, other, after)


def combine_kernel(ids_hbm, gates_hbm, rows_hbm, tok_hbm, gate_hbm, ids, gates, rows, extra, tok, gate, sems, out_sems):
    few = [start(sems, 0, ids_hbm, ids), start(sems, 1, gates_hbm, gates)]
    extra_load = start(sems, 2, rows_hbm.at[:, pl.ds(D, EXTRA)], extra)
    loads = [start(sems, 3 + n, rows_hbm.at[:, pl.ds(n * Q, Q)], rows.at[n]) for n in range(4)]
    wait(few)
    slots = slot_matrix(ids[...])
    stores = []
    for n in range(4):
        loads[n].wait()
        tok[:, n * Q : (n + 1) * Q] = dot(slots, rows[n], 0, 0).astype(BF16)
    stores.append(start(out_sems, 0, tok, tok_hbm))
    extra_load.wait()
    by_expert = dot(extra[...], slots, 0, 0)
    value = by_expert[:N_EXP] + by_expert[N_EXP : 2 * N_EXP]
    expert_at = lax.broadcasted_iota(jnp.int32, (N_EXP, N_TOK), 0)
    choice = lax.broadcasted_iota(jnp.int32, (4, N_TOK), 0)
    grads = jnp.zeros((4, N_TOK), F32)
    for k in range(4):
        mine = jnp.where(ids[k : k + 1, :] == expert_at, value, 0.0)
        grads = jnp.where(choice == k, jnp.sum(mine, axis=0, keepdims=True), grads)
    gate[...] = (grads / gates[...].astype(F32)).astype(BF16)
    stores.append(start(out_sems, 1, gate, gate_hbm))
    wait(stores)


def combine(ids_t, gates_t, rows):
    return pl.pallas_call(
        combine_kernel,
        in_specs=[ANY] * 3,
        out_specs=[ANY] * 2,
        out_shape=[shape(N_TOK, D), shape(4, N_TOK)],
        scratch_shapes=[
            vmem(4, N_TOK, dtype=jnp.int32),
            vmem(4, N_TOK),
            vmem(4, ROWS, Q),
            vmem(ROWS, EXTRA),
            vmem(N_TOK, D),
            vmem(4, N_TOK),
            pltpu.SemaphoreType.DMA((7,)),
            pltpu.SemaphoreType.DMA((2,)),
        ],
        compiler_params=params(16),
        cost_estimate=cost(2 * ROWS * N_TOK * D, 2 * ROWS * D),
    )(ids_t, gates_t, rows)


def exchange_experts(rows):
    width = rows.shape[1]
    moved = lax.all_to_all(
        rows.reshape(N_EXP, CAP, width), "expert", split_axis=0, concat_axis=0, tiled=True
    )
    return moved.reshape(ROWS, width)


def hold_kernel(*refs):
    pass


def hold(a, *after, mib=1):
    place = pl.BlockSpec(memory_space=pl.ANY)
    return pl.pallas_call(
        hold_kernel,
        in_specs=[place] * (1 + len(after)),
        out_specs=place,
        out_shape=jax.ShapeDtypeStruct(a.shape, a.dtype),
        input_output_aliases={0: 0},
        compiler_params=params(mib),
    )(a, *after)


def swap_cores(a):
    return lax.ppermute(a, "dp", [(i, i ^ 1) for i in range(2 * N_Z)])


def pick(a, index):
    return lax.dynamic_index_in_dim(a, index, 0, keepdims=False)


ROUTE = tuple((2 * i, 2 * ((i + 1) % N_Z)) for i in range(N_Z)) + tuple(
    (2 * i + 1, 2 * ((i - 1) % N_Z) + 1) for i in range(N_Z)
)


def ring_step(g, held, z, sign, step, after=None):
    if step == 1:
        held = pick(g, (z - sign) & (N_Z - 1))
    came = lax.ppermute(held, "dp", ROUTE)
    if after is not None:
        came = hold(came, after)
    block = pick(g, (z - (step + 1) * sign) & (N_Z - 1))
    return (came.astype(F32) + block.astype(F32)).astype(BF16)


def body(tokens, out_grad, gates, expert_ids, w_gate, w_up, w_down):
    dp = lax.axis_index("dp").astype(jnp.int32)
    z, core = dp >> 1, dp & 1
    sign = 1 - 2 * core
    core_arg = core.reshape(1)
    me = lax.axis_index("expert").astype(jnp.int32).reshape(1)
    ids_t, gates_t = expert_ids.T, gates.T

    down_t = turn_down(core_arg, w_down)
    gate_t, up_t = turn_up(w_gate, w_up)
    x = exchange_experts(dispatch(core_arg, ids_t, None, tokens))
    dy_rows = hold(dispatch(core_arg, ids_t, gates_t, out_grad), x, down_t, up_t, mib=FULL)
    dy = exchange_experts(dy_rows)

    hidden_t, hidden, factor, active = forward(x, w_gate, w_up)
    hidden_other_t = swap_cores(hidden_t)
    x_own, x_theirs = split_transposed(core_arg, x)
    x_other = swap_cores(x_theirs)

    dy = hold(dy, x_other, hidden_other_t, mib=FULL)
    dy_other = swap_cores(dy)
    d_gate, d_up, prob = backward(me, dy, down_t, hidden, factor, active)
    d_gate_other, d_up_other = swap_cores(d_gate), swap_cores(d_up)
    part_down, flag = outer_sum(hidden_t, hidden_other_t, dy, dy_other, H, H, prob)
    part_gate, flag = outer_sum(x_own, x_other, d_gate, d_gate_other, 0, FF, flag)
    part_up, flag = outer_sum(x_own, x_other, d_up, d_up_other, 0, FF, flag)

    part_down = part_down.reshape(N_Z, FF // N_Z, H)
    part_gate = part_gate.reshape(N_Z, D // (2 * N_Z), FF)
    part_up = part_up.reshape(N_Z, D // (2 * N_Z), FF)
    sum_down = ring_step(part_down, None, z, sign, 1)
    sum_gate = ring_step(part_gate, None, z, sign, 1)
    sum_up = ring_step(part_up, None, z, sign, 1)

    pairs, first_flag = pair_grads(0, d_gate, d_up, gate_t, up_t, prob, flag, (flag, flag, flag))
    pairs, flag = pair_grads(1, d_gate, d_up, gate_t, up_t, prob, pairs, (sum_down, sum_gate, sum_up))
    back_rows = exchange_experts(pairs)
    token_grad, gate_grad_t = combine(ids_t, gates_t, back_rows)

    sum_down = hold(sum_down, first_flag)
    for step in range(2, N_Z):
        sum_down = ring_step(part_down, sum_down, z, sign, step)
        sum_gate = ring_step(part_gate, sum_gate, z, sign, step)
        sum_up = ring_step(part_up, sum_up, z, sign, step, gate_grad_t if step == 6 else None)

    halves = sum_down.reshape(2, FF // (2 * N_Z), H)
    mine = pick(halves, core)
    theirs = swap_cores(pick(halves, 1 - core))
    left = jnp.where(core == 0, mine, theirs)
    right = jnp.where(core == 0, theirs, mine)
    grad_down = jnp.concatenate([left, right], axis=1)
    return token_grad, gate_grad_t.T, sum_gate[None], sum_up[None], grad_down[None]


def solution(mesh):
    both = P(("dp", "expert"), None)
    weight = P("expert", None, None)
    grad = P("expert", "dp", None)
    return jax.shard_map(
        body,
        mesh=mesh,
        in_specs=(both, both, both, both, weight, weight, weight),
        out_specs=(both, both, grad, grad, grad),
        check_vma=False,
    )
```

```python
import jax
import jax.numpy as jnp
from jax import lax
from jax.experimental import pallas as pl
from jax.experimental.pallas import tpu as pltpu
from jax.sharding import Mesh
from jax.sharding import PartitionSpec as P

F32 = jnp.float32
BF16 = jnp.bfloat16
N_TOK = 128
D = 2048
FF = 768
CAP = 40
N_EXP = 16
ROWS = N_EXP * CAP
N_Z = 8
EXTRA = 128
CHUNK = 160
FULL = 64
MID = 26
H = D // 2
Q = D // 4


def params(mib=FULL):
    return pltpu.CompilerParams(vmem_limit_bytes=mib * 1024 * 1024)


def cost(flops, nbytes):
    return pl.CostEstimate(flops=int(flops), bytes_accessed=int(nbytes), transcendentals=0)


def dot(a, b, ca=1, cb=0):
    return lax.dot_general(a, b, (((ca,), (cb,)), ((), ())), preferred_element_type=F32)


def slot_matrix(ids_t, gates_t=None):
    expert = lax.broadcasted_iota(jnp.int32, (N_EXP, N_TOK), 0)
    member = jnp.zeros((N_EXP, N_TOK), F32)
    weight = jnp.zeros((N_EXP, N_TOK), F32)
    for k in range(4):
        hit = ids_t[k : k + 1, :] == expert
        member = jnp.where(hit, 1.0, member)
        if gates_t is not None:
            weight = jnp.where(hit, gates_t[k : k + 1, :].astype(F32), weight)
    row = lax.broadcasted_iota(jnp.int32, (N_TOK, N_TOK), 0)
    col = lax.broadcasted_iota(jnp.int32, (N_TOK, N_TOK), 1)
    before = jnp.where(row < col, 1.0, 0.0).astype(BF16)
    position = dot(member.astype(BF16), before)
    code = jnp.where(member > 0.0, position, -1.0)
    slot = lax.broadcasted_iota(jnp.int32, (CAP, N_TOK), 0).astype(F32)
    pieces = []
    for e in range(N_EXP):
        value = 1.0 if gates_t is None else weight[e : e + 1, :]
        pieces.append(jnp.where(code[e : e + 1, :] == slot, value, 0.0))
    return jnp.concatenate(pieces, axis=0).astype(BF16)


ANY = pl.BlockSpec(memory_space=pl.ANY)
SMEM = pl.BlockSpec(memory_space=pltpu.SMEM)


def shape(*dims):
    return jax.ShapeDtypeStruct(dims, BF16)


def vmem(*dims, dtype=BF16):
    return pltpu.VMEM(dims, dtype)


def start(sems, at, source, target):
    copy = pltpu.make_async_copy(source, target, sems.at[at])
    copy.start()
    return copy


def wait(copies):
    for copy in copies:
        copy.wait()


def dispatch_kernel(core_ref, ids_hbm, gates_hbm, x_hbm, out_hbm, ids, gates, x, slots, out, sems, out_sems):
    few = [start(sems, 0, ids_hbm, ids)]
    if gates_hbm is None:
        loads = [start(sems, 2, x_hbm, x)]
    else:
        few.append(start(sems, 1, gates_hbm, gates))
        core = core_ref[0]
        own = pl.ds(pl.multiple_of(core * H, H), H)
        other = pl.ds(pl.multiple_of((1 - core) * H, H), H)
        loads = [
            start(sems, 2, x_hbm.at[:, own], x.at[:, pl.ds(0, H)]),
            start(sems, 3, x_hbm.at[:, other], x.at[:, pl.ds(H, H)]),
        ]
    wait(few)
    slots[...] = slot_matrix(ids[...], None if gates_hbm is None else gates[...])
    wait(loads)
    stores = []
    for i in range(ROWS // CHUNK):
        part = slice(i * CHUNK, (i + 1) * CHUNK)
        out[part, :] = dot(slots[part, :], x[...]).astype(BF16)
        stores.append(start(out_sems, i, out.at[part, :], out_hbm.at[part, :]))
    wait(stores)


def plain_kernel(core_ref, ids_hbm, x_hbm, *refs):
    dispatch_kernel(core_ref, ids_hbm, None, x_hbm, *refs)


def dispatch(core, ids_t, gates_t, x):
    plain = gates_t is None
    args = [core, ids_t] + ([] if plain else [gates_t]) + [x]
    return pl.pallas_call(
        plain_kernel if plain else dispatch_kernel,
        in_specs=[SMEM] + [ANY] * (len(args) - 1),
        out_specs=ANY,
        out_shape=shape(ROWS, D),
        scratch_shapes=[
            vmem(4, N_TOK, dtype=jnp.int32),
            vmem(4, N_TOK),
            vmem(N_TOK, D),
            vmem(ROWS, N_TOK),
            vmem(ROWS, D),
            pltpu.SemaphoreType.DMA((4,)),
            pltpu.SemaphoreType.DMA((ROWS // CHUNK,)),
        ],
        compiler_params=params(),
        cost_estimate=cost(2 * ROWS * N_TOK * D, 2 * ROWS * D),
    )(*args)


def down_turn_kernel(core_ref, w_ref, out_ref):
    out_ref[0] = w_ref[0].T


def turn_down(core, w):
    return pl.pallas_call(
        down_turn_kernel,
        grid_spec=pltpu.PrefetchScalarGridSpec(
            num_scalar_prefetch=1,
            grid=(3, 2),
            in_specs=[pl.BlockSpec((1, 256, H), lambda n, i, c: (0, n, i + c[0] - 2 * i * c[0]))],
            out_specs=pl.BlockSpec((1, H, 256), lambda n, i, c: (n, i, 0)),
        ),
        out_shape=shape(3, D, 256),
        compiler_params=params(),
        cost_estimate=cost(0, 4 * D * FF),
    )(core, w)


def up_turn_kernel(g_ref, u_ref, gt_ref, ut_ref):
    gt_ref[0] = g_ref[0].T
    ut_ref[0] = u_ref[0].T


def turn_up(wg, wu):
    weight = pl.BlockSpec((1, Q, FF), lambda n: (0, n, 0))
    out = pl.BlockSpec((1, FF, Q), lambda n: (n, 0, 0))
    turned = jax.ShapeDtypeStruct((4, FF, Q), BF16)
    return pl.pallas_call(
        up_turn_kernel,
        grid=(4,),
        in_specs=[weight, weight],
        out_specs=[out, out],
        out_shape=[turned, turned],
        compiler_params=params(),
        cost_estimate=cost(0, 8 * D * FF),
    )(wg, wu)


def forward_kernel(x_ref, wg_ref, wu_ref, ht_ref, h_ref, f_ref, a_ref):
    x = x_ref[...]
    g = dot(x, wg_ref[0])
    u = dot(x, wu_ref[0])
    s = jax.nn.sigmoid(g)
    a = g * s
    h = (a * u).astype(BF16)
    h_ref[0] = h
    ht_ref[...] = h.T
    a_ref[0] = a.astype(BF16)
    f_ref[0] = (u * s * (1.0 + g * (1.0 - s))).astype(BF16)


def forward(x, wg, wu):
    weight = pl.BlockSpec((1, D, 256), lambda n: (0, 0, n))
    out = pl.BlockSpec((1, ROWS, 256), lambda n: (n, 0, 0))
    return pl.pallas_call(
        forward_kernel,
        grid=(3,),
        in_specs=[pl.BlockSpec((ROWS, D), lambda n: (0, 0)), weight, weight],
        out_specs=[pl.BlockSpec((256, ROWS), lambda n: (n, 0)), out, out, out],
        out_shape=[shape(FF, ROWS)] + [shape(3, ROWS, 256)] * 3,
        compiler_params=params(MID),
        cost_estimate=cost(4 * ROWS * D * FF, 13_000_000),
    )(x, wg, wu)


def split_kernel(core_ref, mine_ref, theirs_ref, own_ref, other_ref):
    own_ref[...] = mine_ref[...].T
    other_ref[...] = theirs_ref[...].T


def split_transposed(core, first):
    out = pl.BlockSpec((128, ROWS), lambda n, c: (n, 0))
    return pl.pallas_call(
        split_kernel,
        grid_spec=pltpu.PrefetchScalarGridSpec(
            num_scalar_prefetch=1,
            grid=(N_Z,),
            in_specs=[
                pl.BlockSpec((ROWS, 128), lambda n, c: (0, 2 * n + c[0])),
                pl.BlockSpec((ROWS, 128), lambda n, c: (0, 2 * n + 1 - c[0])),
            ],
            out_specs=[out, out],
        ),
        out_shape=[shape(H, ROWS), shape(H, ROWS)],
        compiler_params=params(MID),
        cost_estimate=cost(0, 4 * ROWS * D),
    )(core, first, first)


def backward_kernel(me_ref, dy_ref, wd_ref, h_ref, f_ref, a_ref, dg_ref, du_ref, gg_ref, total):
    n = pl.program_id(0)
    b = dot(dy_ref[...], wd_ref[0])
    dg_ref[...] = (b * f_ref[0].astype(F32)).astype(BF16)
    du_ref[...] = (b * a_ref[0].astype(F32)).astype(BF16)
    part = jnp.sum(b * h_ref[0].astype(F32), axis=1, keepdims=True)
    part = jnp.broadcast_to(part, (ROWS, EXTRA))

    @pl.when(n == 0)
    def _():
        total[...] = part

    @pl.when(n > 0)
    def _():
        total[...] += part

    @pl.when(n == pl.num_programs(0) - 1)
    def _():
        value = total[...]
        high = value.astype(BF16).astype(F32)
        col = lax.broadcasted_iota(jnp.int32, (ROWS, EXTRA), 1)
        me = me_ref[0]
        low = jnp.where(col == me + N_EXP, value - high, 0.0)
        gg_ref[...] = jnp.where(col == me, high, low).astype(BF16)


def backward(me, dy, wd_t, h, f, a):
    block = pl.BlockSpec((1, ROWS, 256), lambda n: (n, 0, 0))
    part = pl.BlockSpec((ROWS, 256), lambda n: (0, n))
    return pl.pallas_call(
        backward_kernel,
        grid=(3,),
        in_specs=[
            SMEM,
            pl.BlockSpec((ROWS, D), lambda n: (0, 0)),
            pl.BlockSpec((1, D, 256), lambda n: (n, 0, 0)),
            block,
            block,
            block,
        ],
        out_specs=[part, part, pl.BlockSpec((ROWS, EXTRA), lambda n: (0, 0))],
        out_shape=[shape(ROWS, FF), shape(ROWS, FF), shape(ROWS, EXTRA)],
        scratch_shapes=[vmem(ROWS, EXTRA, dtype=F32)],
        compiler_params=params(),
        cost_estimate=cost(2 * ROWS * D * FF, 11_000_000),
    )(me, dy, wd_t, h, f, a)


def pair_kernel(dg_ref, du_ref, wg_ref, wu_ref, gg_ref, after_ref, out_ref):
    n = pl.program_id(0)
    value = dot(dg_ref[...], wg_ref[0]) + dot(du_ref[...], wu_ref[0])
    out_ref[:, pl.ds(pl.multiple_of(n * Q, Q), Q)] = value.astype(BF16)

    @pl.when(n == 0)
    def _():
        out_ref[:, D:] = gg_ref[...]


def pair_grads(dg, du, wg_t, wu_t, gg, after):
    whole = pl.BlockSpec((ROWS, FF), lambda n: (0, 0))
    weight = pl.BlockSpec((1, FF, Q), lambda n: (n, 0, 0))
    return pl.pallas_call(
        pair_kernel,
        grid=(4,),
        in_specs=[whole, whole, weight, weight, pl.BlockSpec((ROWS, EXTRA), lambda n: (0, 0)), ANY],
        out_specs=pl.BlockSpec((ROWS, D + EXTRA), lambda n: (0, 0)),
        out_shape=shape(ROWS, D + EXTRA),
        compiler_params=params(MID),
        cost_estimate=cost(4 * ROWS * D * FF, 12_000_000),
    )(dg, du, wg_t, wu_t, gg, after)


def outer_kernel(at_ref, bt_ref, a_ref, b_ref, after_ref, out_ref, flag_ref):
    value = dot(at_ref[...], a_ref[...]) + dot(bt_ref[...], b_ref[...])
    out_ref[...] = value.astype(BF16)
    flag_ref[...] = jnp.zeros_like(flag_ref)


def outer_sum(own_t, other_t, own, other, other_at, n, after):
    m, width = own_t.shape[0], 256
    left = pl.BlockSpec((m, ROWS), lambda j: (0, 0))
    return pl.pallas_call(
        outer_kernel,
        grid=(n // width,),
        in_specs=[
            left,
            left,
            pl.BlockSpec((ROWS, width), lambda j: (0, j)),
            pl.BlockSpec((ROWS, width), lambda j: (0, j + other_at // width)),
            ANY,
        ],
        out_specs=[
            pl.BlockSpec((m, width), lambda j: (0, j)),
            pl.BlockSpec((16, 128), lambda j: (0, 0)),
        ],
        out_shape=[shape(m, n), shape(16, 128)],
        compiler_params=params(MID),
        cost_estimate=cost(4 * ROWS * m * n, 2 * (m * n + 2 * ROWS * (m + n))),
    )(own_t, other_t, own, other, after)


def combine_kernel(ids_hbm, gates_hbm, rows_hbm, tok_hbm, gate_hbm, ids, gates, rows, extra, tok, gate, sems, out_sems):
    few = [start(sems, 0, ids_hbm, ids), start(sems, 1, gates_hbm, gates)]
    extra_load = start(sems, 2, rows_hbm.at[:, pl.ds(D, EXTRA)], extra)
    loads = [start(sems, 3 + n, rows_hbm.at[:, pl.ds(n * Q, Q)], rows.at[n]) for n in range(4)]
    wait(few)
    slots = slot_matrix(ids[...])
    stores = []
    for n in range(4):
        loads[n].wait()
        tok[:, n * Q : (n + 1) * Q] = dot(slots, rows[n], 0, 0).astype(BF16)
    stores.append(start(out_sems, 0, tok, tok_hbm))
    extra_load.wait()
    by_expert = dot(extra[...], slots, 0, 0)
    value = by_expert[:N_EXP] + by_expert[N_EXP : 2 * N_EXP]
    expert_at = lax.broadcasted_iota(jnp.int32, (N_EXP, N_TOK), 0)
    choice = lax.broadcasted_iota(jnp.int32, (4, N_TOK), 0)
    grads = jnp.zeros((4, N_TOK), F32)
    for k in range(4):
        mine = jnp.where(ids[k : k + 1, :] == expert_at, value, 0.0)
        grads = jnp.where(choice == k, jnp.sum(mine, axis=0, keepdims=True), grads)
    gate[...] = (grads / gates[...].astype(F32)).astype(BF16)
    stores.append(start(out_sems, 1, gate, gate_hbm))
    wait(stores)


def combine(ids_t, gates_t, rows):
    return pl.pallas_call(
        combine_kernel,
        in_specs=[ANY] * 3,
        out_specs=[ANY] * 2,
        out_shape=[shape(N_TOK, D), shape(4, N_TOK)],
        scratch_shapes=[
            vmem(4, N_TOK, dtype=jnp.int32),
            vmem(4, N_TOK),
            vmem(4, ROWS, Q),
            vmem(ROWS, EXTRA),
            vmem(N_TOK, D),
            vmem(4, N_TOK),
            pltpu.SemaphoreType.DMA((7,)),
            pltpu.SemaphoreType.DMA((2,)),
        ],
        compiler_params=params(16),
        cost_estimate=cost(2 * ROWS * N_TOK * D, 2 * ROWS * D),
    )(ids_t, gates_t, rows)


def exchange_experts(rows):
    width = rows.shape[1]
    moved = lax.all_to_all(
        rows.reshape(N_EXP, CAP, width), "expert", split_axis=0, concat_axis=0, tiled=True
    )
    return moved.reshape(ROWS, width)


def hold_kernel(*refs):
    pass


def hold(a, *after, mib=1):
    place = pl.BlockSpec(memory_space=pl.ANY)
    return pl.pallas_call(
        hold_kernel,
        in_specs=[place] * (1 + len(after)),
        out_specs=place,
        out_shape=jax.ShapeDtypeStruct(a.shape, a.dtype),
        input_output_aliases={0: 0},
        compiler_params=params(mib),
    )(a, *after)


def swap_cores(a):
    return lax.ppermute(a, "core", [(0, 1), (1, 0)])


def pick(a, index):
    return lax.dynamic_index_in_dim(a, index, 0, keepdims=False)


ROUTE = tuple((2 * i, 2 * ((i + 1) % N_Z)) for i in range(N_Z)) + tuple(
    (2 * i + 1, 2 * ((i - 1) % N_Z) + 1) for i in range(N_Z)
)


def ring_step(g, held, z, sign, step, after=None):
    if step == 1:
        held = pick(g, (z - sign) & (N_Z - 1))
    came = lax.ppermute(held, ("z", "core"), ROUTE)
    if after is not None:
        came = hold(came, after)
    block = pick(g, (z - (step + 1) * sign) & (N_Z - 1))
    return (came.astype(F32) + block.astype(F32)).astype(BF16)


def body(tokens, out_grad, gates, expert_ids, w_gate, w_up, w_down):
    z = lax.axis_index("z").astype(jnp.int32)
    core = lax.axis_index("core").astype(jnp.int32)
    sign = 1 - 2 * core
    core_arg = core.reshape(1)
    me = lax.axis_index("expert").astype(jnp.int32).reshape(1)
    ids_t, gates_t = expert_ids.T, gates.T

    down_t = turn_down(core_arg, w_down)
    gate_t, up_t = turn_up(w_gate, w_up)
    x = exchange_experts(dispatch(core_arg, ids_t, None, tokens))
    dy_rows = hold(dispatch(core_arg, ids_t, gates_t, out_grad), x, down_t, up_t, mib=FULL)
    dy = exchange_experts(dy_rows)

    hidden_t, hidden, factor, active = forward(x, w_gate, w_up)
    hidden_other_t = swap_cores(hidden_t)
    x_own, x_theirs = split_transposed(core_arg, x)
    x_other = swap_cores(x_theirs)

    dy = hold(dy, x_other, hidden_other_t, mib=FULL)
    dy_other = swap_cores(dy)
    d_gate, d_up, prob = backward(me, dy, down_t, hidden, factor, active)
    d_gate_other, d_up_other = swap_cores(d_gate), swap_cores(d_up)
    part_down, flag = outer_sum(hidden_t, hidden_other_t, dy, dy_other, H, H, prob)
    part_gate, flag = outer_sum(x_own, x_other, d_gate, d_gate_other, 0, FF, flag)
    part_up, flag = outer_sum(x_own, x_other, d_up, d_up_other, 0, FF, flag)

    sum_down = lax.psum_scatter(part_down, "z", scatter_dimension=0, tiled=True)
    part_gate = part_gate.reshape(N_Z, D // (2 * N_Z), FF)
    part_up = part_up.reshape(N_Z, D // (2 * N_Z), FF)
    sum_gate = ring_step(part_gate, None, z, sign, 1)
    sum_up = ring_step(part_up, None, z, sign, 1)

    pairs = pair_grads(d_gate, d_up, gate_t, up_t, prob, flag)
    pairs = hold(pairs, sum_gate[:16, :128], sum_up[:16, :128], mib=62)
    back_rows = exchange_experts(pairs)
    token_grad, gate_grad_t = combine(ids_t, gates_t, back_rows)
    halves = sum_down.reshape(2, FF // (2 * N_Z), H)
    mine = pick(halves, core)
    theirs = swap_cores(pick(halves, 1 - core))
    left = jnp.where(core == 0, mine, theirs)
    right = jnp.where(core == 0, theirs, mine)
    grad_down = jnp.concatenate([left, right], axis=1)
    for step in range(2, N_Z):
        sum_gate = ring_step(part_gate, sum_gate, z, sign, step, theirs if step == 7 else None)
        sum_up = ring_step(part_up, sum_up, z, sign, step, gate_grad_t if step == 7 else None)

    return token_grad, gate_grad_t.T, sum_gate[None], sum_up[None], grad_down[None]


def solution(mesh):
    mesh = Mesh(mesh.devices.reshape(N_Z, 2, N_EXP), ("z", "core", "expert"))
    both = P(("z", "core", "expert"), None)
    weight = P("expert", None, None)
    grad = P("expert", ("z", "core"), None)
    return jax.shard_map(
        body,
        mesh=mesh,
        in_specs=(both, both, both, both, weight, weight, weight),
        out_specs=(both, both, grad, grad, grad),
        check_vma=False,
    )
```

```python
import jax
import jax.numpy as jnp
from jax import lax
from jax.experimental import pallas as pl
from jax.experimental.pallas import tpu as pltpu
from jax.sharding import PartitionSpec as P

F32 = jnp.float32
BF16 = jnp.bfloat16
N_TOK = 128
D = 2048
FF = 768
CAP = 40
N_EXP = 16
ROWS = N_EXP * CAP
N_Z = 8
EXTRA = 128
CHUNK = 160
FULL = 64
MID = 28
H = D // 2
Q = D // 4


def params(mib=FULL):
    return pltpu.CompilerParams(vmem_limit_bytes=mib * 1024 * 1024)


def cost(flops, nbytes):
    return pl.CostEstimate(flops=int(flops), bytes_accessed=int(nbytes), transcendentals=0)


def dot(a, b, ca=1, cb=0):
    return lax.dot_general(a, b, (((ca,), (cb,)), ((), ())), preferred_element_type=F32)


def slot_matrix(ids_t, gates_t=None):
    expert = lax.broadcasted_iota(jnp.int32, (N_EXP, N_TOK), 0)
    member = jnp.zeros((N_EXP, N_TOK), F32)
    weight = jnp.zeros((N_EXP, N_TOK), F32)
    for k in range(4):
        hit = ids_t[k : k + 1, :] == expert
        member = jnp.where(hit, 1.0, member)
        if gates_t is not None:
            weight = jnp.where(hit, gates_t[k : k + 1, :].astype(F32), weight)
    row = lax.broadcasted_iota(jnp.int32, (N_TOK, N_TOK), 0)
    col = lax.broadcasted_iota(jnp.int32, (N_TOK, N_TOK), 1)
    before = jnp.where(row < col, 1.0, 0.0).astype(BF16)
    position = dot(member.astype(BF16), before)
    code = jnp.where(member > 0.0, position, -1.0)
    slot = lax.broadcasted_iota(jnp.int32, (CAP, N_TOK), 0).astype(F32)
    pieces = []
    for e in range(N_EXP):
        value = 1.0 if gates_t is None else weight[e : e + 1, :]
        pieces.append(jnp.where(code[e : e + 1, :] == slot, value, 0.0))
    return jnp.concatenate(pieces, axis=0).astype(BF16)


ANY = pl.BlockSpec(memory_space=pl.ANY)
SMEM = pl.BlockSpec(memory_space=pltpu.SMEM)


def shape(*dims):
    return jax.ShapeDtypeStruct(dims, BF16)


def vmem(*dims, dtype=BF16):
    return pltpu.VMEM(dims, dtype)


def start(sems, at, source, target):
    copy = pltpu.make_async_copy(source, target, sems.at[at])
    copy.start()
    return copy


def wait(copies):
    for copy in copies:
        copy.wait()


def dispatch_kernel(core_ref, ids_hbm, gates_hbm, x_hbm, out_hbm, ids, gates, x, slots, out, sems, out_sems):
    few = [start(sems, 0, ids_hbm, ids)]
    if gates_hbm is None:
        loads = [start(sems, 2, x_hbm, x)]
    else:
        few.append(start(sems, 1, gates_hbm, gates))
        core = core_ref[0]
        own = pl.ds(pl.multiple_of(core * H, H), H)
        other = pl.ds(pl.multiple_of((1 - core) * H, H), H)
        loads = [
            start(sems, 2, x_hbm.at[:, own], x.at[:, pl.ds(0, H)]),
            start(sems, 3, x_hbm.at[:, other], x.at[:, pl.ds(H, H)]),
        ]
    wait(few)
    slots[...] = slot_matrix(ids[...], None if gates_hbm is None else gates[...])
    wait(loads)
    stores = []
    for i in range(ROWS // CHUNK):
        part = slice(i * CHUNK, (i + 1) * CHUNK)
        out[part, :] = dot(slots[part, :], x[...]).astype(BF16)
        stores.append(start(out_sems, i, out.at[part, :], out_hbm.at[part, :]))
    wait(stores)


def plain_kernel(core_ref, ids_hbm, x_hbm, *refs):
    dispatch_kernel(core_ref, ids_hbm, None, x_hbm, *refs)


def dispatch(core, ids_t, gates_t, x):
    plain = gates_t is None
    args = [core, ids_t] + ([] if plain else [gates_t]) + [x]
    return pl.pallas_call(
        plain_kernel if plain else dispatch_kernel,
        in_specs=[SMEM] + [ANY] * (len(args) - 1),
        out_specs=ANY,
        out_shape=shape(ROWS, D),
        scratch_shapes=[
            vmem(4, N_TOK, dtype=jnp.int32),
            vmem(4, N_TOK),
            vmem(N_TOK, D),
            vmem(ROWS, N_TOK),
            vmem(ROWS, D),
            pltpu.SemaphoreType.DMA((4,)),
            pltpu.SemaphoreType.DMA((ROWS // CHUNK,)),
        ],
        compiler_params=params(),
        cost_estimate=cost(2 * ROWS * N_TOK * D, 2 * ROWS * D),
    )(*args)


def down_turn_kernel(core_ref, w_ref, out_ref):
    out_ref[0] = w_ref[0].T


def turn_down(core, w):
    return pl.pallas_call(
        down_turn_kernel,
        grid_spec=pltpu.PrefetchScalarGridSpec(
            num_scalar_prefetch=1,
            grid=(3, 2),
            in_specs=[pl.BlockSpec((1, 256, H), lambda n, i, c: (0, n, i + c[0] - 2 * i * c[0]))],
            out_specs=pl.BlockSpec((1, H, 256), lambda n, i, c: (n, i, 0)),
        ),
        out_shape=shape(3, D, 256),
        compiler_params=params(),
        cost_estimate=cost(0, 4 * D * FF),
    )(core, w)


def up_turn_kernel(g_ref, u_ref, gt_ref, ut_ref):
    gt_ref[0] = g_ref[0].T
    ut_ref[0] = u_ref[0].T


def turn_up(wg, wu):
    weight = pl.BlockSpec((1, Q, FF), lambda n: (0, n, 0))
    out = pl.BlockSpec((1, FF, Q), lambda n: (n, 0, 0))
    turned = jax.ShapeDtypeStruct((4, FF, Q), BF16)
    return pl.pallas_call(
        up_turn_kernel,
        grid=(4,),
        in_specs=[weight, weight],
        out_specs=[out, out],
        out_shape=[turned, turned],
        compiler_params=params(),
        cost_estimate=cost(0, 8 * D * FF),
    )(wg, wu)


def forward_kernel(x_ref, wg_ref, wu_ref, ht_ref, h_ref, f_ref, a_ref):
    x = x_ref[...]
    g = dot(x, wg_ref[0])
    u = dot(x, wu_ref[0])
    s = jax.nn.sigmoid(g)
    a = g * s
    h = (a * u).astype(BF16)
    h_ref[0] = h
    ht_ref[...] = h.T
    a_ref[0] = a.astype(BF16)
    f_ref[0] = (u * s * (1.0 + g * (1.0 - s))).astype(BF16)


def forward(x, wg, wu):
    weight = pl.BlockSpec((1, D, 256), lambda n: (0, 0, n))
    out = pl.BlockSpec((1, ROWS, 256), lambda n: (n, 0, 0))
    return pl.pallas_call(
        forward_kernel,
        grid=(3,),
        in_specs=[pl.BlockSpec((ROWS, D), lambda n: (0, 0)), weight, weight],
        out_specs=[pl.BlockSpec((256, ROWS), lambda n: (n, 0)), out, out, out],
        out_shape=[shape(FF, ROWS)] + [shape(3, ROWS, 256)] * 3,
        compiler_params=params(MID),
        cost_estimate=cost(4 * ROWS * D * FF, 13_000_000),
    )(x, wg, wu)


def split_kernel(core_ref, mine_ref, theirs_ref, own_ref, other_ref):
    own_ref[...] = mine_ref[...].T
    other_ref[...] = theirs_ref[...].T


def split_transposed(core, first):
    out = pl.BlockSpec((128, ROWS), lambda n, c: (n, 0))
    return pl.pallas_call(
        split_kernel,
        grid_spec=pltpu.PrefetchScalarGridSpec(
            num_scalar_prefetch=1,
            grid=(N_Z,),
            in_specs=[
                pl.BlockSpec((ROWS, 128), lambda n, c: (0, 2 * n + c[0])),
                pl.BlockSpec((ROWS, 128), lambda n, c: (0, 2 * n + 1 - c[0])),
            ],
            out_specs=[out, out],
        ),
        out_shape=[shape(H, ROWS), shape(H, ROWS)],
        compiler_params=params(MID),
        cost_estimate=cost(0, 4 * ROWS * D),
    )(core, first, first)


def backward_kernel(me_ref, dy_ref, wd_ref, h_ref, f_ref, a_ref, dg_ref, du_ref, gg_ref, total):
    n = pl.program_id(0)
    b = dot(dy_ref[...], wd_ref[0])
    dg_ref[...] = (b * f_ref[0].astype(F32)).astype(BF16)
    du_ref[...] = (b * a_ref[0].astype(F32)).astype(BF16)
    part = jnp.sum(b * h_ref[0].astype(F32), axis=1, keepdims=True)
    part = jnp.broadcast_to(part, (ROWS, EXTRA))

    @pl.when(n == 0)
    def _():
        total[...] = part

    @pl.when(n > 0)
    def _():
        total[...] += part

    @pl.when(n == pl.num_programs(0) - 1)
    def _():
        value = total[...]
        high = value.astype(BF16).astype(F32)
        col = lax.broadcasted_iota(jnp.int32, (ROWS, EXTRA), 1)
        me = me_ref[0]
        low = jnp.where(col == me + N_EXP, value - high, 0.0)
        gg_ref[...] = jnp.where(col == me, high, low).astype(BF16)


def backward(me, dy, wd_t, h, f, a):
    block = pl.BlockSpec((1, ROWS, 256), lambda n: (n, 0, 0))
    part = pl.BlockSpec((ROWS, 256), lambda n: (0, n))
    return pl.pallas_call(
        backward_kernel,
        grid=(3,),
        in_specs=[
            SMEM,
            pl.BlockSpec((ROWS, D), lambda n: (0, 0)),
            pl.BlockSpec((1, D, 256), lambda n: (n, 0, 0)),
            block,
            block,
            block,
        ],
        out_specs=[part, part, pl.BlockSpec((ROWS, EXTRA), lambda n: (0, 0))],
        out_shape=[shape(ROWS, FF), shape(ROWS, FF), shape(ROWS, EXTRA)],
        scratch_shapes=[vmem(ROWS, EXTRA, dtype=F32)],
        compiler_params=params(),
        cost_estimate=cost(2 * ROWS * D * FF, 11_000_000),
    )(me, dy, wd_t, h, f, a)


def pair_kernel(dg_ref, du_ref, wg_ref, wu_ref, gg_ref, after_ref, out_ref, flag_ref):
    n = pl.program_id(0)
    value = dot(dg_ref[...], wg_ref[0]) + dot(du_ref[...], wu_ref[0])
    out_ref[:, pl.ds(pl.multiple_of(n * Q, Q), Q)] = value.astype(BF16)
    flag_ref[...] = jnp.zeros_like(flag_ref)

    @pl.when(n == 0)
    def _():
        out_ref[:, D:] = gg_ref[...]


def pair_grads(dg, du, wg_t, wu_t, gg, after):
    whole = pl.BlockSpec((ROWS, FF), lambda n: (0, 0))
    weight = pl.BlockSpec((1, FF, Q), lambda n: (n, 0, 0))
    return pl.pallas_call(
        pair_kernel,
        grid=(4,),
        in_specs=[whole, whole, weight, weight, pl.BlockSpec((ROWS, EXTRA), lambda n: (0, 0)), ANY],
        out_specs=[
            pl.BlockSpec((ROWS, D + EXTRA), lambda n: (0, 0)),
            pl.BlockSpec((16, 128), lambda n: (0, 0)),
        ],
        out_shape=[shape(ROWS, D + EXTRA), shape(16, 128)],
        compiler_params=params(MID),
        cost_estimate=cost(4 * ROWS * D * FF, 12_000_000),
    )(dg, du, wg_t, wu_t, gg, after)


def outer_kernel(at_ref, bt_ref, a_ref, b_ref, after_ref, out_ref, flag_ref):
    value = dot(at_ref[...], a_ref[...]) + dot(bt_ref[...], b_ref[...])
    out_ref[...] = value.astype(BF16)
    flag_ref[...] = jnp.zeros_like(flag_ref)


def outer_sum(own_t, other_t, own, other, other_at, n, after):
    m, width = own_t.shape[0], 256
    left = pl.BlockSpec((m, ROWS), lambda j: (0, 0))
    return pl.pallas_call(
        outer_kernel,
        grid=(n // width,),
        in_specs=[
            left,
            left,
            pl.BlockSpec((ROWS, width), lambda j: (0, j)),
            pl.BlockSpec((ROWS, width), lambda j: (0, j + other_at // width)),
            ANY,
        ],
        out_specs=[
            pl.BlockSpec((m, width), lambda j: (0, j)),
            pl.BlockSpec((16, 128), lambda j: (0, 0)),
        ],
        out_shape=[shape(m, n), shape(16, 128)],
        compiler_params=params(MID),
        cost_estimate=cost(4 * ROWS * m * n, 2 * (m * n + 2 * ROWS * (m + n))),
    )(own_t, other_t, own, other, after)


def combine_kernel(ids_hbm, gates_hbm, rows_hbm, tok_hbm, gate_hbm, ids, gates, rows, extra, tok, gate, sems, out_sems):
    few = [start(sems, 0, ids_hbm, ids), start(sems, 1, gates_hbm, gates)]
    extra_load = start(sems, 2, rows_hbm.at[:, pl.ds(D, EXTRA)], extra)
    loads = [start(sems, 3 + n, rows_hbm.at[:, pl.ds(n * Q, Q)], rows.at[n]) for n in range(4)]
    wait(few)
    slots = slot_matrix(ids[...])
    stores = []
    for n in range(4):
        loads[n].wait()
        tok[:, n * Q : (n + 1) * Q] = dot(slots, rows[n], 0, 0).astype(BF16)
    stores.append(start(out_sems, 0, tok, tok_hbm))
    extra_load.wait()
    by_expert = dot(extra[...], slots, 0, 0)
    value = by_expert[:N_EXP] + by_expert[N_EXP : 2 * N_EXP]
    expert_at = lax.broadcasted_iota(jnp.int32, (N_EXP, N_TOK), 0)
    choice = lax.broadcasted_iota(jnp.int32, (4, N_TOK), 0)
    grads = jnp.zeros((4, N_TOK), F32)
    for k in range(4):
        mine = jnp.where(ids[k : k + 1, :] == expert_at, value, 0.0)
        grads = jnp.where(choice == k, jnp.sum(mine, axis=0, keepdims=True), grads)
    gate[...] = (grads / gates[...].astype(F32)).astype(BF16)
    stores.append(start(out_sems, 1, gate, gate_hbm))
    wait(stores)


def combine(ids_t, gates_t, rows):
    return pl.pallas_call(
        combine_kernel,
        in_specs=[ANY] * 3,
        out_specs=[ANY] * 2,
        out_shape=[shape(N_TOK, D), shape(4, N_TOK)],
        scratch_shapes=[
            vmem(4, N_TOK, dtype=jnp.int32),
            vmem(4, N_TOK),
            vmem(4, ROWS, Q),
            vmem(ROWS, EXTRA),
            vmem(N_TOK, D),
            vmem(4, N_TOK),
            pltpu.SemaphoreType.DMA((7,)),
            pltpu.SemaphoreType.DMA((2,)),
        ],
        compiler_params=params(16),
        cost_estimate=cost(2 * ROWS * N_TOK * D, 2 * ROWS * D),
    )(ids_t, gates_t, rows)


def exchange_experts(rows):
    width = rows.shape[1]
    moved = lax.all_to_all(
        rows.reshape(N_EXP, CAP, width), "expert", split_axis=0, concat_axis=0, tiled=True
    )
    return moved.reshape(ROWS, width)


def hold_kernel(*refs):
    pass


def hold(a, *after, mib=1):
    place = pl.BlockSpec(memory_space=pl.ANY)
    return pl.pallas_call(
        hold_kernel,
        in_specs=[place] * (1 + len(after)),
        out_specs=place,
        out_shape=jax.ShapeDtypeStruct(a.shape, a.dtype),
        input_output_aliases={0: 0},
        compiler_params=params(mib),
    )(a, *after)


def swap_cores(a):
    return lax.ppermute(a, "dp", [(i, i ^ 1) for i in range(2 * N_Z)])


def pick(a, index):
    return lax.dynamic_index_in_dim(a, index, 0, keepdims=False)


ROUTE = tuple((2 * i, 2 * ((i + 1) % N_Z)) for i in range(N_Z)) + tuple(
    (2 * i + 1, 2 * ((i - 1) % N_Z) + 1) for i in range(N_Z)
)


def ring_step(g, held, z, sign, step, after=None):
    if step == 1:
        held = pick(g, (z - sign) & (N_Z - 1))
    came = lax.ppermute(held, "dp", ROUTE)
    if after is not None:
        came = hold(came, after)
    block = pick(g, (z - (step + 1) * sign) & (N_Z - 1))
    return (came.astype(F32) + block.astype(F32)).astype(BF16)


def body(tokens, out_grad, gates, expert_ids, w_gate, w_up, w_down):
    dp = lax.axis_index("dp").astype(jnp.int32)
    z, core = dp >> 1, dp & 1
    sign = 1 - 2 * core
    core_arg = core.reshape(1)
    me = lax.axis_index("expert").astype(jnp.int32).reshape(1)
    ids_t, gates_t = expert_ids.T, gates.T

    down_t = turn_down(core_arg, w_down)
    gate_t, up_t = turn_up(w_gate, w_up)
    x = exchange_experts(dispatch(core_arg, ids_t, None, tokens))
    dy_rows = hold(dispatch(core_arg, ids_t, gates_t, out_grad), x, down_t, up_t, mib=FULL)
    dy = exchange_experts(dy_rows)

    hidden_t, hidden, factor, active = forward(x, w_gate, w_up)
    hidden_other_t = swap_cores(hidden_t)
    x_own, x_theirs = split_transposed(core_arg, x)
    x_other = swap_cores(x_theirs)

    dy = hold(dy, x_other, hidden_other_t, mib=FULL)
    dy_other = swap_cores(dy)
    d_gate, d_up, prob = backward(me, dy, down_t, hidden, factor, active)
    d_gate_other, d_up_other = swap_cores(d_gate), swap_cores(d_up)
    part_down, flag = outer_sum(hidden_t, hidden_other_t, dy, dy_other, H, H, me)
    part_gate, flag = outer_sum(x_own, x_other, d_gate, d_gate_other, 0, FF, flag)
    part_up, flag = outer_sum(x_own, x_other, d_up, d_up_other, 0, FF, flag)
    pairs, flag = pair_grads(d_gate, d_up, gate_t, up_t, prob, flag)

    part_down = part_down.reshape(N_Z, FF // N_Z, H)
    part_gate = part_gate.reshape(N_Z, D // (2 * N_Z), FF)
    part_up = part_up.reshape(N_Z, D // (2 * N_Z), FF)
    sum_down = ring_step(part_down, None, z, sign, 1)
    sum_gate = ring_step(part_gate, None, z, sign, 1)
    sum_up = ring_step(part_up, None, z, sign, 1)
    pairs = hold(pairs, sum_down, sum_gate, sum_up, mib=1)
    back_rows = exchange_experts(pairs)
    token_grad, gate_grad_t = combine(ids_t, gates_t, back_rows)
    sum_down = hold(sum_down, flag)
    for step in range(2, N_Z):
        sum_down = ring_step(part_down, sum_down, z, sign, step)
        sum_gate = ring_step(part_gate, sum_gate, z, sign, step)
        sum_up = ring_step(part_up, sum_up, z, sign, step, gate_grad_t if step == 7 else None)

    halves = sum_down.reshape(2, FF // (2 * N_Z), H)
    mine = pick(halves, core)
    theirs = swap_cores(pick(halves, 1 - core))
    left = jnp.where(core == 0, mine, theirs)
    right = jnp.where(core == 0, theirs, mine)
    grad_down = jnp.concatenate([left, right], axis=1)
    return token_grad, gate_grad_t.T, sum_gate[None], sum_up[None], grad_down[None]


def solution(mesh):
    both = P(("dp", "expert"), None)
    weight = P("expert", None, None)
    grad = P("expert", "dp", None)
    return jax.shard_map(
        body,
        mesh=mesh,
        in_specs=(both, both, both, both, weight, weight, weight),
        out_specs=(both, both, grad, grad, grad),
        check_vma=False,
    )
```

```python
import jax
import jax.numpy as jnp
from jax import lax
from jax.experimental import pallas as pl
from jax.experimental.pallas import tpu as pltpu
from jax.sharding import PartitionSpec as P

F32 = jnp.float32
BF16 = jnp.bfloat16
N_TOK = 128
D = 2048
FF = 768
CAP = 40
N_EXP = 16
ROWS = N_EXP * CAP
N_Z = 8
EXTRA = 128
CHUNK = 160
FULL = 64
MID = 28
H = D // 2
Q = D // 4


def params(mib=FULL):
    return pltpu.CompilerParams(vmem_limit_bytes=mib * 1024 * 1024)


def cost(flops, nbytes):
    return pl.CostEstimate(flops=int(flops), bytes_accessed=int(nbytes), transcendentals=0)


def dot(a, b, ca=1, cb=0):
    return lax.dot_general(a, b, (((ca,), (cb,)), ((), ())), preferred_element_type=F32)


def slot_matrix(ids_t, gates_t=None):
    expert = lax.broadcasted_iota(jnp.int32, (N_EXP, N_TOK), 0)
    member = jnp.zeros((N_EXP, N_TOK), F32)
    weight = jnp.zeros((N_EXP, N_TOK), F32)
    for k in range(4):
        hit = ids_t[k : k + 1, :] == expert
        member = jnp.where(hit, 1.0, member)
        if gates_t is not None:
            weight = jnp.where(hit, gates_t[k : k + 1, :].astype(F32), weight)
    row = lax.broadcasted_iota(jnp.int32, (N_TOK, N_TOK), 0)
    col = lax.broadcasted_iota(jnp.int32, (N_TOK, N_TOK), 1)
    before = jnp.where(row < col, 1.0, 0.0).astype(BF16)
    position = dot(member.astype(BF16), before)
    code = jnp.where(member > 0.0, position, -1.0)
    slot = lax.broadcasted_iota(jnp.int32, (CAP, N_TOK), 0).astype(F32)
    pieces = []
    for e in range(N_EXP):
        value = 1.0 if gates_t is None else weight[e : e + 1, :]
        pieces.append(jnp.where(code[e : e + 1, :] == slot, value, 0.0))
    return jnp.concatenate(pieces, axis=0).astype(BF16)


ANY = pl.BlockSpec(memory_space=pl.ANY)
SMEM = pl.BlockSpec(memory_space=pltpu.SMEM)


def shape(*dims):
    return jax.ShapeDtypeStruct(dims, BF16)


def vmem(*dims, dtype=BF16):
    return pltpu.VMEM(dims, dtype)


def start(sems, at, source, target):
    copy = pltpu.make_async_copy(source, target, sems.at[at])
    copy.start()
    return copy


def wait(copies):
    for copy in copies:
        copy.wait()


def dispatch_kernel(core_ref, ids_hbm, gates_hbm, x_hbm, out_hbm, ids, gates, x, slots, out, sems, out_sems):
    few = [start(sems, 0, ids_hbm, ids)]
    if gates_hbm is None:
        loads = [start(sems, 2, x_hbm, x)]
    else:
        few.append(start(sems, 1, gates_hbm, gates))
        core = core_ref[0]
        own = pl.ds(pl.multiple_of(core * H, H), H)
        other = pl.ds(pl.multiple_of((1 - core) * H, H), H)
        loads = [
            start(sems, 2, x_hbm.at[:, own], x.at[:, pl.ds(0, H)]),
            start(sems, 3, x_hbm.at[:, other], x.at[:, pl.ds(H, H)]),
        ]
    wait(few)
    slots[...] = slot_matrix(ids[...], None if gates_hbm is None else gates[...])
    wait(loads)
    stores = []
    for i in range(ROWS // CHUNK):
        part = slice(i * CHUNK, (i + 1) * CHUNK)
        out[part, :] = dot(slots[part, :], x[...]).astype(BF16)
        stores.append(start(out_sems, i, out.at[part, :], out_hbm.at[part, :]))
    wait(stores)


def plain_kernel(core_ref, ids_hbm, x_hbm, *refs):
    dispatch_kernel(core_ref, ids_hbm, None, x_hbm, *refs)


def dispatch(core, ids_t, gates_t, x):
    plain = gates_t is None
    args = [core, ids_t] + ([] if plain else [gates_t]) + [x]
    return pl.pallas_call(
        plain_kernel if plain else dispatch_kernel,
        in_specs=[SMEM] + [ANY] * (len(args) - 1),
        out_specs=ANY,
        out_shape=shape(ROWS, D),
        scratch_shapes=[
            vmem(4, N_TOK, dtype=jnp.int32),
            vmem(4, N_TOK),
            vmem(N_TOK, D),
            vmem(ROWS, N_TOK),
            vmem(ROWS, D),
            pltpu.SemaphoreType.DMA((4,)),
            pltpu.SemaphoreType.DMA((ROWS // CHUNK,)),
        ],
        compiler_params=params(),
        cost_estimate=cost(2 * ROWS * N_TOK * D, 2 * ROWS * D),
    )(*args)


def down_turn_kernel(core_ref, w_ref, out_ref):
    out_ref[0] = w_ref[0].T


def turn_down(core, w):
    return pl.pallas_call(
        down_turn_kernel,
        grid_spec=pltpu.PrefetchScalarGridSpec(
            num_scalar_prefetch=1,
            grid=(3, 2),
            in_specs=[pl.BlockSpec((1, 256, H), lambda n, i, c: (0, n, i + c[0] - 2 * i * c[0]))],
            out_specs=pl.BlockSpec((1, H, 256), lambda n, i, c: (n, i, 0)),
        ),
        out_shape=shape(3, D, 256),
        compiler_params=params(),
        cost_estimate=cost(0, 4 * D * FF),
    )(core, w)


def up_turn_kernel(g_ref, u_ref, gt_ref, ut_ref):
    gt_ref[0] = g_ref[0].T
    ut_ref[0] = u_ref[0].T


def turn_up(wg, wu):
    weight = pl.BlockSpec((1, Q, FF), lambda n: (0, n, 0))
    out = pl.BlockSpec((1, FF, Q), lambda n: (n, 0, 0))
    turned = jax.ShapeDtypeStruct((4, FF, Q), BF16)
    return pl.pallas_call(
        up_turn_kernel,
        grid=(4,),
        in_specs=[weight, weight],
        out_specs=[out, out],
        out_shape=[turned, turned],
        compiler_params=params(),
        cost_estimate=cost(0, 8 * D * FF),
    )(wg, wu)


def forward_kernel(x_ref, wg_ref, wu_ref, ht_ref, h_ref, f_ref, a_ref):
    x = x_ref[...]
    g = dot(x, wg_ref[0])
    u = dot(x, wu_ref[0])
    s = jax.nn.sigmoid(g)
    a = g * s
    h = (a * u).astype(BF16)
    h_ref[0] = h
    ht_ref[...] = h.T
    a_ref[0] = a.astype(BF16)
    f_ref[0] = (u * s * (1.0 + g * (1.0 - s))).astype(BF16)


def forward(x, wg, wu):
    weight = pl.BlockSpec((1, D, 256), lambda n: (0, 0, n))
    out = pl.BlockSpec((1, ROWS, 256), lambda n: (n, 0, 0))
    return pl.pallas_call(
        forward_kernel,
        grid=(3,),
        in_specs=[pl.BlockSpec((ROWS, D), lambda n: (0, 0)), weight, weight],
        out_specs=[pl.BlockSpec((256, ROWS), lambda n: (n, 0)), out, out, out],
        out_shape=[shape(FF, ROWS)] + [shape(3, ROWS, 256)] * 3,
        compiler_params=params(MID),
        cost_estimate=cost(4 * ROWS * D * FF, 13_000_000),
    )(x, wg, wu)


def split_kernel(core_ref, mine_ref, theirs_ref, own_ref, other_ref):
    own_ref[...] = mine_ref[...].T
    other_ref[...] = theirs_ref[...].T


def split_transposed(core, first):
    out = pl.BlockSpec((128, ROWS), lambda n, c: (n, 0))
    return pl.pallas_call(
        split_kernel,
        grid_spec=pltpu.PrefetchScalarGridSpec(
            num_scalar_prefetch=1,
            grid=(N_Z,),
            in_specs=[
                pl.BlockSpec((ROWS, 128), lambda n, c: (0, 2 * n + c[0])),
                pl.BlockSpec((ROWS, 128), lambda n, c: (0, 2 * n + 1 - c[0])),
            ],
            out_specs=[out, out],
        ),
        out_shape=[shape(H, ROWS), shape(H, ROWS)],
        compiler_params=params(MID),
        cost_estimate=cost(0, 4 * ROWS * D),
    )(core, first, first)


def backward_kernel(me_ref, dy_ref, wd_ref, h_ref, f_ref, a_ref, dg_ref, du_ref, gg_ref, total):
    n = pl.program_id(0)
    b = dot(dy_ref[...], wd_ref[0])
    dg_ref[...] = (b * f_ref[0].astype(F32)).astype(BF16)
    du_ref[...] = (b * a_ref[0].astype(F32)).astype(BF16)
    part = jnp.sum(b * h_ref[0].astype(F32), axis=1, keepdims=True)
    part = jnp.broadcast_to(part, (ROWS, EXTRA))

    @pl.when(n == 0)
    def _():
        total[...] = part

    @pl.when(n > 0)
    def _():
        total[...] += part

    @pl.when(n == pl.num_programs(0) - 1)
    def _():
        value = total[...]
        high = value.astype(BF16).astype(F32)
        col = lax.broadcasted_iota(jnp.int32, (ROWS, EXTRA), 1)
        me = me_ref[0]
        low = jnp.where(col == me + N_EXP, value - high, 0.0)
        gg_ref[...] = jnp.where(col == me, high, low).astype(BF16)


def backward(me, dy, wd_t, h, f, a):
    block = pl.BlockSpec((1, ROWS, 256), lambda n: (n, 0, 0))
    part = pl.BlockSpec((ROWS, 256), lambda n: (0, n))
    return pl.pallas_call(
        backward_kernel,
        grid=(3,),
        in_specs=[
            SMEM,
            pl.BlockSpec((ROWS, D), lambda n: (0, 0)),
            pl.BlockSpec((1, D, 256), lambda n: (n, 0, 0)),
            block,
            block,
            block,
        ],
        out_specs=[part, part, pl.BlockSpec((ROWS, EXTRA), lambda n: (0, 0))],
        out_shape=[shape(ROWS, FF), shape(ROWS, FF), shape(ROWS, EXTRA)],
        scratch_shapes=[vmem(ROWS, EXTRA, dtype=F32)],
        compiler_params=params(),
        cost_estimate=cost(2 * ROWS * D * FF, 11_000_000),
    )(me, dy, wd_t, h, f, a)


def pair_kernel(dg_ref, du_ref, wg_ref, wu_ref, gg_ref, after_ref, out_ref, flag_ref):
    n = pl.program_id(0)
    value = dot(dg_ref[...], wg_ref[0]) + dot(du_ref[...], wu_ref[0])
    out_ref[:, pl.ds(pl.multiple_of(n * Q, Q), Q)] = value.astype(BF16)
    flag_ref[...] = jnp.zeros_like(flag_ref)

    @pl.when(n == 0)
    def _():
        out_ref[:, D:] = gg_ref[...]


def pair_grads(dg, du, wg_t, wu_t, gg, after):
    whole = pl.BlockSpec((ROWS, FF), lambda n: (0, 0))
    weight = pl.BlockSpec((1, FF, Q), lambda n: (n, 0, 0))
    return pl.pallas_call(
        pair_kernel,
        grid=(4,),
        in_specs=[whole, whole, weight, weight, pl.BlockSpec((ROWS, EXTRA), lambda n: (0, 0)), ANY],
        out_specs=[
            pl.BlockSpec((ROWS, D + EXTRA), lambda n: (0, 0)),
            pl.BlockSpec((16, 128), lambda n: (0, 0)),
        ],
        out_shape=[shape(ROWS, D + EXTRA), shape(16, 128)],
        compiler_params=params(MID),
        cost_estimate=cost(4 * ROWS * D * FF, 12_000_000),
    )(dg, du, wg_t, wu_t, gg, after)


def outer_kernel(at_ref, bt_ref, a_ref, b_ref, after_ref, out_ref, flag_ref):
    value = dot(at_ref[...], a_ref[...]) + dot(bt_ref[...], b_ref[...])
    out_ref[...] = value.astype(BF16)
    flag_ref[...] = jnp.zeros_like(flag_ref)


def outer_sum(own_t, other_t, own, other, other_at, n, after):
    m, width = own_t.shape[0], 256
    left = pl.BlockSpec((m, ROWS), lambda j: (0, 0))
    return pl.pallas_call(
        outer_kernel,
        grid=(n // width,),
        in_specs=[
            left,
            left,
            pl.BlockSpec((ROWS, width), lambda j: (0, j)),
            pl.BlockSpec((ROWS, width), lambda j: (0, j + other_at // width)),
            ANY,
        ],
        out_specs=[
            pl.BlockSpec((m, width), lambda j: (0, j)),
            pl.BlockSpec((16, 128), lambda j: (0, 0)),
        ],
        out_shape=[shape(m, n), shape(16, 128)],
        compiler_params=params(MID),
        cost_estimate=cost(4 * ROWS * m * n, 2 * (m * n + 2 * ROWS * (m + n))),
    )(own_t, other_t, own, other, after)


def combine_kernel(ids_hbm, gates_hbm, rows_hbm, tok_hbm, gate_hbm, flag_ref, ids, gates, rows, extra, tok, gate, sems, out_sems):
    flag_ref[...] = jnp.zeros_like(flag_ref)
    few = [start(sems, 0, ids_hbm, ids), start(sems, 1, gates_hbm, gates)]
    extra_load = start(sems, 2, rows_hbm.at[:, pl.ds(D, EXTRA)], extra)
    loads = [start(sems, 3 + n, rows_hbm.at[:, pl.ds(n * Q, Q)], rows.at[n]) for n in range(4)]
    wait(few)
    slots = slot_matrix(ids[...])
    stores = []
    for n in range(4):
        loads[n].wait()
        tok[:, n * Q : (n + 1) * Q] = dot(slots, rows[n], 0, 0).astype(BF16)
    stores.append(start(out_sems, 0, tok, tok_hbm))
    extra_load.wait()
    by_expert = dot(extra[...], slots, 0, 0)
    value = by_expert[:N_EXP] + by_expert[N_EXP : 2 * N_EXP]
    expert_at = lax.broadcasted_iota(jnp.int32, (N_EXP, N_TOK), 0)
    choice = lax.broadcasted_iota(jnp.int32, (4, N_TOK), 0)
    grads = jnp.zeros((4, N_TOK), F32)
    for k in range(4):
        mine = jnp.where(ids[k : k + 1, :] == expert_at, value, 0.0)
        grads = jnp.where(choice == k, jnp.sum(mine, axis=0, keepdims=True), grads)
    gate[...] = (grads / gates[...].astype(F32)).astype(BF16)
    stores.append(start(out_sems, 1, gate, gate_hbm))
    wait(stores)


def combine(ids_t, gates_t, rows):
    return pl.pallas_call(
        combine_kernel,
        in_specs=[ANY] * 3,
        out_specs=[ANY, ANY, pl.BlockSpec(memory_space=pltpu.VMEM)],
        out_shape=[shape(N_TOK, D), shape(4, N_TOK), shape(16, 128)],
        scratch_shapes=[
            vmem(4, N_TOK, dtype=jnp.int32),
            vmem(4, N_TOK),
            vmem(4, ROWS, Q),
            vmem(ROWS, EXTRA),
            vmem(N_TOK, D),
            vmem(4, N_TOK),
            pltpu.SemaphoreType.DMA((7,)),
            pltpu.SemaphoreType.DMA((2,)),
        ],
        compiler_params=params(16),
        cost_estimate=cost(2 * ROWS * N_TOK * D, 2 * ROWS * D),
    )(ids_t, gates_t, rows)


def exchange_experts(rows):
    width = rows.shape[1]
    moved = lax.all_to_all(
        rows.reshape(N_EXP, CAP, width), "expert", split_axis=0, concat_axis=0, tiled=True
    )
    return moved.reshape(ROWS, width)


def hold_kernel(*refs):
    pass


def hold(a, *after, mib=1):
    place = pl.BlockSpec(memory_space=pl.ANY)
    return pl.pallas_call(
        hold_kernel,
        in_specs=[place] * (1 + len(after)),
        out_specs=place,
        out_shape=jax.ShapeDtypeStruct(a.shape, a.dtype),
        input_output_aliases={0: 0},
        compiler_params=params(mib),
    )(a, *after)


def swap_cores(a):
    return lax.ppermute(a, "dp", [(i, i ^ 1) for i in range(2 * N_Z)])


def pick(a, index):
    return lax.dynamic_index_in_dim(a, index, 0, keepdims=False)


ROUTE = tuple((2 * i, 2 * ((i + 1) % N_Z)) for i in range(N_Z)) + tuple(
    (2 * i + 1, 2 * ((i - 1) % N_Z) + 1) for i in range(N_Z)
)


def ring_step(g, held, z, sign, step, after=None):
    if step == 1:
        held = pick(g, (z - sign) & (N_Z - 1))
    came = lax.ppermute(held, "dp", ROUTE)
    if after is not None:
        came = hold(came, after)
    block = pick(g, (z - (step + 1) * sign) & (N_Z - 1))
    return (came.astype(F32) + block.astype(F32)).astype(BF16)


def body(tokens, out_grad, gates, expert_ids, w_gate, w_up, w_down):
    dp = lax.axis_index("dp").astype(jnp.int32)
    z, core = dp >> 1, dp & 1
    sign = 1 - 2 * core
    core_arg = core.reshape(1)
    me = lax.axis_index("expert").astype(jnp.int32).reshape(1)
    ids_t, gates_t = expert_ids.T, gates.T

    down_t = turn_down(core_arg, w_down)
    gate_t, up_t = turn_up(w_gate, w_up)
    x = exchange_experts(dispatch(core_arg, ids_t, None, tokens))
    dy_rows = hold(dispatch(core_arg, ids_t, gates_t, out_grad), x, down_t, up_t, mib=FULL)
    dy = exchange_experts(dy_rows)

    hidden_t, hidden, factor, active = forward(x, w_gate, w_up)
    hidden_other_t = swap_cores(hidden_t)
    x_own, x_theirs = split_transposed(core_arg, x)
    x_other = swap_cores(x_theirs)

    dy = hold(dy, x_other, hidden_other_t, mib=FULL)
    dy_other = swap_cores(dy)
    d_gate, d_up, prob = backward(me, dy, down_t, hidden, factor, active)
    d_gate_other, d_up_other = swap_cores(d_gate), swap_cores(d_up)
    part_down, flag = outer_sum(hidden_t, hidden_other_t, dy, dy_other, H, H, me)
    part_gate, flag = outer_sum(x_own, x_other, d_gate, d_gate_other, 0, FF, flag)
    part_up, flag = outer_sum(x_own, x_other, d_up, d_up_other, 0, FF, flag)
    pairs, _ = pair_grads(d_gate, d_up, gate_t, up_t, prob, flag)

    part_down = part_down.reshape(N_Z, FF // N_Z, H)
    part_gate = part_gate.reshape(N_Z, D // (2 * N_Z), FF)
    part_up = part_up.reshape(N_Z, D // (2 * N_Z), FF)
    sum_down = ring_step(part_down, None, z, sign, 1)
    sum_gate = ring_step(part_gate, None, z, sign, 1)
    sum_up = ring_step(part_up, None, z, sign, 1)
    pairs = hold(pairs, sum_down, sum_gate, sum_up, mib=1)
    back_rows = exchange_experts(pairs)
    token_grad, gate_grad_t, flag = combine(ids_t, gates_t, back_rows)
    for step in range(2, N_Z):
        sum_down = ring_step(part_down, sum_down, z, sign, step)
        last = flag if step == 7 else None
        sum_gate = ring_step(part_gate, sum_gate, z, sign, step, last)
        sum_up = ring_step(part_up, sum_up, z, sign, step, last)

    halves = sum_down.reshape(2, FF // (2 * N_Z), H)
    mine = pick(halves, core)
    theirs = swap_cores(pick(halves, 1 - core))
    left = jnp.where(core == 0, mine, theirs)
    right = jnp.where(core == 0, theirs, mine)
    grad_down = jnp.concatenate([left, right], axis=1)
    return token_grad, gate_grad_t.T, sum_gate[None], sum_up[None], grad_down[None]


def solution(mesh):
    both = P(("dp", "expert"), None)
    weight = P("expert", None, None)
    grad = P("expert", "dp", None)
    return jax.shard_map(
        body,
        mesh=mesh,
        in_specs=(both, both, both, both, weight, weight, weight),
        out_specs=(both, both, grad, grad, grad),
        check_vma=False,
    )
```

```python
import jax
import jax.numpy as jnp
from jax import lax
from jax.experimental import pallas as pl
from jax.experimental.pallas import tpu as pltpu
from jax.sharding import PartitionSpec as P

F32 = jnp.float32
BF16 = jnp.bfloat16
N_TOK = 128
D = 2048
FF = 768
CAP = 40
N_EXP = 16
ROWS = N_EXP * CAP
N_Z = 8
EXTRA = 128
CHUNK = 160
FULL = 64
MID = 28
H = D // 2
Q = D // 4


def params(mib=FULL):
    return pltpu.CompilerParams(vmem_limit_bytes=mib * 1024 * 1024)


def cost(flops, nbytes):
    return pl.CostEstimate(flops=int(flops), bytes_accessed=int(nbytes), transcendentals=0)


def dot(a, b, ca=1, cb=0):
    return lax.dot_general(a, b, (((ca,), (cb,)), ((), ())), preferred_element_type=F32)


def slot_matrix(ids_t, gates_t=None):
    expert = lax.broadcasted_iota(jnp.int32, (N_EXP, N_TOK), 0)
    member = jnp.zeros((N_EXP, N_TOK), F32)
    weight = jnp.zeros((N_EXP, N_TOK), F32)
    for k in range(4):
        hit = ids_t[k : k + 1, :] == expert
        member = jnp.where(hit, 1.0, member)
        if gates_t is not None:
            weight = jnp.where(hit, gates_t[k : k + 1, :].astype(F32), weight)
    row = lax.broadcasted_iota(jnp.int32, (N_TOK, N_TOK), 0)
    col = lax.broadcasted_iota(jnp.int32, (N_TOK, N_TOK), 1)
    before = jnp.where(row < col, 1.0, 0.0).astype(BF16)
    position = dot(member.astype(BF16), before)
    code = jnp.where(member > 0.0, position, -1.0)
    slot = lax.broadcasted_iota(jnp.int32, (CAP, N_TOK), 0).astype(F32)
    pieces = []
    for e in range(N_EXP):
        value = 1.0 if gates_t is None else weight[e : e + 1, :]
        pieces.append(jnp.where(code[e : e + 1, :] == slot, value, 0.0))
    return jnp.concatenate(pieces, axis=0).astype(BF16)


ANY = pl.BlockSpec(memory_space=pl.ANY)
SMEM = pl.BlockSpec(memory_space=pltpu.SMEM)


def shape(*dims):
    return jax.ShapeDtypeStruct(dims, BF16)


def vmem(*dims, dtype=BF16):
    return pltpu.VMEM(dims, dtype)


def start(sems, at, source, target):
    copy = pltpu.make_async_copy(source, target, sems.at[at])
    copy.start()
    return copy


def wait(copies):
    for copy in copies:
        copy.wait()


def dispatch_kernel(core_ref, ids_hbm, gates_hbm, x_hbm, out_hbm, ids, gates, x, slots, out, sems, out_sems):
    few = [start(sems, 0, ids_hbm, ids)]
    if gates_hbm is None:
        loads = [start(sems, 2, x_hbm, x)]
    else:
        few.append(start(sems, 1, gates_hbm, gates))
        core = core_ref[0]
        own = pl.ds(pl.multiple_of(core * H, H), H)
        other = pl.ds(pl.multiple_of((1 - core) * H, H), H)
        loads = [
            start(sems, 2, x_hbm.at[:, own], x.at[:, pl.ds(0, H)]),
            start(sems, 3, x_hbm.at[:, other], x.at[:, pl.ds(H, H)]),
        ]
    wait(few)
    slots[...] = slot_matrix(ids[...], None if gates_hbm is None else gates[...])
    wait(loads)
    stores = []
    for i in range(ROWS // CHUNK):
        part = slice(i * CHUNK, (i + 1) * CHUNK)
        out[part, :] = dot(slots[part, :], x[...]).astype(BF16)
        stores.append(start(out_sems, i, out.at[part, :], out_hbm.at[part, :]))
    wait(stores)


def plain_kernel(core_ref, ids_hbm, x_hbm, *refs):
    dispatch_kernel(core_ref, ids_hbm, None, x_hbm, *refs)


def dispatch(core, ids_t, gates_t, x):
    plain = gates_t is None
    args = [core, ids_t] + ([] if plain else [gates_t]) + [x]
    return pl.pallas_call(
        plain_kernel if plain else dispatch_kernel,
        in_specs=[SMEM] + [ANY] * (len(args) - 1),
        out_specs=ANY,
        out_shape=shape(ROWS, D),
        scratch_shapes=[
            vmem(4, N_TOK, dtype=jnp.int32),
            vmem(4, N_TOK),
            vmem(N_TOK, D),
            vmem(ROWS, N_TOK),
            vmem(ROWS, D),
            pltpu.SemaphoreType.DMA((4,)),
            pltpu.SemaphoreType.DMA((ROWS // CHUNK,)),
        ],
        compiler_params=params(),
        cost_estimate=cost(2 * ROWS * N_TOK * D, 2 * ROWS * D),
    )(*args)


def down_turn_kernel(core_ref, w_ref, out_ref):
    out_ref[0] = w_ref[0].T


def turn_down(core, w):
    return pl.pallas_call(
        down_turn_kernel,
        grid_spec=pltpu.PrefetchScalarGridSpec(
            num_scalar_prefetch=1,
            grid=(3, 2),
            in_specs=[pl.BlockSpec((1, 256, H), lambda n, i, c: (0, n, i + c[0] - 2 * i * c[0]))],
            out_specs=pl.BlockSpec((1, H, 256), lambda n, i, c: (n, i, 0)),
        ),
        out_shape=shape(3, D, 256),
        compiler_params=params(),
        cost_estimate=cost(0, 4 * D * FF),
    )(core, w)


def up_turn_kernel(g_ref, u_ref, gt_ref, ut_ref):
    gt_ref[0] = g_ref[0].T
    ut_ref[0] = u_ref[0].T


def turn_up(wg, wu):
    weight = pl.BlockSpec((1, Q, FF), lambda n: (0, n, 0))
    out = pl.BlockSpec((1, FF, Q), lambda n: (n, 0, 0))
    turned = jax.ShapeDtypeStruct((4, FF, Q), BF16)
    return pl.pallas_call(
        up_turn_kernel,
        grid=(4,),
        in_specs=[weight, weight],
        out_specs=[out, out],
        out_shape=[turned, turned],
        compiler_params=params(),
        cost_estimate=cost(0, 8 * D * FF),
    )(wg, wu)


def forward_kernel(x_ref, wg_ref, wu_ref, ht_ref, h_ref, f_ref, a_ref):
    x = x_ref[...]
    g = dot(x, wg_ref[0])
    u = dot(x, wu_ref[0])
    s = jax.nn.sigmoid(g)
    a = g * s
    h = (a * u).astype(BF16)
    h_ref[0] = h
    ht_ref[...] = h.T
    a_ref[0] = a.astype(BF16)
    f_ref[0] = (u * s * (1.0 + g * (1.0 - s))).astype(BF16)


def forward(x, wg, wu):
    weight = pl.BlockSpec((1, D, 256), lambda n: (0, 0, n))
    out = pl.BlockSpec((1, ROWS, 256), lambda n: (n, 0, 0))
    return pl.pallas_call(
        forward_kernel,
        grid=(3,),
        in_specs=[pl.BlockSpec((ROWS, D), lambda n: (0, 0)), weight, weight],
        out_specs=[pl.BlockSpec((256, ROWS), lambda n: (n, 0)), out, out, out],
        out_shape=[shape(FF, ROWS)] + [shape(3, ROWS, 256)] * 3,
        compiler_params=params(MID),
        cost_estimate=cost(4 * ROWS * D * FF, 13_000_000),
    )(x, wg, wu)


def split_kernel(core_ref, mine_ref, theirs_ref, own_ref, other_ref):
    own_ref[...] = mine_ref[...].T
    other_ref[...] = theirs_ref[...].T


def split_transposed(core, first):
    out = pl.BlockSpec((128, ROWS), lambda n, c: (n, 0))
    return pl.pallas_call(
        split_kernel,
        grid_spec=pltpu.PrefetchScalarGridSpec(
            num_scalar_prefetch=1,
            grid=(N_Z,),
            in_specs=[
                pl.BlockSpec((ROWS, 128), lambda n, c: (0, 2 * n + c[0])),
                pl.BlockSpec((ROWS, 128), lambda n, c: (0, 2 * n + 1 - c[0])),
            ],
            out_specs=[out, out],
        ),
        out_shape=[shape(H, ROWS), shape(H, ROWS)],
        compiler_params=params(MID),
        cost_estimate=cost(0, 4 * ROWS * D),
    )(core, first, first)


def backward_kernel(me_ref, dy_ref, wd_ref, h_ref, f_ref, a_ref, dg_ref, du_ref, gg_ref, total):
    n = pl.program_id(0)
    b = dot(dy_ref[...], wd_ref[0])
    dg_ref[...] = (b * f_ref[0].astype(F32)).astype(BF16)
    du_ref[...] = (b * a_ref[0].astype(F32)).astype(BF16)
    part = jnp.sum(b * h_ref[0].astype(F32), axis=1, keepdims=True)
    part = jnp.broadcast_to(part, (ROWS, EXTRA))

    @pl.when(n == 0)
    def _():
        total[...] = part

    @pl.when(n > 0)
    def _():
        total[...] += part

    @pl.when(n == pl.num_programs(0) - 1)
    def _():
        value = total[...]
        high = value.astype(BF16).astype(F32)
        col = lax.broadcasted_iota(jnp.int32, (ROWS, EXTRA), 1)
        me = me_ref[0]
        low = jnp.where(col == me + N_EXP, value - high, 0.0)
        gg_ref[...] = jnp.where(col == me, high, low).astype(BF16)


def backward(me, dy, wd_t, h, f, a):
    block = pl.BlockSpec((1, ROWS, 256), lambda n: (n, 0, 0))
    part = pl.BlockSpec((ROWS, 256), lambda n: (0, n))
    return pl.pallas_call(
        backward_kernel,
        grid=(3,),
        in_specs=[
            SMEM,
            pl.BlockSpec((ROWS, D), lambda n: (0, 0)),
            pl.BlockSpec((1, D, 256), lambda n: (n, 0, 0)),
            block,
            block,
            block,
        ],
        out_specs=[part, part, pl.BlockSpec((ROWS, EXTRA), lambda n: (0, 0))],
        out_shape=[shape(ROWS, FF), shape(ROWS, FF), shape(ROWS, EXTRA)],
        scratch_shapes=[vmem(ROWS, EXTRA, dtype=F32)],
        compiler_params=params(),
        cost_estimate=cost(2 * ROWS * D * FF, 11_000_000),
    )(me, dy, wd_t, h, f, a)


def pair_kernel(dg_ref, du_ref, wg_ref, wu_ref, gg_ref, *refs):
    out_ref, flag_ref = refs[-2:]
    n = pl.program_id(0)
    value = dot(dg_ref[...], wg_ref[0]) + dot(du_ref[...], wu_ref[0])
    out_ref[:, pl.ds(pl.multiple_of(n * Q, Q), Q)] = value.astype(BF16)
    flag_ref[...] = jnp.zeros_like(flag_ref)

    @pl.when(n == 0)
    def _():
        out_ref[:, D:] = gg_ref[...]


def pair_grads(dg, du, wg_t, wu_t, gg, *after):
    whole = pl.BlockSpec((ROWS, FF), lambda n: (0, 0))
    weight = pl.BlockSpec((1, FF, Q), lambda n: (n, 0, 0))
    return pl.pallas_call(
        pair_kernel,
        grid=(4,),
        in_specs=[whole, whole, weight, weight, pl.BlockSpec((ROWS, EXTRA), lambda n: (0, 0))]
        + [ANY] * len(after),
        out_specs=[
            pl.BlockSpec((ROWS, D + EXTRA), lambda n: (0, 0)),
            pl.BlockSpec((16, 128), lambda n: (0, 0)),
        ],
        out_shape=[shape(ROWS, D + EXTRA), shape(16, 128)],
        compiler_params=params(MID),
        cost_estimate=cost(4 * ROWS * D * FF, 12_000_000),
    )(dg, du, wg_t, wu_t, gg, *after)


def outer_kernel(at_ref, bt_ref, a_ref, b_ref, *refs):
    out_ref, flag_ref = refs[-2:]
    value = dot(at_ref[...], a_ref[...]) + dot(bt_ref[...], b_ref[...])
    out_ref[...] = value.astype(BF16)
    flag_ref[...] = jnp.zeros_like(flag_ref)


def outer_sum(own_t, other_t, own, other, other_at, n, *after):
    m, width = own_t.shape[0], 256
    left = pl.BlockSpec((m, ROWS), lambda j: (0, 0))
    return pl.pallas_call(
        outer_kernel,
        grid=(n // width,),
        in_specs=[
            left,
            left,
            pl.BlockSpec((ROWS, width), lambda j: (0, j)),
            pl.BlockSpec((ROWS, width), lambda j: (0, j + other_at // width)),
        ]
        + [ANY] * len(after),
        out_specs=[
            pl.BlockSpec((m, width), lambda j: (0, j)),
            pl.BlockSpec((16, 128), lambda j: (0, 0)),
        ],
        out_shape=[shape(m, n), shape(16, 128)],
        compiler_params=params(MID),
        cost_estimate=cost(4 * ROWS * m * n, 2 * (m * n + 2 * ROWS * (m + n))),
    )(own_t, other_t, own, other, *after)


def combine_kernel(ids_hbm, gates_hbm, rows_hbm, tok_hbm, gate_hbm, flag_ref, ids, gates, rows, extra, tok, gate, sems, out_sems):
    flag_ref[...] = jnp.zeros_like(flag_ref)
    few = [start(sems, 0, ids_hbm, ids), start(sems, 1, gates_hbm, gates)]
    extra_load = start(sems, 2, rows_hbm.at[:, pl.ds(D, EXTRA)], extra)
    loads = [start(sems, 3 + n, rows_hbm.at[:, pl.ds(n * Q, Q)], rows.at[n]) for n in range(4)]
    wait(few)
    slots = slot_matrix(ids[...])
    stores = []
    for n in range(4):
        loads[n].wait()
        tok[:, n * Q : (n + 1) * Q] = dot(slots, rows[n], 0, 0).astype(BF16)
    stores.append(start(out_sems, 0, tok, tok_hbm))
    extra_load.wait()
    by_expert = dot(extra[...], slots, 0, 0)
    value = by_expert[:N_EXP] + by_expert[N_EXP : 2 * N_EXP]
    expert_at = lax.broadcasted_iota(jnp.int32, (N_EXP, N_TOK), 0)
    choice = lax.broadcasted_iota(jnp.int32, (4, N_TOK), 0)
    grads = jnp.zeros((4, N_TOK), F32)
    for k in range(4):
        mine = jnp.where(ids[k : k + 1, :] == expert_at, value, 0.0)
        grads = jnp.where(choice == k, jnp.sum(mine, axis=0, keepdims=True), grads)
    gate[...] = (grads / gates[...].astype(F32)).astype(BF16)
    stores.append(start(out_sems, 1, gate, gate_hbm))
    wait(stores)


def combine(ids_t, gates_t, rows):
    return pl.pallas_call(
        combine_kernel,
        in_specs=[ANY] * 3,
        out_specs=[ANY, ANY, pl.BlockSpec(memory_space=pltpu.VMEM)],
        out_shape=[shape(N_TOK, D), shape(4, N_TOK), shape(16, 128)],
        scratch_shapes=[
            vmem(4, N_TOK, dtype=jnp.int32),
            vmem(4, N_TOK),
            vmem(4, ROWS, Q),
            vmem(ROWS, EXTRA),
            vmem(N_TOK, D),
            vmem(4, N_TOK),
            pltpu.SemaphoreType.DMA((7,)),
            pltpu.SemaphoreType.DMA((2,)),
        ],
        compiler_params=params(16),
        cost_estimate=cost(2 * ROWS * N_TOK * D, 2 * ROWS * D),
    )(ids_t, gates_t, rows)


def exchange_experts(rows):
    width = rows.shape[1]
    moved = lax.all_to_all(
        rows.reshape(N_EXP, CAP, width), "expert", split_axis=0, concat_axis=0, tiled=True
    )
    return moved.reshape(ROWS, width)


def hold_kernel(*refs):
    pass


def hold(a, *after, mib=1):
    place = pl.BlockSpec(memory_space=pl.ANY)
    return pl.pallas_call(
        hold_kernel,
        in_specs=[place] * (1 + len(after)),
        out_specs=place,
        out_shape=jax.ShapeDtypeStruct(a.shape, a.dtype),
        input_output_aliases={0: 0},
        compiler_params=params(mib),
    )(a, *after)


def swap_cores(a):
    return lax.ppermute(a, "dp", [(i, i ^ 1) for i in range(2 * N_Z)])


def pick(a, index):
    return lax.dynamic_index_in_dim(a, index, 0, keepdims=False)


ROUTE = tuple((2 * i, 2 * ((i + 1) % N_Z)) for i in range(N_Z)) + tuple(
    (2 * i + 1, 2 * ((i - 1) % N_Z) + 1) for i in range(N_Z)
)


def ring_step(g, held, z, sign, step, after=None):
    if step == 1:
        held = pick(g, (z - sign) & (N_Z - 1))
    came = lax.ppermute(held, "dp", ROUTE)
    if after is not None:
        came = hold(came, after)
    block = pick(g, (z - (step + 1) * sign) & (N_Z - 1))
    return (came.astype(F32) + block.astype(F32)).astype(BF16)


def body(tokens, out_grad, gates, expert_ids, w_gate, w_up, w_down):
    dp = lax.axis_index("dp").astype(jnp.int32)
    z, core = dp >> 1, dp & 1
    sign = 1 - 2 * core
    core_arg = core.reshape(1)
    me = lax.axis_index("expert").astype(jnp.int32).reshape(1)
    ids_t, gates_t = expert_ids.T, gates.T

    down_t = turn_down(core_arg, w_down)
    gate_t, up_t = turn_up(w_gate, w_up)
    x = exchange_experts(dispatch(core_arg, ids_t, None, tokens))
    dy_rows = hold(dispatch(core_arg, ids_t, gates_t, out_grad), x, down_t, up_t, mib=FULL)
    dy = exchange_experts(dy_rows)

    hidden_t, hidden, factor, active = forward(x, w_gate, w_up)
    hidden_other_t = swap_cores(hidden_t)
    x_own, x_theirs = split_transposed(core_arg, x)
    x_other = swap_cores(x_theirs)

    dy = hold(dy, x_other, hidden_other_t, mib=FULL)
    dy_other = swap_cores(dy)
    d_gate, d_up, prob = backward(me, dy, down_t, hidden, factor, active)
    d_gate_other, d_up_other = swap_cores(d_gate), swap_cores(d_up)
    part_down, flag = outer_sum(hidden_t, hidden_other_t, dy, dy_other, H, H, me)
    part_down = part_down.reshape(N_Z, FF // N_Z, H)
    sum_down = ring_step(part_down, None, z, sign, 1)
    part_gate, flag = outer_sum(x_own, x_other, d_gate, d_gate_other, 0, FF, flag)
    part_gate = part_gate.reshape(N_Z, D // (2 * N_Z), FF)
    sum_gate = ring_step(part_gate, None, z, sign, 1)
    part_up, flag = outer_sum(x_own, x_other, d_up, d_up_other, 0, FF, flag, sum_down)
    part_up = part_up.reshape(N_Z, D // (2 * N_Z), FF)
    sum_up = ring_step(part_up, None, z, sign, 1)
    sum_down = ring_step(part_down, sum_down, z, sign, 2)
    pairs, _ = pair_grads(d_gate, d_up, gate_t, up_t, prob, flag, sum_gate)
    sum_down = ring_step(part_down, sum_down, z, sign, 3)
    sum_gate = ring_step(part_gate, sum_gate, z, sign, 2)
    pairs = hold(pairs, sum_up, mib=1)
    back_rows = exchange_experts(pairs)
    token_grad, gate_grad_t, flag = combine(ids_t, gates_t, back_rows)
    for step in range(4, N_Z):
        sum_down = ring_step(part_down, sum_down, z, sign, step)
    for step in range(3, N_Z):
        sum_gate = ring_step(part_gate, sum_gate, z, sign, step)
    for step in range(2, N_Z):
        sum_up = ring_step(part_up, sum_up, z, sign, step, flag if step == 7 else None)

    halves = sum_down.reshape(2, FF // (2 * N_Z), H)
    mine = pick(halves, core)
    theirs = swap_cores(pick(halves, 1 - core))
    left = jnp.where(core == 0, mine, theirs)
    right = jnp.where(core == 0, theirs, mine)
    grad_down = jnp.concatenate([left, right], axis=1)
    return token_grad, gate_grad_t.T, sum_gate[None], sum_up[None], grad_down[None]


def solution(mesh):
    both = P(("dp", "expert"), None)
    weight = P("expert", None, None)
    grad = P("expert", "dp", None)
    return jax.shard_map(
        body,
        mesh=mesh,
        in_specs=(both, both, both, both, weight, weight, weight),
        out_specs=(both, both, grad, grad, grad),
        check_vma=False,
    )
```

```python
import jax
import jax.numpy as jnp
from jax import lax
from jax.experimental import pallas as pl
from jax.experimental.pallas import tpu as pltpu
from jax.sharding import PartitionSpec as P

F32 = jnp.float32
BF16 = jnp.bfloat16
N_TOK = 128
D = 2048
FF = 768
CAP = 40
N_EXP = 16
ROWS = N_EXP * CAP
N_Z = 8
EXTRA = 128
CHUNK = 160
FULL = 64
MID = 28
H = D // 2
Q = D // 4


def params(mib=FULL):
    return pltpu.CompilerParams(vmem_limit_bytes=mib * 1024 * 1024)


def cost(flops, nbytes):
    return pl.CostEstimate(flops=int(flops), bytes_accessed=int(nbytes), transcendentals=0)


def dot(a, b, ca=1, cb=0):
    return lax.dot_general(a, b, (((ca,), (cb,)), ((), ())), preferred_element_type=F32)


def slot_matrix(ids_t, gates_t=None):
    expert = lax.broadcasted_iota(jnp.int32, (N_EXP, N_TOK), 0)
    member = jnp.zeros((N_EXP, N_TOK), F32)
    weight = jnp.zeros((N_EXP, N_TOK), F32)
    for k in range(4):
        hit = ids_t[k : k + 1, :] == expert
        member = jnp.where(hit, 1.0, member)
        if gates_t is not None:
            weight = jnp.where(hit, gates_t[k : k + 1, :].astype(F32), weight)
    row = lax.broadcasted_iota(jnp.int32, (N_TOK, N_TOK), 0)
    col = lax.broadcasted_iota(jnp.int32, (N_TOK, N_TOK), 1)
    before = jnp.where(row < col, 1.0, 0.0).astype(BF16)
    position = dot(member.astype(BF16), before)
    code = jnp.where(member > 0.0, position, -1.0)
    slot = lax.broadcasted_iota(jnp.int32, (CAP, N_TOK), 0).astype(F32)
    pieces = []
    for e in range(N_EXP):
        value = 1.0 if gates_t is None else weight[e : e + 1, :]
        pieces.append(jnp.where(code[e : e + 1, :] == slot, value, 0.0))
    return jnp.concatenate(pieces, axis=0).astype(BF16)


ANY = pl.BlockSpec(memory_space=pl.ANY)
SMEM = pl.BlockSpec(memory_space=pltpu.SMEM)


def shape(*dims):
    return jax.ShapeDtypeStruct(dims, BF16)


def vmem(*dims, dtype=BF16):
    return pltpu.VMEM(dims, dtype)


def start(sems, at, source, target):
    copy = pltpu.make_async_copy(source, target, sems.at[at])
    copy.start()
    return copy


def wait(copies):
    for copy in copies:
        copy.wait()


def dispatch_kernel(core_ref, ids_hbm, gates_hbm, x_hbm, out_hbm, ids, gates, x, slots, out, sems, out_sems):
    few = [start(sems, 0, ids_hbm, ids)]
    if gates_hbm is None:
        loads = [start(sems, 2, x_hbm, x)]
    else:
        few.append(start(sems, 1, gates_hbm, gates))
        core = core_ref[0]
        own = pl.ds(pl.multiple_of(core * H, H), H)
        other = pl.ds(pl.multiple_of((1 - core) * H, H), H)
        loads = [
            start(sems, 2, x_hbm.at[:, own], x.at[:, pl.ds(0, H)]),
            start(sems, 3, x_hbm.at[:, other], x.at[:, pl.ds(H, H)]),
        ]
    wait(few)
    slots[...] = slot_matrix(ids[...], None if gates_hbm is None else gates[...])
    wait(loads)
    stores = []
    for i in range(ROWS // CHUNK):
        part = slice(i * CHUNK, (i + 1) * CHUNK)
        out[part, :] = dot(slots[part, :], x[...]).astype(BF16)
        stores.append(start(out_sems, i, out.at[part, :], out_hbm.at[part, :]))
    wait(stores)


def plain_kernel(core_ref, ids_hbm, x_hbm, *refs):
    dispatch_kernel(core_ref, ids_hbm, None, x_hbm, *refs)


def dispatch(core, ids_t, gates_t, x):
    plain = gates_t is None
    args = [core, ids_t] + ([] if plain else [gates_t]) + [x]
    return pl.pallas_call(
        plain_kernel if plain else dispatch_kernel,
        in_specs=[SMEM] + [ANY] * (len(args) - 1),
        out_specs=ANY,
        out_shape=shape(ROWS, D),
        scratch_shapes=[
            vmem(4, N_TOK, dtype=jnp.int32),
            vmem(4, N_TOK),
            vmem(N_TOK, D),
            vmem(ROWS, N_TOK),
            vmem(ROWS, D),
            pltpu.SemaphoreType.DMA((4,)),
            pltpu.SemaphoreType.DMA((ROWS // CHUNK,)),
        ],
        compiler_params=params(),
        cost_estimate=cost(2 * ROWS * N_TOK * D, 2 * ROWS * D),
    )(*args)


def down_turn_kernel(core_ref, w_ref, out_ref):
    out_ref[0] = w_ref[0].T


def turn_down(core, w):
    return pl.pallas_call(
        down_turn_kernel,
        grid_spec=pltpu.PrefetchScalarGridSpec(
            num_scalar_prefetch=1,
            grid=(3, 2),
            in_specs=[pl.BlockSpec((1, 256, H), lambda n, i, c: (0, n, i + c[0] - 2 * i * c[0]))],
            out_specs=pl.BlockSpec((1, H, 256), lambda n, i, c: (n, i, 0)),
        ),
        out_shape=shape(3, D, 256),
        compiler_params=params(),
        cost_estimate=cost(0, 4 * D * FF),
    )(core, w)


def up_turn_kernel(g_ref, u_ref, gt_ref, ut_ref):
    gt_ref[0] = g_ref[0].T
    ut_ref[0] = u_ref[0].T


def turn_up(wg, wu):
    weight = pl.BlockSpec((1, Q, FF), lambda n: (0, n, 0))
    out = pl.BlockSpec((1, FF, Q), lambda n: (n, 0, 0))
    turned = jax.ShapeDtypeStruct((4, FF, Q), BF16)
    return pl.pallas_call(
        up_turn_kernel,
        grid=(4,),
        in_specs=[weight, weight],
        out_specs=[out, out],
        out_shape=[turned, turned],
        compiler_params=params(),
        cost_estimate=cost(0, 8 * D * FF),
    )(wg, wu)


def forward_kernel(x_ref, wg_ref, wu_ref, ht_ref, h_ref, f_ref, a_ref):
    x = x_ref[...]
    g = dot(x, wg_ref[0])
    u = dot(x, wu_ref[0])
    s = jax.nn.sigmoid(g)
    a = g * s
    h = (a * u).astype(BF16)
    h_ref[0] = h
    ht_ref[...] = h.T
    a_ref[0] = a.astype(BF16)
    f_ref[0] = (u * s * (1.0 + g * (1.0 - s))).astype(BF16)


def forward(x, wg, wu):
    weight = pl.BlockSpec((1, D, 256), lambda n: (0, 0, n))
    out = pl.BlockSpec((1, ROWS, 256), lambda n: (n, 0, 0))
    return pl.pallas_call(
        forward_kernel,
        grid=(3,),
        in_specs=[pl.BlockSpec((ROWS, D), lambda n: (0, 0)), weight, weight],
        out_specs=[pl.BlockSpec((256, ROWS), lambda n: (n, 0)), out, out, out],
        out_shape=[shape(FF, ROWS)] + [shape(3, ROWS, 256)] * 3,
        compiler_params=params(MID),
        cost_estimate=cost(4 * ROWS * D * FF, 13_000_000),
    )(x, wg, wu)


def split_kernel(core_ref, mine_ref, theirs_ref, own_ref, other_ref):
    own_ref[...] = mine_ref[...].T
    other_ref[...] = theirs_ref[...].T


def split_transposed(core, first):
    out = pl.BlockSpec((128, ROWS), lambda n, c: (n, 0))
    return pl.pallas_call(
        split_kernel,
        grid_spec=pltpu.PrefetchScalarGridSpec(
            num_scalar_prefetch=1,
            grid=(N_Z,),
            in_specs=[
                pl.BlockSpec((ROWS, 128), lambda n, c: (0, 2 * n + c[0])),
                pl.BlockSpec((ROWS, 128), lambda n, c: (0, 2 * n + 1 - c[0])),
            ],
            out_specs=[out, out],
        ),
        out_shape=[shape(H, ROWS), shape(H, ROWS)],
        compiler_params=params(MID),
        cost_estimate=cost(0, 4 * ROWS * D),
    )(core, first, first)


def backward_kernel(me_ref, dy_ref, wd_ref, h_ref, f_ref, a_ref, dg_ref, du_ref, gg_ref, total):
    n = pl.program_id(0)
    b = dot(dy_ref[...], wd_ref[0])
    dg_ref[...] = (b * f_ref[0].astype(F32)).astype(BF16)
    du_ref[...] = (b * a_ref[0].astype(F32)).astype(BF16)
    part = jnp.sum(b * h_ref[0].astype(F32), axis=1, keepdims=True)
    part = jnp.broadcast_to(part, (ROWS, EXTRA))

    @pl.when(n == 0)
    def _():
        total[...] = part

    @pl.when(n > 0)
    def _():
        total[...] += part

    @pl.when(n == pl.num_programs(0) - 1)
    def _():
        value = total[...]
        high = value.astype(BF16).astype(F32)
        col = lax.broadcasted_iota(jnp.int32, (ROWS, EXTRA), 1)
        me = me_ref[0]
        low = jnp.where(col == me + N_EXP, value - high, 0.0)
        gg_ref[...] = jnp.where(col == me, high, low).astype(BF16)


def backward(me, dy, wd_t, h, f, a):
    block = pl.BlockSpec((1, ROWS, 256), lambda n: (n, 0, 0))
    part = pl.BlockSpec((ROWS, 256), lambda n: (0, n))
    return pl.pallas_call(
        backward_kernel,
        grid=(3,),
        in_specs=[
            SMEM,
            pl.BlockSpec((ROWS, D), lambda n: (0, 0)),
            pl.BlockSpec((1, D, 256), lambda n: (n, 0, 0)),
            block,
            block,
            block,
        ],
        out_specs=[part, part, pl.BlockSpec((ROWS, EXTRA), lambda n: (0, 0))],
        out_shape=[shape(ROWS, FF), shape(ROWS, FF), shape(ROWS, EXTRA)],
        scratch_shapes=[vmem(ROWS, EXTRA, dtype=F32)],
        compiler_params=params(),
        cost_estimate=cost(2 * ROWS * D * FF, 11_000_000),
    )(me, dy, wd_t, h, f, a)


def pair_kernel(dg_ref, du_ref, wg_ref, wu_ref, gg_ref, *refs):
    out_ref, flag_ref = refs[-2:]
    n = pl.program_id(0)
    value = dot(dg_ref[...], wg_ref[0]) + dot(du_ref[...], wu_ref[0])
    out_ref[:, pl.ds(pl.multiple_of(n * Q, Q), Q)] = value.astype(BF16)
    flag_ref[...] = jnp.zeros_like(flag_ref)

    @pl.when(n == 0)
    def _():
        out_ref[:, D:] = gg_ref[...]


def pair_grads(dg, du, wg_t, wu_t, gg, *after):
    whole = pl.BlockSpec((ROWS, FF), lambda n: (0, 0))
    weight = pl.BlockSpec((1, FF, Q), lambda n: (n, 0, 0))
    return pl.pallas_call(
        pair_kernel,
        grid=(4,),
        in_specs=[whole, whole, weight, weight, pl.BlockSpec((ROWS, EXTRA), lambda n: (0, 0))]
        + [ANY] * len(after),
        out_specs=[
            pl.BlockSpec((ROWS, D + EXTRA), lambda n: (0, 0)),
            pl.BlockSpec((16, 128), lambda n: (0, 0)),
        ],
        out_shape=[shape(ROWS, D + EXTRA), shape(16, 128)],
        compiler_params=params(MID),
        cost_estimate=cost(4 * ROWS * D * FF, 12_000_000),
    )(dg, du, wg_t, wu_t, gg, *after)


def outer_kernel(at_ref, bt_ref, a_ref, b_ref, *refs):
    out_ref, flag_ref = refs[-2:]
    value = dot(at_ref[...], a_ref[...]) + dot(bt_ref[...], b_ref[...])
    out_ref[...] = value.astype(BF16)
    flag_ref[...] = jnp.zeros_like(flag_ref)


def outer_sum(own_t, other_t, own, other, other_at, n, *after):
    m, width = own_t.shape[0], 256
    left = pl.BlockSpec((m, ROWS), lambda j: (0, 0))
    return pl.pallas_call(
        outer_kernel,
        grid=(n // width,),
        in_specs=[
            left,
            left,
            pl.BlockSpec((ROWS, width), lambda j: (0, j)),
            pl.BlockSpec((ROWS, width), lambda j: (0, j + other_at // width)),
        ]
        + [ANY] * len(after),
        out_specs=[
            pl.BlockSpec((m, width), lambda j: (0, j)),
            pl.BlockSpec((16, 128), lambda j: (0, 0)),
        ],
        out_shape=[shape(m, n), shape(16, 128)],
        compiler_params=params(MID),
        cost_estimate=cost(4 * ROWS * m * n, 2 * (m * n + 2 * ROWS * (m + n))),
    )(own_t, other_t, own, other, *after)


def combine_kernel(ids_hbm, gates_hbm, rows_hbm, tok_hbm, gate_hbm, flag_ref, ids, gates, rows, extra, tok, gate, sems, out_sems):
    flag_ref[...] = jnp.zeros_like(flag_ref)
    few = [start(sems, 0, ids_hbm, ids), start(sems, 1, gates_hbm, gates)]
    extra_load = start(sems, 2, rows_hbm.at[:, pl.ds(D, EXTRA)], extra)
    loads = [start(sems, 3 + n, rows_hbm.at[:, pl.ds(n * Q, Q)], rows.at[n]) for n in range(4)]
    wait(few)
    slots = slot_matrix(ids[...])
    stores = []
    for n in range(4):
        loads[n].wait()
        tok[:, n * Q : (n + 1) * Q] = dot(slots, rows[n], 0, 0).astype(BF16)
    stores.append(start(out_sems, 0, tok, tok_hbm))
    extra_load.wait()
    by_expert = dot(extra[...], slots, 0, 0)
    value = by_expert[:N_EXP] + by_expert[N_EXP : 2 * N_EXP]
    expert_at = lax.broadcasted_iota(jnp.int32, (N_EXP, N_TOK), 0)
    choice = lax.broadcasted_iota(jnp.int32, (4, N_TOK), 0)
    grads = jnp.zeros((4, N_TOK), F32)
    for k in range(4):
        mine = jnp.where(ids[k : k + 1, :] == expert_at, value, 0.0)
        grads = jnp.where(choice == k, jnp.sum(mine, axis=0, keepdims=True), grads)
    gate[...] = (grads / gates[...].astype(F32)).astype(BF16)
    stores.append(start(out_sems, 1, gate, gate_hbm))
    wait(stores)


def combine(ids_t, gates_t, rows):
    return pl.pallas_call(
        combine_kernel,
        in_specs=[ANY] * 3,
        out_specs=[ANY, ANY, pl.BlockSpec(memory_space=pltpu.VMEM)],
        out_shape=[shape(N_TOK, D), shape(4, N_TOK), shape(16, 128)],
        scratch_shapes=[
            vmem(4, N_TOK, dtype=jnp.int32),
            vmem(4, N_TOK),
            vmem(4, ROWS, Q),
            vmem(ROWS, EXTRA),
            vmem(N_TOK, D),
            vmem(4, N_TOK),
            pltpu.SemaphoreType.DMA((7,)),
            pltpu.SemaphoreType.DMA((2,)),
        ],
        compiler_params=params(16),
        cost_estimate=cost(2 * ROWS * N_TOK * D, 2 * ROWS * D),
    )(ids_t, gates_t, rows)


def exchange_experts(rows):
    width = rows.shape[1]
    moved = lax.all_to_all(
        rows.reshape(N_EXP, CAP, width), "expert", split_axis=0, concat_axis=0, tiled=True
    )
    return moved.reshape(ROWS, width)


def hold_kernel(*refs):
    pass


def hold(a, *after, mib=1):
    place = pl.BlockSpec(memory_space=pl.ANY)
    return pl.pallas_call(
        hold_kernel,
        in_specs=[place] * (1 + len(after)),
        out_specs=place,
        out_shape=jax.ShapeDtypeStruct(a.shape, a.dtype),
        input_output_aliases={0: 0},
        compiler_params=params(mib),
    )(a, *after)


def swap_cores(a):
    return lax.ppermute(a, "dp", [(i, i ^ 1) for i in range(2 * N_Z)])


def pick(a, index):
    return lax.dynamic_index_in_dim(a, index, 0, keepdims=False)


ROUTE = tuple((2 * i, 2 * ((i + 1) % N_Z)) for i in range(N_Z)) + tuple(
    (2 * i + 1, 2 * ((i - 1) % N_Z) + 1) for i in range(N_Z)
)


def ring_step(g, held, z, sign, step, after=None):
    if step == 1:
        held = pick(g, (z - sign) & (N_Z - 1))
    came = lax.ppermute(held, "dp", ROUTE)
    if after is not None:
        came = hold(came, after)
    block = pick(g, (z - (step + 1) * sign) & (N_Z - 1))
    return (came.astype(F32) + block.astype(F32)).astype(BF16)


def body(tokens, out_grad, gates, expert_ids, w_gate, w_up, w_down):
    dp = lax.axis_index("dp").astype(jnp.int32)
    z, core = dp >> 1, dp & 1
    sign = 1 - 2 * core
    core_arg = core.reshape(1)
    me = lax.axis_index("expert").astype(jnp.int32).reshape(1)
    ids_t, gates_t = expert_ids.T, gates.T

    down_t = turn_down(core_arg, w_down)
    gate_t, up_t = turn_up(w_gate, w_up)
    x = exchange_experts(dispatch(core_arg, ids_t, None, tokens))
    dy_rows = hold(dispatch(core_arg, ids_t, gates_t, out_grad), x, down_t, up_t, mib=FULL)
    dy = exchange_experts(dy_rows)

    hidden_t, hidden, factor, active = forward(x, w_gate, w_up)
    hidden_other_t = swap_cores(hidden_t)
    x_own, x_theirs = split_transposed(core_arg, x)
    x_other = swap_cores(x_theirs)

    dy = hold(dy, x_other, hidden_other_t, mib=FULL)
    dy_other = swap_cores(dy)
    d_gate, d_up, prob = backward(me, dy, down_t, hidden, factor, active)
    d_gate_other, d_up_other = swap_cores(d_gate), swap_cores(d_up)
    part_down, flag = outer_sum(hidden_t, hidden_other_t, dy, dy_other, H, H, me)
    part_down = part_down.reshape(N_Z, FF // N_Z, H)
    sum_down = ring_step(part_down, None, z, sign, 1)
    part_gate, flag = outer_sum(x_own, x_other, d_gate, d_gate_other, 0, FF, flag)
    part_gate = part_gate.reshape(N_Z, D // (2 * N_Z), FF)
    sum_gate = ring_step(part_gate, None, z, sign, 1)
    part_up, flag = outer_sum(x_own, x_other, d_up, d_up_other, 0, FF, flag, sum_down)
    part_up = part_up.reshape(N_Z, D // (2 * N_Z), FF)
    sum_up = ring_step(part_up, None, z, sign, 1)
    sum_down = ring_step(part_down, sum_down, z, sign, 2)
    pairs, _ = pair_grads(d_gate, d_up, gate_t, up_t, prob, flag, sum_gate)
    sum_down = ring_step(part_down, sum_down, z, sign, 3)
    sum_gate = ring_step(part_gate, sum_gate, z, sign, 2)
    pairs = hold(pairs, sum_up, mib=1)
    back_rows = exchange_experts(pairs)
    token_grad, gate_grad_t, flag = combine(ids_t, gates_t, back_rows)
    for step in range(4, N_Z):
        sum_down = ring_step(part_down, sum_down, z, sign, step, flag if step == 7 else None)
    for step in range(3, N_Z):
        sum_gate = ring_step(part_gate, sum_gate, z, sign, step)
    for step in range(2, N_Z):
        sum_up = ring_step(part_up, sum_up, z, sign, step)

    halves = sum_down.reshape(2, FF // (2 * N_Z), H)
    mine = pick(halves, core)
    theirs = swap_cores(pick(halves, 1 - core))
    left = jnp.where(core == 0, mine, theirs)
    right = jnp.where(core == 0, theirs, mine)
    grad_down = jnp.concatenate([left, right], axis=1)
    return token_grad, gate_grad_t.T, sum_gate[None], sum_up[None], grad_down[None]


def solution(mesh):
    both = P(("dp", "expert"), None)
    weight = P("expert", None, None)
    grad = P("expert", "dp", None)
    return jax.shard_map(
        body,
        mesh=mesh,
        in_specs=(both, both, both, both, weight, weight, weight),
        out_specs=(both, both, grad, grad, grad),
        check_vma=False,
    )
```

```python
import jax
import jax.numpy as jnp
from jax import lax
from jax.experimental import pallas as pl
from jax.experimental.pallas import tpu as pltpu
from jax.sharding import PartitionSpec as P

F32 = jnp.float32
BF16 = jnp.bfloat16
N_TOK = 128
D = 2048
FF = 768
CAP = 40
N_EXP = 16
ROWS = N_EXP * CAP
N_Z = 8
EXTRA = 128
CHUNK = 160
FULL = 64
MID = 28
H = D // 2
Q = D // 4


def params(mib=FULL):
    return pltpu.CompilerParams(vmem_limit_bytes=mib * 1024 * 1024)


def cost(flops, nbytes):
    return pl.CostEstimate(flops=int(flops), bytes_accessed=int(nbytes), transcendentals=0)


def dot(a, b, ca=1, cb=0):
    return lax.dot_general(a, b, (((ca,), (cb,)), ((), ())), preferred_element_type=F32)


def slot_matrix(ids_t, gates_t=None):
    expert = lax.broadcasted_iota(jnp.int32, (N_EXP, N_TOK), 0)
    member = jnp.zeros((N_EXP, N_TOK), F32)
    weight = jnp.zeros((N_EXP, N_TOK), F32)
    for k in range(4):
        hit = ids_t[k : k + 1, :] == expert
        member = jnp.where(hit, 1.0, member)
        if gates_t is not None:
            weight = jnp.where(hit, gates_t[k : k + 1, :].astype(F32), weight)
    row = lax.broadcasted_iota(jnp.int32, (N_TOK, N_TOK), 0)
    col = lax.broadcasted_iota(jnp.int32, (N_TOK, N_TOK), 1)
    before = jnp.where(row < col, 1.0, 0.0).astype(BF16)
    position = dot(member.astype(BF16), before)
    code = jnp.where(member > 0.0, position, -1.0)
    slot = lax.broadcasted_iota(jnp.int32, (CAP, N_TOK), 0).astype(F32)
    pieces = []
    for e in range(N_EXP):
        value = 1.0 if gates_t is None else weight[e : e + 1, :]
        pieces.append(jnp.where(code[e : e + 1, :] == slot, value, 0.0))
    return jnp.concatenate(pieces, axis=0).astype(BF16)


ANY = pl.BlockSpec(memory_space=pl.ANY)
SMEM = pl.BlockSpec(memory_space=pltpu.SMEM)


def shape(*dims):
    return jax.ShapeDtypeStruct(dims, BF16)


def vmem(*dims, dtype=BF16):
    return pltpu.VMEM(dims, dtype)


def start(sems, at, source, target):
    copy = pltpu.make_async_copy(source, target, sems.at[at])
    copy.start()
    return copy


def wait(copies):
    for copy in copies:
        copy.wait()


def dispatch_kernel(core_ref, ids_hbm, gates_hbm, x_hbm, out_hbm, ids, gates, x, slots, out, sems, out_sems):
    few = [start(sems, 0, ids_hbm, ids)]
    if gates_hbm is None:
        loads = [start(sems, 2, x_hbm, x)]
    else:
        few.append(start(sems, 1, gates_hbm, gates))
        core = core_ref[0]
        own = pl.ds(pl.multiple_of(core * H, H), H)
        other = pl.ds(pl.multiple_of((1 - core) * H, H), H)
        loads = [
            start(sems, 2, x_hbm.at[:, own], x.at[:, pl.ds(0, H)]),
            start(sems, 3, x_hbm.at[:, other], x.at[:, pl.ds(H, H)]),
        ]
    wait(few)
    slots[...] = slot_matrix(ids[...], None if gates_hbm is None else gates[...])
    wait(loads)
    stores = []
    for i in range(ROWS // CHUNK):
        part = slice(i * CHUNK, (i + 1) * CHUNK)
        out[part, :] = dot(slots[part, :], x[...]).astype(BF16)
        stores.append(start(out_sems, i, out.at[part, :], out_hbm.at[part, :]))
    wait(stores)


def plain_kernel(core_ref, ids_hbm, x_hbm, *refs):
    dispatch_kernel(core_ref, ids_hbm, None, x_hbm, *refs)


def dispatch(core, ids_t, gates_t, x):
    plain = gates_t is None
    args = [core, ids_t] + ([] if plain else [gates_t]) + [x]
    return pl.pallas_call(
        plain_kernel if plain else dispatch_kernel,
        in_specs=[SMEM] + [ANY] * (len(args) - 1),
        out_specs=ANY,
        out_shape=shape(ROWS, D),
        scratch_shapes=[
            vmem(4, N_TOK, dtype=jnp.int32),
            vmem(4, N_TOK),
            vmem(N_TOK, D),
            vmem(ROWS, N_TOK),
            vmem(ROWS, D),
            pltpu.SemaphoreType.DMA((4,)),
            pltpu.SemaphoreType.DMA((ROWS // CHUNK,)),
        ],
        compiler_params=params(),
        cost_estimate=cost(2 * ROWS * N_TOK * D, 2 * ROWS * D),
    )(*args)


def down_turn_kernel(core_ref, w_ref, out_ref):
    out_ref[0] = w_ref[0].T


def turn_down(core, w):
    return pl.pallas_call(
        down_turn_kernel,
        grid_spec=pltpu.PrefetchScalarGridSpec(
            num_scalar_prefetch=1,
            grid=(3, 2),
            in_specs=[pl.BlockSpec((1, 256, H), lambda n, i, c: (0, n, i + c[0] - 2 * i * c[0]))],
            out_specs=pl.BlockSpec((1, H, 256), lambda n, i, c: (n, i, 0)),
        ),
        out_shape=shape(3, D, 256),
        compiler_params=params(),
        cost_estimate=cost(0, 4 * D * FF),
    )(core, w)


def up_turn_kernel(g_ref, u_ref, gt_ref, ut_ref):
    gt_ref[0] = g_ref[0].T
    ut_ref[0] = u_ref[0].T


def turn_up(wg, wu):
    weight = pl.BlockSpec((1, Q, FF), lambda n: (0, n, 0))
    out = pl.BlockSpec((1, FF, Q), lambda n: (n, 0, 0))
    turned = jax.ShapeDtypeStruct((4, FF, Q), BF16)
    return pl.pallas_call(
        up_turn_kernel,
        grid=(4,),
        in_specs=[weight, weight],
        out_specs=[out, out],
        out_shape=[turned, turned],
        compiler_params=params(),
        cost_estimate=cost(0, 8 * D * FF),
    )(wg, wu)


def forward_kernel(x_ref, wg_ref, wu_ref, ht_ref, h_ref, f_ref, a_ref):
    x = x_ref[...]
    g = dot(x, wg_ref[0])
    u = dot(x, wu_ref[0])
    s = jax.nn.sigmoid(g)
    a = g * s
    h = (a * u).astype(BF16)
    h_ref[0] = h
    ht_ref[...] = h.T
    a_ref[0] = a.astype(BF16)
    f_ref[0] = (u * s * (1.0 + g * (1.0 - s))).astype(BF16)


def forward(x, wg, wu):
    weight = pl.BlockSpec((1, D, 256), lambda n: (0, 0, n))
    out = pl.BlockSpec((1, ROWS, 256), lambda n: (n, 0, 0))
    return pl.pallas_call(
        forward_kernel,
        grid=(3,),
        in_specs=[pl.BlockSpec((ROWS, D), lambda n: (0, 0)), weight, weight],
        out_specs=[pl.BlockSpec((256, ROWS), lambda n: (n, 0)), out, out, out],
        out_shape=[shape(FF, ROWS)] + [shape(3, ROWS, 256)] * 3,
        compiler_params=params(MID),
        cost_estimate=cost(4 * ROWS * D * FF, 13_000_000),
    )(x, wg, wu)


def split_kernel(core_ref, mine_ref, theirs_ref, own_ref, other_ref):
    own_ref[...] = mine_ref[...].T
    other_ref[...] = theirs_ref[...].T


def split_transposed(core, first):
    out = pl.BlockSpec((128, ROWS), lambda n, c: (n, 0))
    return pl.pallas_call(
        split_kernel,
        grid_spec=pltpu.PrefetchScalarGridSpec(
            num_scalar_prefetch=1,
            grid=(N_Z,),
            in_specs=[
                pl.BlockSpec((ROWS, 128), lambda n, c: (0, 2 * n + c[0])),
                pl.BlockSpec((ROWS, 128), lambda n, c: (0, 2 * n + 1 - c[0])),
            ],
            out_specs=[out, out],
        ),
        out_shape=[shape(H, ROWS), shape(H, ROWS)],
        compiler_params=params(MID),
        cost_estimate=cost(0, 4 * ROWS * D),
    )(core, first, first)


def backward_kernel(me_ref, dy_ref, wd_ref, h_ref, f_ref, a_ref, dg_ref, du_ref, gg_ref, total):
    n = pl.program_id(0)
    b = dot(dy_ref[...], wd_ref[0])
    dg_ref[...] = (b * f_ref[0].astype(F32)).astype(BF16)
    du_ref[...] = (b * a_ref[0].astype(F32)).astype(BF16)
    part = jnp.sum(b * h_ref[0].astype(F32), axis=1, keepdims=True)
    part = jnp.broadcast_to(part, (ROWS, EXTRA))

    @pl.when(n == 0)
    def _():
        total[...] = part

    @pl.when(n > 0)
    def _():
        total[...] += part

    @pl.when(n == pl.num_programs(0) - 1)
    def _():
        value = total[...]
        high = value.astype(BF16).astype(F32)
        col = lax.broadcasted_iota(jnp.int32, (ROWS, EXTRA), 1)
        me = me_ref[0]
        low = jnp.where(col == me + N_EXP, value - high, 0.0)
        gg_ref[...] = jnp.where(col == me, high, low).astype(BF16)


def backward(me, dy, wd_t, h, f, a):
    block = pl.BlockSpec((1, ROWS, 256), lambda n: (n, 0, 0))
    part = pl.BlockSpec((ROWS, 256), lambda n: (0, n))
    return pl.pallas_call(
        backward_kernel,
        grid=(3,),
        in_specs=[
            SMEM,
            pl.BlockSpec((ROWS, D), lambda n: (0, 0)),
            pl.BlockSpec((1, D, 256), lambda n: (n, 0, 0)),
            block,
            block,
            block,
        ],
        out_specs=[part, part, pl.BlockSpec((ROWS, EXTRA), lambda n: (0, 0))],
        out_shape=[shape(ROWS, FF), shape(ROWS, FF), shape(ROWS, EXTRA)],
        scratch_shapes=[vmem(ROWS, EXTRA, dtype=F32)],
        compiler_params=params(),
        cost_estimate=cost(2 * ROWS * D * FF, 11_000_000),
    )(me, dy, wd_t, h, f, a)


def pair_kernel(dg_ref, du_ref, wg_ref, wu_ref, gg_ref, *refs):
    out_ref, flag_ref = refs[-2:]
    n = pl.program_id(0)
    value = dot(dg_ref[...], wg_ref[0]) + dot(du_ref[...], wu_ref[0])
    out_ref[:, pl.ds(pl.multiple_of(n * Q, Q), Q)] = value.astype(BF16)
    flag_ref[...] = jnp.zeros_like(flag_ref)

    @pl.when(n == 0)
    def _():
        out_ref[:, D:] = gg_ref[...]


def pair_grads(dg, du, wg_t, wu_t, gg, *after):
    whole = pl.BlockSpec((ROWS, FF), lambda n: (0, 0))
    weight = pl.BlockSpec((1, FF, Q), lambda n: (n, 0, 0))
    return pl.pallas_call(
        pair_kernel,
        grid=(4,),
        in_specs=[whole, whole, weight, weight, pl.BlockSpec((ROWS, EXTRA), lambda n: (0, 0))]
        + [ANY] * len(after),
        out_specs=[
            pl.BlockSpec((ROWS, D + EXTRA), lambda n: (0, 0)),
            pl.BlockSpec((16, 128), lambda n: (0, 0)),
        ],
        out_shape=[shape(ROWS, D + EXTRA), shape(16, 128)],
        compiler_params=params(MID),
        cost_estimate=cost(4 * ROWS * D * FF, 12_000_000),
    )(dg, du, wg_t, wu_t, gg, *after)


def outer_kernel(at_ref, bt_ref, a_ref, b_ref, *refs):
    out_ref, flag_ref = refs[-2:]
    value = dot(at_ref[...], a_ref[...]) + dot(bt_ref[...], b_ref[...])
    out_ref[...] = value.astype(BF16)
    flag_ref[...] = jnp.zeros_like(flag_ref)


def outer_sum(own_t, other_t, own, other, other_at, n, *after):
    m, width = own_t.shape[0], 256
    left = pl.BlockSpec((m, ROWS), lambda j: (0, 0))
    return pl.pallas_call(
        outer_kernel,
        grid=(n // width,),
        in_specs=[
            left,
            left,
            pl.BlockSpec((ROWS, width), lambda j: (0, j)),
            pl.BlockSpec((ROWS, width), lambda j: (0, j + other_at // width)),
        ]
        + [ANY] * len(after),
        out_specs=[
            pl.BlockSpec((m, width), lambda j: (0, j)),
            pl.BlockSpec((16, 128), lambda j: (0, 0)),
        ],
        out_shape=[shape(m, n), shape(16, 128)],
        compiler_params=params(MID),
        cost_estimate=cost(4 * ROWS * m * n, 2 * (m * n + 2 * ROWS * (m + n))),
    )(own_t, other_t, own, other, *after)


def combine_kernel(ids_hbm, gates_hbm, rows_hbm, tok_hbm, gate_hbm, flag_ref, ids, gates, rows, extra, tok, gate, sems, out_sems):
    flag_ref[...] = jnp.zeros_like(flag_ref)
    few = [start(sems, 0, ids_hbm, ids), start(sems, 1, gates_hbm, gates)]
    extra_load = start(sems, 2, rows_hbm.at[:, pl.ds(D, EXTRA)], extra)
    loads = [start(sems, 3 + n, rows_hbm.at[:, pl.ds(n * Q, Q)], rows.at[n]) for n in range(4)]
    wait(few)
    slots = slot_matrix(ids[...])
    stores = []
    for n in range(4):
        loads[n].wait()
        tok[:, n * Q : (n + 1) * Q] = dot(slots, rows[n], 0, 0).astype(BF16)
    stores.append(start(out_sems, 0, tok, tok_hbm))
    extra_load.wait()
    by_expert = dot(extra[...], slots, 0, 0)
    value = by_expert[:N_EXP] + by_expert[N_EXP : 2 * N_EXP]
    expert_at = lax.broadcasted_iota(jnp.int32, (N_EXP, N_TOK), 0)
    choice = lax.broadcasted_iota(jnp.int32, (4, N_TOK), 0)
    grads = jnp.zeros((4, N_TOK), F32)
    for k in range(4):
        mine = jnp.where(ids[k : k + 1, :] == expert_at, value, 0.0)
        grads = jnp.where(choice == k, jnp.sum(mine, axis=0, keepdims=True), grads)
    gate[...] = (grads / gates[...].astype(F32)).astype(BF16)
    stores.append(start(out_sems, 1, gate, gate_hbm))
    wait(stores)


def combine(ids_t, gates_t, rows):
    return pl.pallas_call(
        combine_kernel,
        in_specs=[ANY] * 3,
        out_specs=[ANY, ANY, pl.BlockSpec(memory_space=pltpu.VMEM)],
        out_shape=[shape(N_TOK, D), shape(4, N_TOK), shape(16, 128)],
        scratch_shapes=[
            vmem(4, N_TOK, dtype=jnp.int32),
            vmem(4, N_TOK),
            vmem(4, ROWS, Q),
            vmem(ROWS, EXTRA),
            vmem(N_TOK, D),
            vmem(4, N_TOK),
            pltpu.SemaphoreType.DMA((7,)),
            pltpu.SemaphoreType.DMA((2,)),
        ],
        compiler_params=params(16),
        cost_estimate=cost(2 * ROWS * N_TOK * D, 2 * ROWS * D),
    )(ids_t, gates_t, rows)


def exchange_experts(rows):
    width = rows.shape[1]
    moved = lax.all_to_all(
        rows.reshape(N_EXP, CAP, width), "expert", split_axis=0, concat_axis=0, tiled=True
    )
    return moved.reshape(ROWS, width)


def hold_kernel(*refs):
    pass


def hold(a, *after, mib=1):
    place = pl.BlockSpec(memory_space=pl.ANY)
    return pl.pallas_call(
        hold_kernel,
        in_specs=[place] * (1 + len(after)),
        out_specs=place,
        out_shape=jax.ShapeDtypeStruct(a.shape, a.dtype),
        input_output_aliases={0: 0},
        compiler_params=params(mib),
    )(a, *after)


def swap_cores(a):
    return lax.ppermute(a, "dp", [(i, i ^ 1) for i in range(2 * N_Z)])


def pick(a, index):
    return lax.dynamic_index_in_dim(a, index, 0, keepdims=False)


ROUTE = tuple((2 * i, 2 * ((i + 1) % N_Z)) for i in range(N_Z)) + tuple(
    (2 * i + 1, 2 * ((i - 1) % N_Z) + 1) for i in range(N_Z)
)


def ring_step(g, held, z, sign, step, after=None):
    if step == 1:
        held = pick(g, (z - sign) & (N_Z - 1))
    came = lax.ppermute(held, "dp", ROUTE)
    if after is not None:
        came = hold(came, after)
    block = pick(g, (z - (step + 1) * sign) & (N_Z - 1))
    return (came.astype(F32) + block.astype(F32)).astype(BF16)


def body(tokens, out_grad, gates, expert_ids, w_gate, w_up, w_down):
    dp = lax.axis_index("dp").astype(jnp.int32)
    z, core = dp >> 1, dp & 1
    sign = 1 - 2 * core
    core_arg = core.reshape(1)
    me = lax.axis_index("expert").astype(jnp.int32).reshape(1)
    ids_t, gates_t = expert_ids.T, gates.T

    down_t = turn_down(core_arg, w_down)
    gate_t, up_t = turn_up(w_gate, w_up)
    x = exchange_experts(dispatch(core_arg, ids_t, None, tokens))
    dy_rows = hold(dispatch(core_arg, ids_t, gates_t, out_grad), x, down_t, up_t, mib=FULL)
    dy = exchange_experts(dy_rows)

    hidden_t, hidden, factor, active = forward(x, w_gate, w_up)
    hidden_other_t = swap_cores(hidden_t)
    x_own, x_theirs = split_transposed(core_arg, x)
    x_other = swap_cores(x_theirs)

    dy = hold(dy, x_other, hidden_other_t, mib=FULL)
    dy_other = swap_cores(dy)
    d_gate, d_up, prob = backward(me, dy, down_t, hidden, factor, active)
    d_gate_other, d_up_other = swap_cores(d_gate), swap_cores(d_up)
    part_down, flag = outer_sum(hidden_t, hidden_other_t, dy, dy_other, H, H, me)
    part_down = part_down.reshape(N_Z, FF // N_Z, H)
    sum_down = ring_step(part_down, None, z, sign, 1)
    part_gate, flag = outer_sum(x_own, x_other, d_gate, d_gate_other, 0, FF, flag)
    part_gate = part_gate.reshape(N_Z, D // (2 * N_Z), FF)
    sum_gate = ring_step(part_gate, None, z, sign, 1)
    part_up, flag = outer_sum(x_own, x_other, d_up, d_up_other, 0, FF, flag, sum_down)
    part_up = part_up.reshape(N_Z, D // (2 * N_Z), FF)
    sum_up = ring_step(part_up, None, z, sign, 1)
    sum_down = ring_step(part_down, sum_down, z, sign, 2)
    pairs, _ = pair_grads(d_gate, d_up, gate_t, up_t, prob, flag, sum_gate)
    sum_down = ring_step(part_down, sum_down, z, sign, 3)
    sum_gate = ring_step(part_gate, sum_gate, z, sign, 2)
    pairs = hold(pairs, sum_up[:16, :128], mib=62)
    back_rows = exchange_experts(pairs)
    token_grad, gate_grad_t, flag = combine(ids_t, gates_t, back_rows)
    for step in range(4, N_Z):
        sum_down = ring_step(part_down, sum_down, z, sign, step, flag if step == 7 else None)
    for step in range(3, N_Z):
        sum_gate = ring_step(part_gate, sum_gate, z, sign, step)
    for step in range(2, N_Z):
        sum_up = ring_step(part_up, sum_up, z, sign, step)

    halves = sum_down.reshape(2, FF // (2 * N_Z), H)
    mine = pick(halves, core)
    theirs = swap_cores(pick(halves, 1 - core))
    left = jnp.where(core == 0, mine, theirs)
    right = jnp.where(core == 0, theirs, mine)
    grad_down = jnp.concatenate([left, right], axis=1)
    return token_grad, gate_grad_t.T, sum_gate[None], sum_up[None], grad_down[None]


def solution(mesh):
    both = P(("dp", "expert"), None)
    weight = P("expert", None, None)
    grad = P("expert", "dp", None)
    return jax.shard_map(
        body,
        mesh=mesh,
        in_specs=(both, both, both, both, weight, weight, weight),
        out_specs=(both, both, grad, grad, grad),
        check_vma=False,
    )
```
